128 devices in a mesh: wide: 16 (over x, y), narrow: 8 (over z, core).
Axes of the slice: x: 4, y: 4, z: 4, core: 2. Of those that a mesh axis runs over, the one named last changes fastest.
Arguments:
- pixels: bfloat16 [64, 64, 256, 768], P('wide', 'narrow')
- coarse_pixels: bfloat16 [256, 256, 768], P('wide', 'narrow')
- unsure: int32 [64, 64], P('wide', 'narrow'), may hold values from 0 to 1, as said below
- patch_weight: bfloat16 [768, 1024], replicated, may hold values from -0.21875 to 0.21875
- position: bfloat16 [256, 1024], replicated, may hold values from -3 to 3
- qkv_weight: bfloat16 [1024, 3072], replicated
- out_weight: bfloat16 [1024, 1024], replicated, may hold values from -0.1875 to 0.1875
- join_weight: bfloat16 [1024, 1024], replicated, may hold values from -0.1875 to 0.1875
- gain_attn: float32 [1024], replicated, may hold values from 0.25 to 1.75
- gain_head: float32 [1024], replicated, may hold values from 0.25 to 1.75
- head_weight: bfloat16 [1024, 16], replicated, may hold values from -0.1875 to 0.1875
Outputs:
- logits: bfloat16 [64, 64, 16, 256], P('wide', 'narrow')
The draws below stay inside these ranges and needn't reach their ends.
Inputs may be any that keep to these rules, and one draw needn't show every extreme that they name: `unsure`: A device holds at most 25 flagged tiles, and in every column of devices along wide one device holds exactly that many; the devices of one column along wide hold 7 * 16 flagged tiles together.
All inputs are finite; a program needn't handle non-finite values.
Results may differ from the reference program's by a relative error of at most 0.01.
Values may be sent and summed in bfloat16 or wider, within the bound.
No kernel may reach another device: no remote copies, remote signals or barrier semaphores. Data moves between devices by JAX's collectives and lax.ppermute only.
A program may use at most 320 MiB of HBM per device.

```python
import math
import jax
import jax.numpy as jnp
from jax import lax

D = 1024
HEADS = 16
HD = 64
PD = 768
CLASSES = 16
TS = 16
TR = 4
TC = 8
TT = 256
CS = 4
TILE_DEV = 32
UNSURE_MOST = 25
RECV = 7
TROWS = 64
TCOLS = 64
CROWS = 256
CCOLS = 256
ESCALATED = 896
N_WIDE = 16
N_NARROW = 8


def draw_pixels(key, part):
    key = jax.random.fold_in(key, 3)
    first, second = jax.random.split(key, 2)
    shape = (TROWS, TCOLS, TT, PD)
    token_shape = (TROWS, TCOLS, TT, 1)
    base = jax.random.normal(first, shape, jnp.float32)
    scale = jnp.exp(jax.random.uniform(second, token_shape, jnp.float32, math.log(0.3), math.log(3.0)))
    values = jnp.clip(base, -5.0, 5.0) * scale
    return values.astype(jnp.bfloat16)


def draw_coarse_pixels(key, part):
    key = jax.random.fold_in(key, 7)
    first, second = jax.random.split(key, 2)
    shape = (CROWS, CCOLS, PD)
    token_shape = (CROWS, CCOLS, 1)
    base = jax.random.normal(first, shape, jnp.float32)
    scale = jnp.exp(jax.random.uniform(second, token_shape, jnp.float32, math.log(0.3), math.log(3.0)))
    values = jnp.clip(base, -5.0, 5.0) * scale
    return values.astype(jnp.bfloat16)


def draw_qkv_weight(key, part):
    key = jax.random.fold_in(key, 5)
    first = jax.random.fold_in(key, 0)
    base = jnp.clip(jax.random.normal(first, (D, 3 * D), jnp.float32), -5.0, 5.0) * D ** (-0.5)
    return base.astype(jnp.bfloat16)


def draw_unsure(key, part):
    key = jax.random.fold_in(key, 11)
    first, second, third = jax.random.split(key, 3)
    extra_total = RECV * N_WIDE - UNSURE_MOST - (N_WIDE - 1)
    cap_extra = UNSURE_MOST // 2
    pool = (N_WIDE - 1) * cap_extra
    hottest = jax.random.randint(first, (N_NARROW,), 0, N_WIDE)
    shuffled = jax.vmap(lambda sub: jax.random.permutation(sub, pool))(jax.random.split(second, N_NARROW))
    owners = shuffled[:, :extra_total] // cap_extra
    others = jnp.sum((owners[:, :, None] == jnp.arange(N_WIDE - 1, dtype=jnp.int32)[None, None, :]).astype(jnp.int32), axis=1) + 1
    wide_pos = jnp.arange(N_WIDE, dtype=jnp.int32)
    lookup = wide_pos[None, :] - (wide_pos[None, :] > hottest[:, None]).astype(jnp.int32)
    lookup = jnp.clip(lookup, 0, N_WIDE - 2)
    taken = jnp.take_along_axis(others, lookup, axis=1)
    counts = jnp.where(wide_pos[None, :] == hottest[:, None], UNSURE_MOST, taken)
    ranks = jax.vmap(lambda sub: jax.random.permutation(sub, TILE_DEV))(jax.random.split(third, N_NARROW * N_WIDE))
    ranks = ranks.reshape(N_NARROW, N_WIDE, TILE_DEV)
    flags = (ranks < counts[:, :, None]).astype(jnp.int32)
    flags = flags.reshape(N_NARROW, N_WIDE, TR, TC).transpose(1, 2, 0, 3)
    return flags.reshape(TROWS, TCOLS)


def scatter_about(key, extent, width, bound, held_as=jnp.bfloat16):
    values = width * jax.random.normal(key, extent, jnp.float32)
    return jnp.clip(values, min=-bound, max=bound).astype(held_as)


def setup_inputs(seed: int = 0) -> dict:
    key_list = jax.random.split(jax.random.key(seed), 12)
    return {
        "pixels": draw_pixels(jax.random.fold_in(key_list[11], 71), 0),
        "coarse_pixels": draw_coarse_pixels(jax.random.fold_in(key_list[11], 71), 0),
        "unsure": draw_unsure(jax.random.fold_in(key_list[11], 71), 0),
        "patch_weight": scatter_about(key_list[3], (PD, D), PD ** -0.5, 0.21875),
        "position": scatter_about(key_list[4], (TT, D), 0.5, 3.0),
        "qkv_weight": draw_qkv_weight(jax.random.fold_in(key_list[11], 71), 0),
        "out_weight": scatter_about(key_list[6], (D, D), D ** -0.5, 0.1875),
        "join_weight": scatter_about(key_list[7], (D, D), D ** -0.5, 0.1875),
        "gain_attn": jnp.clip(1.0 + 0.15 * jax.random.normal(key_list[8], (D,), jnp.float32), 0.25, 1.75),
        "gain_head": jnp.clip(1.0 + 0.15 * jax.random.normal(key_list[9], (D,), jnp.float32), 0.25, 1.75),
        "head_weight": scatter_about(key_list[10], (D, CLASSES), D ** -0.5, 0.1875),
    }


EPS = 1e-06

def interp_table():
    fine = jnp.arange(TS, dtype=jnp.int32)
    eighths = 2 * fine - 3
    lower = eighths // 8
    frac = (eighths - 8 * lower).astype(jnp.float32) / 8.0
    column = jnp.arange(CS + 2, dtype=jnp.int32)
    left = (column[None, :] == (lower + 1)[:, None]).astype(jnp.float32)
    right = (column[None, :] == (lower + 2)[:, None]).astype(jnp.float32)
    return left * (1.0 - frac)[:, None] + right * frac[:, None]

def layer_norm(values, gain):
    center = values - lax.optimization_barrier(jnp.mean(values, axis=-1, keepdims=True))
    spread = lax.optimization_barrier(jnp.mean(center * center, axis=-1, keepdims=True))
    return center * lax.rsqrt(spread + EPS) * gain

def attend(tokens, gain_attn, qkv_weight, out_weight):
    count = tokens.shape[0]
    normed = layer_norm(tokens, gain_attn).astype(jnp.bfloat16).reshape(-1, D)
    packed = jnp.dot(normed, qkv_weight, preferred_element_type=jnp.float32).astype(jnp.bfloat16)
    packed = packed.reshape(count, TT, 3, HEADS, HD)
    queries = packed[:, :, 0].astype(jnp.float32)
    key_rows = packed[:, :, 1].astype(jnp.float32)
    value_rows = packed[:, :, 2].astype(jnp.float32)
    scores = jnp.einsum('nqhd,nkhd->nhqk', queries, key_rows) * HD ** (-0.5)
    weights = jax.nn.softmax(scores, axis=-1).astype(jnp.bfloat16)
    mixed = jnp.einsum('nhqk,nkhd->nqhd', weights.astype(jnp.float32), value_rows)
    mixed = mixed.astype(jnp.bfloat16).reshape(-1, D)
    return tokens + jnp.dot(mixed, out_weight, preferred_element_type=jnp.float32).reshape(count, TT, D)

def reference(pixels, coarse_pixels, unsure, patch_weight, position, qkv_weight, out_weight, join_weight, gain_attn, gain_head, head_weight):
    table = interp_table()
    highest = lax.Precision.HIGHEST
    win_rows = CROWS // TS
    win_cols = CCOLS // TS
    windows = coarse_pixels.reshape(win_rows, TS, win_cols, TS, PD).transpose(0, 2, 1, 3, 4)
    windows = windows.reshape(win_rows, win_cols * TT, PD)

    def glance_band(band):
        embed = jnp.dot(band, patch_weight, preferred_element_type=jnp.float32).reshape(win_cols, TT, D)
        embed = embed + position.astype(jnp.float32)
        return attend(embed, gain_attn, qkv_weight, out_weight).astype(jnp.bfloat16)
    bands = lax.map(glance_band, windows)
    features = bands.reshape(win_rows, win_cols, TS, TS, D).transpose(0, 2, 1, 3, 4).reshape(CROWS, CCOLS, D)
    padded = jnp.pad(features, ((1, 1), (1, 1), (0, 0)), mode='edge')

    def head_row(row):
        normed = layer_norm(row.astype(jnp.float32), gain_head).astype(jnp.bfloat16)
        return jnp.dot(normed, head_weight, preferred_element_type=jnp.float32)
    coarse_logits = lax.map(head_row, padded)
    row_index = (jnp.arange(TROWS, dtype=jnp.int32)[:, None] * CS + jnp.arange(CS + 2, dtype=jnp.int32)[None, :]).reshape(-1)
    col_index = (jnp.arange(TCOLS, dtype=jnp.int32)[:, None] * CS + jnp.arange(CS + 2, dtype=jnp.int32)[None, :]).reshape(-1)
    tile_logits = jnp.take(jnp.take(coarse_logits, row_index, axis=0), col_index, axis=1)
    tile_logits = tile_logits.reshape(TROWS, CS + 2, TCOLS, CS + 2, CLASSES)
    glance_logits = jnp.einsum('pi,qj,aibjc->abcpq', table, table, tile_logits, precision=highest)
    glance_logits = glance_logits.reshape(TROWS * TCOLS, CLASSES, TT)
    flags = unsure.reshape(-1)
    chosen = jnp.nonzero(flags > 0, size=ESCALATED)[0].astype(jnp.int32)
    flat_pixels = pixels.reshape(TROWS * TCOLS, TT, PD)

    def cut_rim(row_start, col_start):
        zero = jnp.zeros((), jnp.int32)
        return lax.dynamic_slice(padded, (row_start.astype(jnp.int32), col_start.astype(jnp.int32), zero), (CS + 2, CS + 2, D))

    def focus_block(block):
        tile_rows = block // TCOLS
        tile_cols = block % TCOLS
        rims = jax.vmap(cut_rim)(tile_rows * CS, tile_cols * CS)
        lifted = jnp.einsum('pi,qj,nijd->npqd', table, table, rims.astype(jnp.float32), precision=highest)
        lifted = lifted.astype(jnp.bfloat16).reshape(-1, D)
        tile_pixels = flat_pixels[block].reshape(-1, PD)
        embed = jnp.dot(tile_pixels, patch_weight, preferred_element_type=jnp.float32)
        embed = embed + jnp.dot(lifted, join_weight, preferred_element_type=jnp.float32)
        embed = embed.reshape(-1, TT, D) + position.astype(jnp.float32)
        result = attend(embed, gain_attn, qkv_weight, out_weight)
        normed = layer_norm(result, gain_head).astype(jnp.bfloat16).reshape(-1, D)
        answer = jnp.dot(normed, head_weight, preferred_element_type=jnp.float32).reshape(-1, TT, CLASSES)
        return answer.transpose(0, 2, 1).astype(jnp.bfloat16)
    focused = lax.map(focus_block, chosen.reshape(-1, 8)).reshape(ESCALATED, CLASSES, TT)
    combined = glance_logits.astype(jnp.bfloat16).at[chosen].set(focused)
    return combined.reshape(TROWS, TCOLS, CLASSES, TT)
```

```python
import jax
import jax.numpy as jnp
import numpy as np
from jax import lax
from jax.experimental import pallas as pl
from jax.experimental.pallas import tpu as pltpu
from jax.sharding import PartitionSpec as P

D = 1024
HEADS = 16
HD = 64
PD = 768
CLASSES = 16
TS = 16
TT = 256
CS = 4
EPS = 1e-06
GROUP = 256
GROUP_HEADS = GROUP // HD
LANES = 128
JW = D + LANES
RIM_K = 256
TR = 4
TC = 8
TILES = TR * TC
CR = TR * CS
CC = TC * CS
BF = jnp.bfloat16
F32 = jnp.float32
NT = (((1,), (1,)), ((), ()))
VMEM_LIMIT = 60 * 1024 * 1024


def interp_table():
    table = np.zeros((TS, CS + 2), np.float64)
    for p in range(TS):
        c = (2 * p - 3) / 8
        i = int(np.floor(c))
        table[p, i + 1] = 1 - (c - i)
        table[p, i + 2] = c - i
    return table


def rim_slots():
    slots = np.zeros((CS + 2, CC + 2), np.int64)
    for i in range(CS + 2):
        for c in range(1, CC + 1):
            slots[i, c] = i * CC + c - 1
        slots[i, 0] = (CS + 2) * CC + i
        slots[i, CC + 1] = (CS + 2) * CC + 8 + i
    return slots


def lift_tables():
    table = interp_table()
    slots = rim_slots()
    lift = np.zeros((TC, TT, RIM_K), np.float32)
    for b in range(TC):
        for i in range(CS + 2):
            for j in range(CS + 2):
                lift[b, :, slots[i, b * CS + j]] += np.outer(table[:, i], table[:, j]).reshape(-1)
    return lift


def side_tables():
    pick = np.zeros((2, TR, 16, 32), np.float32)
    for a in range(TR):
        for i in range(CS + 2):
            pick[0, a, i, a * CS + i] = 1
            pick[1, a, 8 + i, a * CS + i] = 1
    return pick


def dot(a, b):
    return jnp.dot(a, b, preferred_element_type=F32)


def dot_nt(a, b):
    return lax.dot_general(a, b, NT, preferred_element_type=F32)


def layer_norm(values, gain):
    center = values - jnp.mean(values, axis=-1, keepdims=True)
    spread = jnp.mean(center * center, axis=-1, keepdims=True)
    return center * lax.rsqrt(spread + EPS) * gain


def attend(tokens, normed, packed, mixed, gain_attn, qkv_weight, out_weight):
    count = tokens.shape[0] // TT
    normed[...] = layer_norm(tokens[...], gain_attn[...]).astype(BF)
    lane_head = lax.broadcasted_iota(jnp.int32, (TT, GROUP), 1) // HD
    for g in range(HEADS // GROUP_HEADS):
        for part in range(3):
            cols = slice(part * D + g * GROUP, part * D + (g + 1) * GROUP)
            packed[:, cols] = dot(normed[...], qkv_weight[:, cols]).astype(BF)
    for w in range(count):
        rows = slice(w * TT, (w + 1) * TT)
        for g in range(HEADS // GROUP_HEADS):
            queries = packed[rows, g * GROUP : (g + 1) * GROUP]
            keys = packed[rows, D + g * GROUP : D + (g + 1) * GROUP]
            values = packed[rows, 2 * D + g * GROUP : 2 * D + (g + 1) * GROUP]
            total = None
            for h in range(GROUP_HEADS):
                mine = lane_head == h
                scores = dot_nt(jnp.where(mine, queries, jnp.zeros_like(queries)), keys)
                top = jnp.max(scores, axis=-1, keepdims=True)
                weights = jnp.exp((scores - top) * HD ** (-0.5))
                norm = 1.0 / jnp.sum(weights, axis=-1, keepdims=True)
                probs = (weights * norm).astype(BF)
                term = dot(probs, jnp.where(mine, values, jnp.zeros_like(values)))
                total = term if total is None else total + term
            mixed[rows, g * GROUP : (g + 1) * GROUP] = total.astype(BF)
    for n in range(D // GROUP):
        cols = slice(n * GROUP, (n + 1) * GROUP)
        tokens[:, cols] = tokens[:, cols] + dot(mixed[...], out_weight[:, cols])


def glance_kernel(
    coarse, patch_weight, position, qkv_weight, out_weight, join_weight, gain_attn, gain_head, head,
    joined, tokens, normed, packed, mixed,
):
    windows = CC // TS
    for w in range(windows):
        rows = slice(w * TT, (w + 1) * TT)
        cells = coarse[:, w * TS : (w + 1) * TS, :].reshape(TT, PD)
        tokens[rows, :] = dot(cells, patch_weight[...]) + position[...].astype(F32)
    attend(tokens, normed, packed, mixed, gain_attn, qkv_weight, out_weight)
    features = tokens[...].astype(BF)
    normed[...] = layer_norm(features.astype(F32), gain_head[...]).astype(BF)
    mixed[...] = features
    logits = dot(normed[...], head[...])
    high = logits.astype(BF)
    low = (logits - high.astype(F32)).astype(BF)
    lane = lax.broadcasted_iota(jnp.int32, high.shape, 1)
    both = jnp.where(lane < CLASSES, high, low)
    lifted = dot(mixed[...], join_weight[...]).astype(BF)
    for w in range(windows):
        rows = slice(w * TT, (w + 1) * TT)
        cols = slice(w * TS, (w + 1) * TS)
        joined[:, cols, :D] = lifted[rows].reshape(TS, TS, D)
        joined[:, cols, D:] = both[rows].reshape(TS, TS, LANES)


def focus_kernel(
    flags, pixels, joined, up, down, left, right, lift, pick, patch_weight, position, qkv_weight,
    out_weight, gain_attn, gain_head, head,
    logits, chosen, buffer, sem, rims, tokens, normed, packed, mixed,
):
    def mark(t, count):
        @pl.when(flags[t] == 1)
        def _():
            chosen[count] = t

        return count + flags[t]

    count = lax.fori_loop(0, TILES, mark, jnp.int32(0))

    def fetch(k):
        return pltpu.make_async_copy(pixels.at[chosen[k]], buffer.at[k % 2], sem.at[k % 2])

    @pl.when(count > 0)
    def _():
        fetch(0).start()

    for a in range(TR):
        for i in range(CS + 2):
            row = a * CS + i
            if row == 0:
                cells = up[...]
            elif row == CR + 1:
                cells = down[...]
            else:
                cells = joined[(row - 1) * CC : row * CC, :]
            rims[a, i * CC : (i + 1) * CC, :] = cells
        edge = (CS + 2) * CC
        sides = dot(pick[0, a], left[...]) + dot(pick[1, a], right[...])
        rims[a, edge : edge + 16, :] = sides.astype(BF)
        rims[a, edge + 16 :, :] = jnp.zeros((RIM_K - edge - 16, JW), BF)
    coarse = []
    for a in range(TR):
        turned = jnp.transpose(rims[a, :, D:].astype(F32))
        coarse.append(turned[: 2 * CLASSES])
    coarse = jnp.concatenate(coarse, axis=0).astype(BF)
    for b in range(TC):
        fine = dot_nt(coarse, lift[b])
        for a in range(TR):
            at = a * 2 * CLASSES
            logits[a * TC + b] = (fine[at : at + CLASSES] + fine[at + CLASSES : at + 2 * CLASSES]).astype(BF)

    def work(k, carry):
        fetch(k).wait()

        @pl.when(k + 1 < count)
        def _():
            fetch(k + 1).start()

        tile = chosen[k]
        a = tile // TC
        b = tile % TC
        embed = dot(buffer[k % 2], patch_weight[...])
        embed = embed + dot(lift[b], rims[a, :, :D])
        tokens[...] = embed + position[...].astype(F32)
        attend(tokens, normed, packed, mixed, gain_attn, qkv_weight, out_weight)
        normed[...] = layer_norm(tokens[...], gain_head[...]).astype(BF)
        answer = jnp.transpose(dot(normed[...], head[...]))
        logits[tile] = answer[:CLASSES].astype(BF)
        return carry

    lax.fori_loop(0, count, work, jnp.int32(0))


def vmem():
    return pl.BlockSpec(memory_space=pltpu.VMEM)


def smem():
    return pl.BlockSpec(memory_space=pltpu.SMEM)


def hbm():
    return pl.BlockSpec(memory_space=pl.ANY)


def block_scratch(rows):
    return [
        pltpu.VMEM((rows, D), F32),
        pltpu.VMEM((rows, D), BF),
        pltpu.VMEM((rows, 3 * D), BF),
        pltpu.VMEM((rows, D), BF),
    ]


def glance(coarse_pixels, patch_weight, position, qkv_weight, out_weight, join_weight, gain_attn, gain_head, head):
    rows = CR * CC
    return pl.pallas_call(
        glance_kernel,
        out_shape=jax.ShapeDtypeStruct((CR, CC, JW), BF),
        in_specs=[vmem()] * 9,
        out_specs=vmem(),
        scratch_shapes=block_scratch(rows),
        compiler_params=pltpu.CompilerParams(vmem_limit_bytes=VMEM_LIMIT),
        name="glance",
    )(coarse_pixels, patch_weight, position, qkv_weight, out_weight, join_weight, gain_attn, gain_head, head)


def focus(flags, pixels, joined, up, down, left, right, lift, pick, patch_weight, position, qkv_weight, out_weight, gain_attn, gain_head, head):
    return pl.pallas_call(
        focus_kernel,
        out_shape=jax.ShapeDtypeStruct((TILES, CLASSES, TT), BF),
        in_specs=[smem(), hbm()] + [vmem()] * 14,
        out_specs=vmem(),
        scratch_shapes=[
            pltpu.SMEM((TILES,), jnp.int32),
            pltpu.VMEM((2, TT, PD), BF),
            pltpu.SemaphoreType.DMA((2,)),
            pltpu.VMEM((TR, RIM_K, JW), BF),
        ]
        + block_scratch(TT),
        compiler_params=pltpu.CompilerParams(vmem_limit_bytes=VMEM_LIMIT),
        name="focus",
    )(flags, pixels, joined, up, down, left, right, lift, pick, patch_weight, position, qkv_weight, out_weight, gain_attn, gain_head, head)


def shifted(x, axis, step):
    count = lax.axis_size(axis)
    pairs = [(i, i + step) for i in range(count) if 0 <= i + step < count]
    return lax.ppermute(x, axis, pairs)


def borders(joined):
    wide_pos = lax.axis_index("wide")
    wide_end = lax.axis_size("wide") - 1
    narrow_pos = lax.axis_index("narrow")
    narrow_end = lax.axis_size("narrow") - 1
    up = jnp.where(wide_pos == 0, joined[0], shifted(joined[-1], "wide", 1))
    down = jnp.where(wide_pos == wide_end, joined[-1], shifted(joined[0], "wide", -1))
    blank = jnp.zeros((32 - CR - 2, JW), BF)
    first = jnp.concatenate([up[:1], joined[:, 0], down[:1], blank], axis=0)
    last = jnp.concatenate([up[-1:], joined[:, -1], down[-1:], blank], axis=0)
    left = jnp.where(narrow_pos == 0, first, shifted(last, "narrow", 1))
    right = jnp.where(narrow_pos == narrow_end, last, shifted(first, "narrow", -1))
    return up, down, left, right


def per_device(
    pixels,
    coarse_pixels,
    unsure,
    patch_weight,
    position,
    qkv_weight,
    out_weight,
    join_weight,
    gain_attn,
    gain_head,
    head_weight,
):
    tile_rows, tile_cols = unsure.shape
    flags = unsure.reshape(-1)
    gain_attn = gain_attn.reshape(1, D)
    gain_head = gain_head.reshape(1, D)
    head = jnp.concatenate([head_weight, head_weight, jnp.zeros((D, LANES - 2 * CLASSES), BF)], axis=1)
    lift = jnp.asarray(lift_tables(), BF)
    pick = jnp.asarray(side_tables(), BF)
    joined = glance(coarse_pixels, patch_weight, position, qkv_weight, out_weight, join_weight, gain_attn, gain_head, head)
    up, down, left, right = borders(joined)
    logits = focus(
        flags, pixels.reshape(TILES, TT, PD), joined.reshape(CR * CC, JW), up, down, left, right, lift, pick,
        patch_weight, position, qkv_weight, out_weight, gain_attn, gain_head, head,
    )
    return logits.reshape(tile_rows, tile_cols, CLASSES, TT)


def solution(mesh):
    return jax.shard_map(
        per_device,
        mesh=mesh,
        in_specs=(
            P("wide", "narrow", None, None),
            P("wide", "narrow", None),
            P("wide", "narrow"),
            P(),
            P(),
            P(),
            P(),
            P(),
            P(),
            P(),
            P(),
        ),
        out_specs=P("wide", "narrow", None, None),
        check_vma=False,
    )
```

```python
import jax
import jax.numpy as jnp
import numpy as np
from jax import lax
from jax.experimental import pallas as pl
from jax.experimental.pallas import tpu as pltpu
from jax.sharding import PartitionSpec as P

D = 1024
HEADS = 16
HD = 64
PD = 768
CLASSES = 16
TS = 16
TT = 256
CS = 4
EPS = 1e-06
GROUP = 256
GROUP_HEADS = GROUP // HD
LANES = 128
JW = D + LANES
RIM_K = 256
TR = 4
TC = 8
TILES = TR * TC
CR = TR * CS
CC = TC * CS
KEEP = 7
SEND = (3, 3, 3, 3, 2)
SLOTS = ((4, 0), (0, 0), (2, 0), (1, 0), (3, 0), (4, 1), (0, 1), (2, 1), (1, 1), (3, 1), (0, 2), (2, 2), (1, 2), (3, 2))
RIM = 48
SLOT_ROWS = TT + RIM + 16
BF = jnp.bfloat16
F32 = jnp.float32
NT = (((1,), (1,)), ((), ()))
VMEM_LIMIT = 60 * 1024 * 1024


def interp_table():
    table = np.zeros((TS, CS + 2), np.float64)
    for p in range(TS):
        c = (2 * p - 3) / 8
        i = int(np.floor(c))
        table[p, i + 1] = 1 - (c - i)
        table[p, i + 2] = c - i
    return table


def rim_slots():
    slots = np.zeros((CS + 2, CC + 2), np.int64)
    for i in range(CS + 2):
        for c in range(1, CC + 1):
            slots[i, c] = i * CC + c - 1
        slots[i, 0] = (CS + 2) * CC + i
        slots[i, CC + 1] = (CS + 2) * CC + 8 + i
    return slots


def lift_tables():
    table = interp_table()
    slots = rim_slots()
    lift = np.zeros((TC, TT, RIM_K), np.float32)
    for b in range(TC):
        for i in range(CS + 2):
            for j in range(CS + 2):
                lift[b, :, slots[i, b * CS + j]] += np.outer(table[:, i], table[:, j]).reshape(-1)
    return lift


def side_tables():
    pick = np.zeros((2, TR, 16, 32), np.float32)
    for a in range(TR):
        for i in range(CS + 2):
            pick[0, a, i, a * CS + i] = 1
            pick[1, a, 8 + i, a * CS + i] = 1
    return pick


def rim_tables():
    table = interp_table()
    slots = rim_slots()
    pick = np.zeros((TC, RIM, RIM_K), np.float32)
    lift = np.zeros((TT, RIM), np.float32)
    for i in range(CS + 2):
        for j in range(CS + 2):
            r = i * (CS + 2) + j
            lift[:, r] = np.outer(table[:, i], table[:, j]).reshape(-1)
            for b in range(TC):
                pick[b, r, slots[i, b * CS + j]] = 1
    return pick, lift


def dot(a, b):
    return jnp.dot(a, b, preferred_element_type=F32)


def dot_nt(a, b):
    return lax.dot_general(a, b, NT, preferred_element_type=F32)


def layer_norm(values, gain):
    center = values - jnp.mean(values, axis=-1, keepdims=True)
    spread = jnp.mean(center * center, axis=-1, keepdims=True)
    return center * lax.rsqrt(spread + EPS) * gain


def attend(tokens, normed, packed, mixed, gain_attn, qkv_weight, out_weight):
    count = tokens.shape[0] // TT
    normed[...] = layer_norm(tokens[...], gain_attn[...]).astype(BF)
    lane_head = lax.broadcasted_iota(jnp.int32, (TT, GROUP), 1) // HD
    for g in range(HEADS // GROUP_HEADS):
        for part in range(3):
            cols = slice(part * D + g * GROUP, part * D + (g + 1) * GROUP)
            packed[:, cols] = dot(normed[...], qkv_weight[:, cols]).astype(BF)
    for w in range(count):
        rows = slice(w * TT, (w + 1) * TT)
        for g in range(HEADS // GROUP_HEADS):
            queries = packed[rows, g * GROUP : (g + 1) * GROUP]
            keys = packed[rows, D + g * GROUP : D + (g + 1) * GROUP]
            values = packed[rows, 2 * D + g * GROUP : 2 * D + (g + 1) * GROUP]
            total = None
            for h in range(GROUP_HEADS):
                mine = lane_head == h
                scores = dot_nt(jnp.where(mine, queries, jnp.zeros_like(queries)), keys)
                top = jnp.max(scores, axis=-1, keepdims=True)
                weights = jnp.exp((scores - top) * HD ** (-0.5))
                norm = 1.0 / jnp.sum(weights, axis=-1, keepdims=True)
                probs = (weights * norm).astype(BF)
                term = dot(probs, jnp.where(mine, values, jnp.zeros_like(values)))
                total = term if total is None else total + term
            mixed[rows, g * GROUP : (g + 1) * GROUP] = total.astype(BF)
    for n in range(D // GROUP):
        cols = slice(n * GROUP, (n + 1) * GROUP)
        tokens[:, cols] = tokens[:, cols] + dot(mixed[...], out_weight[:, cols])


def glance_kernel(
    coarse, patch_weight, position, qkv_weight, out_weight, join_weight, gain_attn, gain_head, head,
    joined, tokens, normed, packed, mixed,
):
    windows = CC // TS
    for w in range(windows):
        rows = slice(w * TT, (w + 1) * TT)
        cells = coarse[:, w * TS : (w + 1) * TS, :].reshape(TT, PD)
        tokens[rows, :] = dot(cells, patch_weight[...]) + position[...].astype(F32)
    attend(tokens, normed, packed, mixed, gain_attn, qkv_weight, out_weight)
    features = tokens[...].astype(BF)
    normed[...] = layer_norm(features.astype(F32), gain_head[...]).astype(BF)
    mixed[...] = features
    logits = dot(normed[...], head[...])
    high = logits.astype(BF)
    low = (logits - high.astype(F32)).astype(BF)
    lane = lax.broadcasted_iota(jnp.int32, high.shape, 1)
    both = jnp.where(lane < CLASSES, high, low)
    lifted = dot(mixed[...], join_weight[...]).astype(BF)
    for w in range(windows):
        rows = slice(w * TT, (w + 1) * TT)
        cols = slice(w * TS, (w + 1) * TS)
        joined[:, cols, :D] = lifted[rows].reshape(TS, TS, D)
        joined[:, cols, D:] = both[rows].reshape(TS, TS, LANES)


def list_flagged(flags, chosen):
    def mark(t, count):
        @pl.when(flags[t] == 1)
        def _():
            chosen[count] = t

        return count + flags[t]

    count = lax.fori_loop(0, TILES, mark, jnp.int32(0))
    away = jnp.clip(count - KEEP, 0, len(SLOTS))
    return count - away, away


def pack_kernel(
    flags, pixels, joined, up, down, left, right, pick, rim_pick,
    rims, *refs,
):
    sends = refs[: len(SEND)]
    chosen, rim_rows, pixel_sem, rim_sem = refs[len(SEND) :]
    keep, away = list_flagged(flags, chosen)

    def pixel_copy(s):
        way, at = SLOTS[s]
        return pltpu.make_async_copy(pixels.at[chosen[keep + s]], sends[way].at[at, pl.ds(0, TT)], pixel_sem.at[s])

    def rim_copy(s):
        way, at = SLOTS[s]
        return pltpu.make_async_copy(rim_rows.at[s], sends[way].at[at, pl.ds(TT, RIM + 16)], rim_sem.at[s])

    for s in range(len(SLOTS)):

        @pl.when(s < away)
        def _():
            pixel_copy(s).start()

    for a in range(TR):
        for i in range(CS + 2):
            row = a * CS + i
            if row == 0:
                cells = up[...]
            elif row == CR + 1:
                cells = down[...]
            else:
                cells = joined[(row - 1) * CC : row * CC, :]
            rims[a, i * CC : (i + 1) * CC, :] = cells
        edge = (CS + 2) * CC
        sides = dot(pick[0, a], left[...]) + dot(pick[1, a], right[...])
        rims[a, edge : edge + 16, :] = sides.astype(BF)
        rims[a, edge + 16 :, :] = jnp.zeros((RIM_K - edge - 16, JW), BF)
    for s in range(len(SLOTS)):

        @pl.when(s < away)
        def _():
            tile = chosen[keep + s]
            rim = dot(rim_pick[tile % TC], rims[tile // TC, :, :D])
            row = lax.broadcasted_iota(jnp.int32, rim.shape, 0)
            rim = jnp.where(row == RIM - 1, 1.0, rim).astype(BF)
            rim_rows[s, :RIM, :] = rim[:, :PD]
            for part in range(RIM // 16):
                rim_rows[s, RIM:, part * GROUP : (part + 1) * GROUP] = rim[part * 16 : (part + 1) * 16, PD:]

        @pl.when(s >= away)
        def _():
            rim_rows[s] = jnp.zeros((RIM + 16, PD), BF)

        rim_copy(s).start()
    for s in range(len(SLOTS)):
        rim_copy(s).wait()

        @pl.when(s < away)
        def _():
            pixel_copy(s).wait()


def classify(tokens, normed, gain_head, head):
    normed[...] = layer_norm(tokens[...], gain_head[...]).astype(BF)
    answer = jnp.transpose(dot(normed[...], head[...]))
    return answer[:CLASSES].astype(BF)


def local_kernel(
    flags, pixels, rims, lift, patch_weight, position, qkv_weight, out_weight, gain_attn, gain_head, head,
    logits, chosen, buffer, sem, tokens, normed, packed, mixed,
):
    keep, _ = list_flagged(flags, chosen)

    def fetch(k):
        return pltpu.make_async_copy(pixels.at[chosen[k]], buffer.at[k % 2], sem.at[k % 2])

    @pl.when(keep > 0)
    def _():
        fetch(0).start()

    coarse = []
    for a in range(TR):
        turned = jnp.transpose(rims[a, :, D:].astype(F32))
        coarse.append(turned[: 2 * CLASSES])
    coarse = jnp.concatenate(coarse, axis=0).astype(BF)
    for b in range(TC):
        fine = dot_nt(coarse, lift[b])
        for a in range(TR):
            at = a * 2 * CLASSES
            logits[a * TC + b] = (fine[at : at + CLASSES] + fine[at + CLASSES : at + 2 * CLASSES]).astype(BF)

    def work(k, carry):
        fetch(k).wait()

        @pl.when(k + 1 < keep)
        def _():
            fetch(k + 1).start()

        tile = chosen[k]
        embed = dot(buffer[k % 2], patch_weight[...])
        embed = embed + dot(lift[tile % TC], rims[tile // TC, :, :D])
        tokens[...] = embed + position[...].astype(F32)
        attend(tokens, normed, packed, mixed, gain_attn, qkv_weight, out_weight)
        logits[tile] = classify(tokens, normed, gain_head, head)
        return carry

    lax.fori_loop(0, keep, work, jnp.int32(0))


def remote_kernel(*refs):
    ways = len(SEND)
    got = refs[:ways]
    rim_lift, patch_weight, position, qkv_weight, out_weight, gain_attn, gain_head, head = refs[ways : ways + 8]
    answers = refs[ways + 8 : 2 * ways + 8]
    filled, flag_rows, buffer, flag_sem, sem, tokens, normed, packed, mixed = refs[2 * ways + 8 :]

    def flag_copy(s):
        way, at = SLOTS[s]
        return pltpu.make_async_copy(got[way].at[at, pl.ds(TT + RIM - 16, 16)], flag_rows.at[s], flag_sem.at[s])

    for s in range(len(SLOTS)):
        flag_copy(s).start()
    count = jnp.int32(0)
    for s in range(len(SLOTS)):
        flag_copy(s).wait()
        here = (jnp.max(flag_rows[s, :, :LANES].astype(F32)[15:16]) > 0.5).astype(jnp.int32)

        @pl.when(here == 1)
        def _():
            filled[count] = s

        count = count + here

    def each_slot(k, then):
        for s in range(len(SLOTS)):

            @pl.when(filled[k] == s)
            def _():
                then(*SLOTS[s])

    def fetch(k, way, at):
        return pltpu.make_async_copy(got[way].at[at], buffer.at[k % 2], sem.at[k % 2])

    @pl.when(count > 0)
    def _():
        each_slot(0, lambda way, at: fetch(0, way, at).start())

    def work(k, carry):
        fetch(k, 0, 0).wait()

        @pl.when(k + 1 < count)
        def _():
            each_slot(k + 1, lambda way, at: fetch(k + 1, way, at).start())

        slot = buffer.at[k % 2]
        tail = slot[TT + RIM :, :]
        rest = jnp.concatenate([tail[:, part * GROUP : (part + 1) * GROUP] for part in range(RIM // 16)], axis=0)
        place = position[...].astype(F32)
        embed = dot(slot[:TT, :], patch_weight[...])
        tokens[:, :PD] = embed[:, :PD] + dot(rim_lift[...], slot[TT : TT + RIM, :]) + place[:, :PD]
        tokens[:, PD:] = embed[:, PD:] + dot(rim_lift[...], rest) + place[:, PD:]
        attend(tokens, normed, packed, mixed, gain_attn, qkv_weight, out_weight)
        answer = classify(tokens, normed, gain_head, head)

        def store(way, at):
            answers[way][at] = answer

        each_slot(k, store)
        return carry

    lax.fori_loop(0, count, work, jnp.int32(0))


def merge_kernel(flags, base, *refs):
    returned = refs[: len(SEND)]
    logits, chosen = refs[len(SEND) :]
    keep, away = list_flagged(flags, chosen)
    logits[...] = base[...]
    for s in range(len(SLOTS)):

        @pl.when(s < away)
        def _():
            way, at = SLOTS[s]
            logits[chosen[keep + s]] = returned[way][at]


def vmem():
    return pl.BlockSpec(memory_space=pltpu.VMEM)


def smem():
    return pl.BlockSpec(memory_space=pltpu.SMEM)


def hbm():
    return pl.BlockSpec(memory_space=pl.ANY)


def block_scratch(rows):
    return [
        pltpu.VMEM((rows, D), F32),
        pltpu.VMEM((rows, D), BF),
        pltpu.VMEM((rows, 3 * D), BF),
        pltpu.VMEM((rows, D), BF),
    ]


def glance(coarse_pixels, patch_weight, position, qkv_weight, out_weight, join_weight, gain_attn, gain_head, head):
    rows = CR * CC
    return pl.pallas_call(
        glance_kernel,
        out_shape=jax.ShapeDtypeStruct((CR, CC, JW), BF),
        in_specs=[vmem()] * 9,
        out_specs=vmem(),
        scratch_shapes=block_scratch(rows),
        compiler_params=pltpu.CompilerParams(vmem_limit_bytes=VMEM_LIMIT),
        name="glance",
    )(coarse_pixels, patch_weight, position, qkv_weight, out_weight, join_weight, gain_attn, gain_head, head)


def tile_cost(tiles):
    return pl.CostEstimate(flops=tiles * 3_500_000_000, bytes_accessed=12_000_000, transcendentals=0)


def params():
    return pltpu.CompilerParams(vmem_limit_bytes=VMEM_LIMIT)


def chosen_scratch():
    return pltpu.SMEM((TILES,), jnp.int32)


def pack(flags, pixels, joined, up, down, left, right, pick, rim_pick):
    return pl.pallas_call(
        pack_kernel,
        out_shape=[jax.ShapeDtypeStruct((TR, RIM_K, JW), BF)]
        + [jax.ShapeDtypeStruct((n, SLOT_ROWS, PD), BF) for n in SEND],
        in_specs=[smem(), hbm()] + [vmem()] * 7,
        out_specs=[vmem()] + [hbm()] * len(SEND),
        scratch_shapes=[
            chosen_scratch(),
            pltpu.VMEM((len(SLOTS), RIM + 16, PD), BF),
            pltpu.SemaphoreType.DMA((len(SLOTS),)),
            pltpu.SemaphoreType.DMA((len(SLOTS),)),
        ],
        compiler_params=params(),
        name="pack",
    )(flags, pixels, joined, up, down, left, right, pick, rim_pick)


def focus_local(flags, pixels, rims, lift, *weights):
    return pl.pallas_call(
        local_kernel,
        out_shape=jax.ShapeDtypeStruct((TILES, CLASSES, TT), BF),
        in_specs=[smem(), hbm()] + [vmem()] * (2 + len(weights)),
        out_specs=vmem(),
        scratch_shapes=[
            chosen_scratch(),
            pltpu.VMEM((2, TT, PD), BF),
            pltpu.SemaphoreType.DMA((2,)),
        ]
        + block_scratch(TT),
        compiler_params=params(),
        cost_estimate=tile_cost(9),
        name="focus_local",
    )(flags, pixels, rims, lift, *weights)


def focus_remote(got, rim_lift, *weights):
    return pl.pallas_call(
        remote_kernel,
        out_shape=[jax.ShapeDtypeStruct((n, CLASSES, TT), BF) for n in SEND],
        in_specs=[hbm()] * len(SEND) + [vmem()] * (1 + len(weights)),
        out_specs=[vmem()] * len(SEND),
        scratch_shapes=[
            pltpu.SMEM((len(SLOTS),), jnp.int32),
            pltpu.VMEM((len(SLOTS), 16, PD), BF),
            pltpu.VMEM((2, SLOT_ROWS, PD), BF),
            pltpu.SemaphoreType.DMA((len(SLOTS),)),
            pltpu.SemaphoreType.DMA((2,)),
        ]
        + block_scratch(TT),
        compiler_params=params(),
        cost_estimate=tile_cost(4),
        name="focus_remote",
    )(*got, rim_lift, *weights)


def merge(flags, base, returned):
    return pl.pallas_call(
        merge_kernel,
        out_shape=jax.ShapeDtypeStruct((TILES, CLASSES, TT), BF),
        in_specs=[smem()] + [vmem()] * (1 + len(SEND)),
        out_specs=vmem(),
        scratch_shapes=[chosen_scratch()],
        compiler_params=params(),
        name="merge",
    )(flags, base, *returned)


def routes():
    wide = lax.axis_size("wide")
    narrow = lax.axis_size("narrow")
    side = int(np.sqrt(wide))

    def along_x(step):
        return "wide", [(i, (i // side + step) % side * side + i % side) for i in range(wide)]

    def along_y(step):
        return "wide", [(i, i // side * side + (i % side + step) % side) for i in range(wide)]

    return [along_x(1), along_x(-1), along_y(1), along_y(-1), ("narrow", [(i, i ^ 1) for i in range(narrow)])]


def shifted(x, axis, step):
    count = lax.axis_size(axis)
    pairs = [(i, i + step) for i in range(count) if 0 <= i + step < count]
    return lax.ppermute(x, axis, pairs)


def borders(joined):
    wide_pos = lax.axis_index("wide")
    wide_end = lax.axis_size("wide") - 1
    narrow_pos = lax.axis_index("narrow")
    narrow_end = lax.axis_size("narrow") - 1
    up = jnp.where(wide_pos == 0, joined[0], shifted(joined[-1], "wide", 1))
    down = jnp.where(wide_pos == wide_end, joined[-1], shifted(joined[0], "wide", -1))
    blank = jnp.zeros((32 - CR - 2, JW), BF)
    first = jnp.concatenate([up[:1], joined[:, 0], down[:1], blank], axis=0)
    last = jnp.concatenate([up[-1:], joined[:, -1], down[-1:], blank], axis=0)
    left = jnp.where(narrow_pos == 0, first, shifted(last, "narrow", 1))
    right = jnp.where(narrow_pos == narrow_end, last, shifted(first, "narrow", -1))
    return up, down, left, right


def per_device(
    pixels,
    coarse_pixels,
    unsure,
    patch_weight,
    position,
    qkv_weight,
    out_weight,
    join_weight,
    gain_attn,
    gain_head,
    head_weight,
):
    tile_rows, tile_cols = unsure.shape
    flags = unsure.reshape(-1)
    gain_attn = gain_attn.reshape(1, D)
    gain_head = gain_head.reshape(1, D)
    head = jnp.concatenate([head_weight, head_weight, jnp.zeros((D, LANES - 2 * CLASSES), BF)], axis=1)
    lift = jnp.asarray(lift_tables(), BF)
    pick = jnp.asarray(side_tables(), BF)
    joined = glance(coarse_pixels, patch_weight, position, qkv_weight, out_weight, join_weight, gain_attn, gain_head, head)
    up, down, left, right = borders(joined)
    rim_pick, rim_lift = (jnp.asarray(t, BF) for t in rim_tables())
    weights = (patch_weight, position, qkv_weight, out_weight, gain_attn, gain_head, head)
    flat_pixels = pixels.reshape(TILES, TT, PD)
    flat_joined = joined.reshape(CR * CC, JW)
    rims, *sends = pack(flags, flat_pixels, flat_joined, up, down, left, right, pick, rim_pick)
    ways = routes()
    got = [lax.ppermute(block, axis, pairs) for block, (axis, pairs) in zip(sends, ways)]
    base = focus_local(flags, flat_pixels, rims, lift, *weights)
    answers = focus_remote(got, rim_lift, *weights)
    returned = [
        lax.ppermute(block, axis, [(b, a) for a, b in pairs]) for block, (axis, pairs) in zip(answers, ways)
    ]
    logits = merge(flags, base, returned)
    return logits.reshape(tile_rows, tile_cols, CLASSES, TT)


def solution(mesh):
    return jax.shard_map(
        per_device,
        mesh=mesh,
        in_specs=(
            P("wide", "narrow", None, None),
            P("wide", "narrow", None),
            P("wide", "narrow"),
            P(),
            P(),
            P(),
            P(),
            P(),
            P(),
            P(),
            P(),
        ),
        out_specs=P("wide", "narrow", None, None),
        check_vma=False,
    )
```

```python
import jax
import jax.numpy as jnp
import numpy as np
from jax import lax
from jax.experimental import pallas as pl
from jax.experimental.pallas import tpu as pltpu
from jax.sharding import PartitionSpec as P

D = 1024
HEADS = 16
HD = 64
PD = 768
CLASSES = 16
TS = 16
TT = 256
CS = 4
EPS = 1e-06
GROUP = 256
GROUP_HEADS = GROUP // HD
LANES = 128
JW = D + LANES
RIM_K = 256
TR = 4
TC = 8
TILES = TR * TC
CR = TR * CS
CC = TC * CS
KEEP = 7
SEND = (3, 3, 3, 3, 2)
SLOTS = ((4, 0), (0, 0), (2, 0), (1, 0), (3, 0), (4, 1), (0, 1), (2, 1), (1, 1), (3, 1), (0, 2), (2, 2), (1, 2), (3, 2))
RIM = 48
SLOT_ROWS = TT + RIM + 16
BF = jnp.bfloat16
F32 = jnp.float32
NT = (((1,), (1,)), ((), ()))
VMEM_LIMIT = 60 * 1024 * 1024


def interp_table():
    table = np.zeros((TS, CS + 2), np.float64)
    for p in range(TS):
        c = (2 * p - 3) / 8
        i = int(np.floor(c))
        table[p, i + 1] = 1 - (c - i)
        table[p, i + 2] = c - i
    return table


def rim_slots():
    slots = np.zeros((CS + 2, CC + 2), np.int64)
    for i in range(CS + 2):
        for c in range(1, CC + 1):
            slots[i, c] = i * CC + c - 1
        slots[i, 0] = (CS + 2) * CC + i
        slots[i, CC + 1] = (CS + 2) * CC + 8 + i
    return slots


def lift_tables():
    table = interp_table()
    slots = rim_slots()
    lift = np.zeros((TC, TT, RIM_K), np.float32)
    for b in range(TC):
        for i in range(CS + 2):
            for j in range(CS + 2):
                lift[b, :, slots[i, b * CS + j]] += np.outer(table[:, i], table[:, j]).reshape(-1)
    return lift


def side_tables():
    pick = np.zeros((2, TR, 16, 32), np.float32)
    for a in range(TR):
        for i in range(CS + 2):
            pick[0, a, i, a * CS + i] = 1
            pick[1, a, 8 + i, a * CS + i] = 1
    return pick


def rim_tables():
    table = interp_table()
    slots = rim_slots()
    pick = np.zeros((TC, RIM, RIM_K), np.float32)
    lift = np.zeros((TT, RIM), np.float32)
    for i in range(CS + 2):
        for j in range(CS + 2):
            r = i * (CS + 2) + j
            lift[:, r] = np.outer(table[:, i], table[:, j]).reshape(-1)
            for b in range(TC):
                pick[b, r, slots[i, b * CS + j]] = 1
    return pick, lift


def dot(a, b):
    return jnp.dot(a, b, preferred_element_type=F32)


def dot_nt(a, b):
    return lax.dot_general(a, b, NT, preferred_element_type=F32)


def layer_norm(values, gain):
    center = values - jnp.mean(values, axis=-1, keepdims=True)
    spread = jnp.mean(center * center, axis=-1, keepdims=True)
    return center * lax.rsqrt(spread + EPS) * gain


def attend(tokens, normed, packed, mixed, gain_attn, qkv_weight, out_weight):
    count = tokens.shape[0] // TT
    normed[...] = layer_norm(tokens[...], gain_attn[...]).astype(BF)
    lane_head = lax.broadcasted_iota(jnp.int32, (TT, GROUP), 1) // HD
    for g in range(HEADS // GROUP_HEADS):
        for part in range(3):
            cols = slice(part * D + g * GROUP, part * D + (g + 1) * GROUP)
            packed[:, cols] = dot(normed[...], qkv_weight[:, cols]).astype(BF)
    for w in range(count):
        rows = slice(w * TT, (w + 1) * TT)
        for g in range(HEADS // GROUP_HEADS):
            queries = packed[rows, g * GROUP : (g + 1) * GROUP]
            keys = packed[rows, D + g * GROUP : D + (g + 1) * GROUP]
            values = packed[rows, 2 * D + g * GROUP : 2 * D + (g + 1) * GROUP]
            total = None
            for h in range(GROUP_HEADS):
                mine = lane_head == h
                scores = dot_nt(jnp.where(mine, queries, jnp.zeros_like(queries)), keys)
                top = jnp.max(scores, axis=-1, keepdims=True)
                weights = jnp.exp((scores - top) * HD ** (-0.5))
                norm = 1.0 / jnp.sum(weights, axis=-1, keepdims=True)
                probs = (weights * norm).astype(BF)
                term = dot(probs, jnp.where(mine, values, jnp.zeros_like(values)))
                total = term if total is None else total + term
            mixed[rows, g * GROUP : (g + 1) * GROUP] = total.astype(BF)
    for n in range(D // GROUP):
        cols = slice(n * GROUP, (n + 1) * GROUP)
        tokens[:, cols] = tokens[:, cols] + dot(mixed[...], out_weight[:, cols])


def glance_kernel(
    coarse, patch_weight, position, qkv_weight, out_weight, join_weight, gain_attn, gain_head, head,
    joined, tokens, normed, packed, mixed,
):
    windows = CC // TS
    for w in range(windows):
        rows = slice(w * TT, (w + 1) * TT)
        cells = coarse[:, w * TS : (w + 1) * TS, :].reshape(TT, PD)
        tokens[rows, :] = dot(cells, patch_weight[...]) + position[...].astype(F32)
    attend(tokens, normed, packed, mixed, gain_attn, qkv_weight, out_weight)
    features = tokens[...].astype(BF)
    normed[...] = layer_norm(features.astype(F32), gain_head[...]).astype(BF)
    mixed[...] = features
    logits = dot(normed[...], head[...])
    high = logits.astype(BF)
    low = (logits - high.astype(F32)).astype(BF)
    lane = lax.broadcasted_iota(jnp.int32, high.shape, 1)
    both = jnp.where(lane < CLASSES, high, low)
    lifted = dot(mixed[...], join_weight[...]).astype(BF)
    for w in range(windows):
        rows = slice(w * TT, (w + 1) * TT)
        cols = slice(w * TS, (w + 1) * TS)
        joined[:, cols, :D] = lifted[rows].reshape(TS, TS, D)
        joined[:, cols, D:] = both[rows].reshape(TS, TS, LANES)


def list_flagged(flags, chosen):
    def mark(t, count):
        @pl.when(flags[t] == 1)
        def _():
            chosen[count] = t

        return count + flags[t]

    count = lax.fori_loop(0, TILES, mark, jnp.int32(0))
    away = jnp.clip(count - KEEP, 0, len(SLOTS))
    return count - away, away


def pack_kernel(
    flags, pixels, joined, up, down, left, right, pick, rim_pick,
    rims, *refs,
):
    sends = refs[: len(SEND)]
    chosen, stage, in_sem, out_sem = refs[len(SEND) :]
    keep, away = list_flagged(flags, chosen)

    def pixel_copy(s):
        return pltpu.make_async_copy(pixels.at[chosen[keep + s]], stage.at[s, pl.ds(0, TT)], in_sem.at[s])

    def whole_copy(s):
        way, at = SLOTS[s]
        return pltpu.make_async_copy(stage.at[s], sends[way].at[at], out_sem.at[s])

    def tail_copy(s):
        way, at = SLOTS[s]
        rows = pl.ds(TT, RIM + 16)
        return pltpu.make_async_copy(stage.at[s, rows], sends[way].at[at, rows], out_sem.at[s])

    for s in range(len(SLOTS)):

        @pl.when(s < away)
        def _():
            pixel_copy(s).start()

    for a in range(TR):
        for i in range(CS + 2):
            row = a * CS + i
            if row == 0:
                cells = up[...]
            elif row == CR + 1:
                cells = down[...]
            else:
                cells = joined[(row - 1) * CC : row * CC, :]
            rims[a, i * CC : (i + 1) * CC, :] = cells
        edge = (CS + 2) * CC
        sides = dot(pick[0, a], left[...]) + dot(pick[1, a], right[...])
        rims[a, edge : edge + 16, :] = sides.astype(BF)
        rims[a, edge + 16 :, :] = jnp.zeros((RIM_K - edge - 16, JW), BF)
    for s in range(len(SLOTS)):

        @pl.when(s < away)
        def _():
            tile = chosen[keep + s]
            rim = dot(rim_pick[tile % TC], rims[tile // TC, :, :D])
            row = lax.broadcasted_iota(jnp.int32, rim.shape, 0)
            rim = jnp.where(row == RIM - 1, 1.0, rim).astype(BF)
            stage[s, TT : TT + RIM, :] = rim[:, :PD]
            for part in range(RIM // 16):
                cols = slice(part * GROUP, (part + 1) * GROUP)
                stage[s, TT + RIM :, cols] = rim[part * 16 : (part + 1) * 16, PD:]
            pixel_copy(s).wait()
            whole_copy(s).start()

        @pl.when(s >= away)
        def _():
            stage[s, TT:, :] = jnp.zeros((RIM + 16, PD), BF)
            tail_copy(s).start()

    for s in range(len(SLOTS)):

        @pl.when(s < away)
        def _():
            whole_copy(s).wait()

        @pl.when(s >= away)
        def _():
            tail_copy(s).wait()


def classify(tokens, normed, gain_head, head):
    normed[...] = layer_norm(tokens[...], gain_head[...]).astype(BF)
    answer = jnp.transpose(dot(normed[...], head[...]))
    return answer[:CLASSES].astype(BF)


def local_kernel(
    flags, pixels, rims, lift, patch_weight, position, qkv_weight, out_weight, gain_attn, gain_head, head,
    logits, chosen, buffer, sem, tokens, normed, packed, mixed,
):
    keep, _ = list_flagged(flags, chosen)

    def fetch(k):
        return pltpu.make_async_copy(pixels.at[chosen[k]], buffer.at[k % 2], sem.at[k % 2])

    @pl.when(keep > 0)
    def _():
        fetch(0).start()

    coarse = []
    for a in range(TR):
        turned = jnp.transpose(rims[a, :, D:].astype(F32))
        coarse.append(turned[: 2 * CLASSES])
    coarse = jnp.concatenate(coarse, axis=0).astype(BF)
    for b in range(TC):
        fine = dot_nt(coarse, lift[b])
        for a in range(TR):
            at = a * 2 * CLASSES
            logits[a * TC + b] = (fine[at : at + CLASSES] + fine[at + CLASSES : at + 2 * CLASSES]).astype(BF)

    def work(k, carry):
        fetch(k).wait()

        @pl.when(k + 1 < keep)
        def _():
            fetch(k + 1).start()

        tile = chosen[k]
        embed = dot(buffer[k % 2], patch_weight[...])
        embed = embed + dot(lift[tile % TC], rims[tile // TC, :, :D])
        tokens[...] = embed + position[...].astype(F32)
        attend(tokens, normed, packed, mixed, gain_attn, qkv_weight, out_weight)
        logits[tile] = classify(tokens, normed, gain_head, head)
        return carry

    lax.fori_loop(0, keep, work, jnp.int32(0))


def remote_kernel(*refs):
    ways = len(SEND)
    got = refs[:ways]
    refs = refs[1:]
    rim_lift, patch_weight, position, qkv_weight, out_weight, gain_attn, gain_head, head = refs[ways : ways + 8]
    answers = refs[ways + 8 : 2 * ways + 8]
    filled, flag_rows, buffer, flag_sem, sem, tokens, normed, packed, mixed = refs[2 * ways + 8 :]

    def flag_copy(s):
        way, at = SLOTS[s]
        return pltpu.make_async_copy(got[way].at[at, pl.ds(TT + RIM - 16, 16)], flag_rows.at[s], flag_sem.at[s])

    for s in range(len(SLOTS)):
        flag_copy(s).start()
    count = jnp.int32(0)
    for s in range(len(SLOTS)):
        flag_copy(s).wait()
        here = (jnp.max(flag_rows[s, :, :LANES].astype(F32)[15:16]) > 0.5).astype(jnp.int32)

        @pl.when(here == 1)
        def _():
            filled[count] = s

        count = count + here

    def each_slot(k, then):
        for s in range(len(SLOTS)):

            @pl.when(filled[k] == s)
            def _():
                then(*SLOTS[s])

    def fetch(k, way, at):
        return pltpu.make_async_copy(got[way].at[at], buffer.at[k % 2], sem.at[k % 2])

    @pl.when(count > 0)
    def _():
        each_slot(0, lambda way, at: fetch(0, way, at).start())

    def work(k, carry):
        fetch(k, 0, 0).wait()

        @pl.when(k + 1 < count)
        def _():
            each_slot(k + 1, lambda way, at: fetch(k + 1, way, at).start())

        slot = buffer.at[k % 2]
        tail = slot[TT + RIM :, :]
        rest = jnp.concatenate([tail[:, part * GROUP : (part + 1) * GROUP] for part in range(RIM // 16)], axis=0)
        place = position[...].astype(F32)
        embed = dot(slot[:TT, :], patch_weight[...])
        tokens[:, :PD] = embed[:, :PD] + dot(rim_lift[...], slot[TT : TT + RIM, :]) + place[:, :PD]
        tokens[:, PD:] = embed[:, PD:] + dot(rim_lift[...], rest) + place[:, PD:]
        attend(tokens, normed, packed, mixed, gain_attn, qkv_weight, out_weight)
        answer = classify(tokens, normed, gain_head, head)

        def store(way, at):
            answers[way][at] = answer

        each_slot(k, store)
        return carry

    lax.fori_loop(0, count, work, jnp.int32(0))


def merge_kernel(flags, base, *refs):
    returned = refs[: len(SEND)]
    logits, chosen = refs[len(SEND) :]
    keep, away = list_flagged(flags, chosen)
    logits[...] = base[...]
    for s in range(len(SLOTS)):

        @pl.when(s < away)
        def _():
            way, at = SLOTS[s]
            logits[chosen[keep + s]] = returned[way][at]


def vmem():
    return pl.BlockSpec(memory_space=pltpu.VMEM)


def smem():
    return pl.BlockSpec(memory_space=pltpu.SMEM)


def hbm():
    return pl.BlockSpec(memory_space=pl.ANY)


def block_scratch(rows):
    return [
        pltpu.VMEM((rows, D), F32),
        pltpu.VMEM((rows, D), BF),
        pltpu.VMEM((rows, 3 * D), BF),
        pltpu.VMEM((rows, D), BF),
    ]


def glance(coarse_pixels, patch_weight, position, qkv_weight, out_weight, join_weight, gain_attn, gain_head, head):
    rows = CR * CC
    return pl.pallas_call(
        glance_kernel,
        out_shape=jax.ShapeDtypeStruct((CR, CC, JW), BF),
        in_specs=[vmem()] * 9,
        out_specs=vmem(),
        scratch_shapes=block_scratch(rows),
        compiler_params=pltpu.CompilerParams(vmem_limit_bytes=VMEM_LIMIT),
        name="glance",
    )(coarse_pixels, patch_weight, position, qkv_weight, out_weight, join_weight, gain_attn, gain_head, head)


def tile_cost(tiles):
    return pl.CostEstimate(flops=tiles * 3_500_000_000, bytes_accessed=12_000_000, transcendentals=0)


def params():
    return pltpu.CompilerParams(vmem_limit_bytes=VMEM_LIMIT)


def chosen_scratch():
    return pltpu.SMEM((TILES,), jnp.int32)


def pack(flags, pixels, joined, up, down, left, right, pick, rim_pick):
    return pl.pallas_call(
        pack_kernel,
        out_shape=[jax.ShapeDtypeStruct((TR, RIM_K, JW), BF)]
        + [jax.ShapeDtypeStruct((n, SLOT_ROWS, PD), BF) for n in SEND],
        in_specs=[smem(), hbm()] + [vmem()] * 7,
        out_specs=[vmem()] + [hbm()] * len(SEND),
        scratch_shapes=[
            chosen_scratch(),
            pltpu.VMEM((len(SLOTS), SLOT_ROWS, PD), BF),
            pltpu.SemaphoreType.DMA((len(SLOTS),)),
            pltpu.SemaphoreType.DMA((len(SLOTS),)),
        ],
        compiler_params=params(),
        name="pack",
    )(flags, pixels, joined, up, down, left, right, pick, rim_pick)


def focus_local(flags, pixels, rims, lift, *weights):
    return pl.pallas_call(
        local_kernel,
        out_shape=jax.ShapeDtypeStruct((TILES, CLASSES, TT), BF),
        in_specs=[smem(), hbm()] + [vmem()] * (2 + len(weights)),
        out_specs=vmem(),
        scratch_shapes=[
            chosen_scratch(),
            pltpu.VMEM((2, TT, PD), BF),
            pltpu.SemaphoreType.DMA((2,)),
        ]
        + block_scratch(TT),
        compiler_params=params(),
        cost_estimate=tile_cost(9),
        name="focus_local",
    )(flags, pixels, rims, lift, *weights)


def focus_remote(got, base, rim_lift, *weights):
    return pl.pallas_call(
        remote_kernel,
        out_shape=[jax.ShapeDtypeStruct((n, CLASSES, TT), BF) for n in SEND],
        in_specs=[hbm()] * (len(SEND) + 1) + [vmem()] * (1 + len(weights)),
        out_specs=[vmem()] * len(SEND),
        scratch_shapes=[
            pltpu.SMEM((len(SLOTS),), jnp.int32),
            pltpu.VMEM((len(SLOTS), 16, PD), BF),
            pltpu.VMEM((2, SLOT_ROWS, PD), BF),
            pltpu.SemaphoreType.DMA((len(SLOTS),)),
            pltpu.SemaphoreType.DMA((2,)),
        ]
        + block_scratch(TT),
        compiler_params=params(),
        cost_estimate=tile_cost(4),
        name="focus_remote",
    )(*got, base, rim_lift, *weights)


def merge(flags, base, returned):
    return pl.pallas_call(
        merge_kernel,
        out_shape=jax.ShapeDtypeStruct((TILES, CLASSES, TT), BF),
        in_specs=[smem()] + [vmem()] * (1 + len(SEND)),
        out_specs=vmem(),
        scratch_shapes=[chosen_scratch()],
        compiler_params=params(),
        name="merge",
    )(flags, base, *returned)


def routes():
    wide = lax.axis_size("wide")
    narrow = lax.axis_size("narrow")
    side = int(np.sqrt(wide))

    def along_x(step):
        return "wide", [(i, (i // side + step) % side * side + i % side) for i in range(wide)]

    def along_y(step):
        return "wide", [(i, i // side * side + (i % side + step) % side) for i in range(wide)]

    return [along_x(1), along_x(-1), along_y(1), along_y(-1), ("narrow", [(i, i ^ 1) for i in range(narrow)])]


def shifted(x, axis, step):
    count = lax.axis_size(axis)
    pairs = [(i, i + step) for i in range(count) if 0 <= i + step < count]
    return lax.ppermute(x, axis, pairs)


def borders(joined):
    wide_pos = lax.axis_index("wide")
    wide_end = lax.axis_size("wide") - 1
    narrow_pos = lax.axis_index("narrow")
    narrow_end = lax.axis_size("narrow") - 1
    up = jnp.where(wide_pos == 0, joined[0], shifted(joined[-1], "wide", 1))
    down = jnp.where(wide_pos == wide_end, joined[-1], shifted(joined[0], "wide", -1))
    blank = jnp.zeros((32 - CR - 2, JW), BF)
    first = jnp.concatenate([up[:1], joined[:, 0], down[:1], blank], axis=0)
    last = jnp.concatenate([up[-1:], joined[:, -1], down[-1:], blank], axis=0)
    left = jnp.where(narrow_pos == 0, first, shifted(last, "narrow", 1))
    right = jnp.where(narrow_pos == narrow_end, last, shifted(first, "narrow", -1))
    return up, down, left, right


def per_device(
    pixels,
    coarse_pixels,
    unsure,
    patch_weight,
    position,
    qkv_weight,
    out_weight,
    join_weight,
    gain_attn,
    gain_head,
    head_weight,
):
    tile_rows, tile_cols = unsure.shape
    flags = unsure.reshape(-1)
    gain_attn = gain_attn.reshape(1, D)
    gain_head = gain_head.reshape(1, D)
    head = jnp.concatenate([head_weight, head_weight, jnp.zeros((D, LANES - 2 * CLASSES), BF)], axis=1)
    lift = jnp.asarray(lift_tables(), BF)
    pick = jnp.asarray(side_tables(), BF)
    joined = glance(coarse_pixels, patch_weight, position, qkv_weight, out_weight, join_weight, gain_attn, gain_head, head)
    up, down, left, right = borders(joined)
    rim_pick, rim_lift = (jnp.asarray(t, BF) for t in rim_tables())
    weights = (patch_weight, position, qkv_weight, out_weight, gain_attn, gain_head, head)
    flat_pixels = pixels.reshape(TILES, TT, PD)
    flat_joined = joined.reshape(CR * CC, JW)
    rims, *sends = pack(flags, flat_pixels, flat_joined, up, down, left, right, pick, rim_pick)
    ways = routes()
    got = [lax.ppermute(block, axis, pairs) for block, (axis, pairs) in zip(sends, ways)]
    base = focus_local(flags, flat_pixels, rims, lift, *weights)
    answers = focus_remote(got, base, rim_lift, *weights)
    returned = [
        lax.ppermute(block, axis, [(b, a) for a, b in pairs]) for block, (axis, pairs) in zip(answers, ways)
    ]
    logits = merge(flags, base, returned)
    return logits.reshape(tile_rows, tile_cols, CLASSES, TT)


def solution(mesh):
    return jax.shard_map(
        per_device,
        mesh=mesh,
        in_specs=(
            P("wide", "narrow", None, None),
            P("wide", "narrow", None),
            P("wide", "narrow"),
            P(),
            P(),
            P(),
            P(),
            P(),
            P(),
            P(),
            P(),
        ),
        out_specs=P("wide", "narrow", None, None),
        check_vma=False,
    )
```

```python
import jax
import jax.numpy as jnp
import numpy as np
from jax import lax
from jax.experimental import pallas as pl
from jax.experimental.pallas import tpu as pltpu
from jax.sharding import PartitionSpec as P

D = 1024
HEADS = 16
HD = 64
PD = 768
CLASSES = 16
TS = 16
TT = 256
CS = 4
EPS = 1e-06
LOG2E = 1.4426950408889634
GROUP = 256
GROUP_HEADS = GROUP // HD
LANES = 128
JW = D + LANES
RIM_K = 256
TR = 4
TC = 8
TILES = TR * TC
CR = TR * CS
CC = TC * CS
KEEP = 7
SEND = (3, 3, 3, 3, 2)
SLOTS = ((4, 0), (0, 0), (2, 0), (1, 0), (3, 0), (4, 1), (0, 1), (2, 1), (1, 1), (3, 1), (0, 2), (2, 2), (1, 2), (3, 2))
RIM = 48
SLOT_ROWS = TT + RIM + 16
BF = jnp.bfloat16
F32 = jnp.float32
NT = (((1,), (1,)), ((), ()))
VMEM_LIMIT = 60 * 1024 * 1024


def interp_table():
    table = np.zeros((TS, CS + 2), np.float64)
    for p in range(TS):
        c = (2 * p - 3) / 8
        i = int(np.floor(c))
        table[p, i + 1] = 1 - (c - i)
        table[p, i + 2] = c - i
    return table


def rim_slots():
    slots = np.zeros((CS + 2, CC + 2), np.int64)
    for i in range(CS + 2):
        for c in range(1, CC + 1):
            slots[i, c] = i * CC + c - 1
        slots[i, 0] = (CS + 2) * CC + i
        slots[i, CC + 1] = (CS + 2) * CC + 8 + i
    return slots


def lift_tables():
    table = interp_table()
    slots = rim_slots()
    lift = np.zeros((TC, TT, RIM_K), np.float32)
    for b in range(TC):
        for i in range(CS + 2):
            for j in range(CS + 2):
                lift[b, :, slots[i, b * CS + j]] += np.outer(table[:, i], table[:, j]).reshape(-1)
    return lift


def side_tables():
    pick = np.zeros((2, TR, 16, 32), np.float32)
    for a in range(TR):
        for i in range(CS + 2):
            pick[0, a, i, a * CS + i] = 1
            pick[1, a, 8 + i, a * CS + i] = 1
    return pick


def rim_tables():
    table = interp_table()
    slots = rim_slots()
    pick = np.zeros((TC, RIM, RIM_K), np.float32)
    lift = np.zeros((TT, RIM), np.float32)
    for i in range(CS + 2):
        for j in range(CS + 2):
            r = i * (CS + 2) + j
            lift[:, r] = np.outer(table[:, i], table[:, j]).reshape(-1)
            for b in range(TC):
                pick[b, r, slots[i, b * CS + j]] = 1
    return pick, lift


def dot(a, b):
    return jnp.dot(a, b, preferred_element_type=F32)


def dot_nt(a, b):
    return lax.dot_general(a, b, NT, preferred_element_type=F32)


def layer_norm(values, gain):
    center = values - jnp.mean(values, axis=-1, keepdims=True)
    spread = jnp.mean(center * center, axis=-1, keepdims=True)
    return center * lax.rsqrt(spread + EPS) * gain


def attend(tokens, normed, packed, mixed, gain_attn, qkv_weight, out_weight, need_qkv, need_out):
    count = tokens.shape[0] // TT
    normed[...] = layer_norm(tokens[...], gain_attn[...]).astype(BF)
    lane_head = lax.broadcasted_iota(jnp.int32, (TT, GROUP), 1) // HD
    need_qkv()
    for g in range(HEADS // GROUP_HEADS):
        for part in range(3):
            cols = slice(part * D + g * GROUP, part * D + (g + 1) * GROUP)
            packed[:, cols] = dot(normed[...], qkv_weight[:, cols]).astype(BF)
    for w in range(count):
        rows = slice(w * TT, (w + 1) * TT)
        for g in range(HEADS // GROUP_HEADS):
            queries = packed[rows, g * GROUP : (g + 1) * GROUP]
            keys = packed[rows, D + g * GROUP : D + (g + 1) * GROUP]
            values = packed[rows, 2 * D + g * GROUP : 2 * D + (g + 1) * GROUP]
            total = None
            norms = None
            for h in range(GROUP_HEADS):
                mine = lane_head == h
                scores = dot_nt(jnp.where(mine, queries, jnp.zeros_like(queries)), keys)
                top = jnp.max(scores, axis=-1, keepdims=True)
                weights = jnp.exp2((scores - top) * (HD ** (-0.5) * LOG2E))
                norm = 1.0 / jnp.sum(weights, axis=-1, keepdims=True)
                norms = norm if norms is None else jnp.where(lane_head >= h, norm, norms)
                term = dot(weights.astype(BF), jnp.where(mine, values, jnp.zeros_like(values)))
                total = term if total is None else total + term
            mixed[rows, g * GROUP : (g + 1) * GROUP] = (total * norms).astype(BF)
    need_out()
    for n in range(D // GROUP):
        cols = slice(n * GROUP, (n + 1) * GROUP)
        tokens[:, cols] = tokens[:, cols] + dot(mixed[...], out_weight[:, cols])


class Weights:
    def __init__(self, sources, scratch, sem):
        self.refs = scratch
        self.copies = [pltpu.make_async_copy(a, b, sem.at[i]) for i, (a, b) in enumerate(zip(sources, scratch))]

    def start(self):
        for copy in self.copies:
            copy.start()

    def need(self, *which):
        for i in which:
            self.copies[i].wait()

    def first(self, k, *which):
        @pl.when(k == 0)
        def _():
            self.need(*which)


def spread_head(head_rows, head):
    rows = head_rows[...].astype(F32)
    rows = jnp.concatenate([rows, rows, jnp.zeros((LANES - 2 * CLASSES, D), F32)], axis=0)
    head[...] = jnp.transpose(rows).astype(BF)


def glance_kernel(
    coarse, gain_attn, gain_head, head_rows, patch_hbm, position_hbm, qkv_hbm, out_hbm, join_hbm,
    joined, patch_weight, position, qkv_weight, out_weight, join_weight, head, sem, tokens, normed, packed, mixed,
):
    weights = Weights(
        [patch_hbm, position_hbm, qkv_hbm, out_hbm, join_hbm],
        [patch_weight, position, qkv_weight, out_weight, join_weight],
        sem,
    )
    weights.start()
    spread_head(head_rows, head)
    weights.need(0, 1)
    windows = CC // TS
    for w in range(windows):
        rows = slice(w * TT, (w + 1) * TT)
        cells = coarse[:, w * TS : (w + 1) * TS, :].reshape(TT, PD)
        tokens[rows, :] = dot(cells, patch_weight[...]) + position[...].astype(F32)
    attend(
        tokens, normed, packed, mixed, gain_attn, qkv_weight, out_weight, lambda: weights.need(2), lambda: weights.need(3)
    )
    features = tokens[...].astype(BF)
    normed[...] = layer_norm(features.astype(F32), gain_head[...]).astype(BF)
    mixed[...] = features
    logits = dot(normed[...], head[...])
    high = logits.astype(BF)
    low = (logits - high.astype(F32)).astype(BF)
    lane = lax.broadcasted_iota(jnp.int32, high.shape, 1)
    both = jnp.where(lane < CLASSES, high, low)
    weights.need(4)
    lifted = dot(mixed[...], join_weight[...]).astype(BF)
    for w in range(windows):
        rows = slice(w * TT, (w + 1) * TT)
        cols = slice(w * TS, (w + 1) * TS)
        joined[:, cols, :D] = lifted[rows].reshape(TS, TS, D)
        joined[:, cols, D:] = both[rows].reshape(TS, TS, LANES)


def list_flagged(flags, chosen):
    def mark(t, count):
        @pl.when(flags[t] == 1)
        def _():
            chosen[count] = t

        return count + flags[t]

    count = lax.fori_loop(0, TILES, mark, jnp.int32(0))
    away = jnp.clip(count - KEEP, 0, len(SLOTS))
    return count - away, away


def pack_kernel(
    flags, pixels, joined, up, down, left, right, pick, rim_pick,
    rims, *refs,
):
    sends = refs[: len(SEND)]
    chosen, stage, in_sem, out_sem = refs[len(SEND) :]
    keep, away = list_flagged(flags, chosen)

    def pixel_copy(s):
        return pltpu.make_async_copy(pixels.at[chosen[keep + s]], stage.at[s, pl.ds(0, TT)], in_sem.at[s])

    def whole_copy(s):
        way, at = SLOTS[s]
        return pltpu.make_async_copy(stage.at[s], sends[way].at[at], out_sem.at[s])

    def tail_copy(s):
        way, at = SLOTS[s]
        rows = pl.ds(TT, RIM + 16)
        return pltpu.make_async_copy(stage.at[s, rows], sends[way].at[at, rows], out_sem.at[s])

    for s in range(len(SLOTS)):

        @pl.when(s < away)
        def _():
            pixel_copy(s).start()

    for a in range(TR):
        for i in range(CS + 2):
            row = a * CS + i
            if row == 0:
                cells = up[...]
            elif row == CR + 1:
                cells = down[...]
            else:
                cells = joined[(row - 1) * CC : row * CC, :]
            rims[a, i * CC : (i + 1) * CC, :] = cells
        edge = (CS + 2) * CC
        sides = dot(pick[0, a], left[...]) + dot(pick[1, a], right[...])
        rims[a, edge : edge + 16, :] = sides.astype(BF)
        rims[a, edge + 16 :, :] = jnp.zeros((RIM_K - edge - 16, JW), BF)
    for s in range(len(SLOTS)):

        @pl.when(s < away)
        def _():
            tile = chosen[keep + s]
            rim = dot(rim_pick[tile % TC], rims[tile // TC, :, :D])
            row = lax.broadcasted_iota(jnp.int32, rim.shape, 0)
            rim = jnp.where(row == RIM - 1, 1.0, rim).astype(BF)
            stage[s, TT : TT + RIM, :] = rim[:, :PD]
            for part in range(RIM // 16):
                cols = slice(part * GROUP, (part + 1) * GROUP)
                stage[s, TT + RIM :, cols] = rim[part * 16 : (part + 1) * 16, PD:]
            pixel_copy(s).wait()
            whole_copy(s).start()

        @pl.when(s >= away)
        def _():
            stage[s, TT:, :] = jnp.zeros((RIM + 16, PD), BF)
            tail_copy(s).start()

    for s in range(len(SLOTS)):

        @pl.when(s < away)
        def _():
            whole_copy(s).wait()

        @pl.when(s >= away)
        def _():
            tail_copy(s).wait()


def classify(tokens, normed, gain_head, head):
    normed[...] = layer_norm(tokens[...], gain_head[...]).astype(BF)
    answer = jnp.transpose(dot(normed[...], head[...]))
    return answer[:CLASSES].astype(BF)


def local_kernel(
    flags, pixels, rims, lift, gain_attn, gain_head, head_rows, patch_hbm, position_hbm, qkv_hbm, out_hbm,
    logits, chosen, buffer, sem, patch_weight, position, qkv_weight, out_weight, head, weight_sem, tokens, normed, packed, mixed,
):
    weights = Weights(
        [patch_hbm, position_hbm, qkv_hbm, out_hbm], [patch_weight, position, qkv_weight, out_weight], weight_sem
    )
    weights.start()
    keep, _ = list_flagged(flags, chosen)

    def fetch(k):
        return pltpu.make_async_copy(pixels.at[chosen[k]], buffer.at[k % 2], sem.at[k % 2])

    @pl.when(keep > 0)
    def _():
        fetch(0).start()

    spread_head(head_rows, head)
    coarse = []
    for a in range(TR):
        turned = jnp.transpose(rims[a, :, D:].astype(F32))
        coarse.append(turned[: 2 * CLASSES])
    coarse = jnp.concatenate(coarse, axis=0).astype(BF)
    for b in range(TC):
        fine = dot_nt(coarse, lift[b])
        for a in range(TR):
            at = a * 2 * CLASSES
            logits[a * TC + b] = (fine[at : at + CLASSES] + fine[at + CLASSES : at + 2 * CLASSES]).astype(BF)

    def work(k, carry):
        fetch(k).wait()

        @pl.when(k + 1 < keep)
        def _():
            fetch(k + 1).start()

        tile = chosen[k]
        embed = dot(buffer[k % 2], patch_weight[...])
        embed = embed + dot(lift[tile % TC], rims[tile // TC, :, :D])
        tokens[...] = embed + position[...].astype(F32)
        attend(tokens, normed, packed, mixed, gain_attn, qkv_weight, out_weight, lambda: None, lambda: None)
        logits[tile] = classify(tokens, normed, gain_head, head)
        return carry

    weights.need(0, 1, 2, 3)
    lax.fori_loop(0, keep, work, jnp.int32(0))


def remote_kernel(*refs):
    ways = len(SEND)
    got = refs[:ways]
    refs = refs[1:]
    rim_lift, gain_attn, gain_head, head_rows = refs[ways : ways + 4]
    sources = refs[ways + 4 : ways + 8]
    answers = refs[ways + 8 : 2 * ways + 8]
    filled, flag_rows, buffer, flag_sem, sem = refs[2 * ways + 8 : 2 * ways + 13]
    held = refs[2 * ways + 13 : 2 * ways + 17]
    head, weight_sem, tokens, normed, packed, mixed = refs[2 * ways + 17 :]
    patch_weight, position, qkv_weight, out_weight = held
    weights = Weights(sources, held, weight_sem)

    def flag_copy(s):
        way, at = SLOTS[s]
        return pltpu.make_async_copy(got[way].at[at, pl.ds(TT + RIM - 16, 16)], flag_rows.at[s], flag_sem.at[s])

    for s in range(len(SLOTS)):
        flag_copy(s).start()
    count = jnp.int32(0)
    for s in range(len(SLOTS)):
        flag_copy(s).wait()
        here = (jnp.max(flag_rows[s, :, :LANES].astype(F32)[15:16]) > 0.5).astype(jnp.int32)

        @pl.when(here == 1)
        def _():
            filled[count] = s

        count = count + here

    def each_slot(k, then):
        for s in range(len(SLOTS)):

            @pl.when(filled[k] == s)
            def _():
                then(*SLOTS[s])

    def fetch(k, way, at):
        return pltpu.make_async_copy(got[way].at[at], buffer.at[k % 2], sem.at[k % 2])

    @pl.when(count > 0)
    def _():
        each_slot(0, lambda way, at: fetch(0, way, at).start())
        weights.start()
        spread_head(head_rows, head)

    def work(k, carry):
        fetch(k, 0, 0).wait()

        @pl.when(k + 1 < count)
        def _():
            each_slot(k + 1, lambda way, at: fetch(k + 1, way, at).start())

        weights.first(k, 0, 1)
        slot = buffer.at[k % 2]
        tail = slot[TT + RIM :, :]
        rest = jnp.concatenate([tail[:, part * GROUP : (part + 1) * GROUP] for part in range(RIM // 16)], axis=0)
        place = position[...].astype(F32)
        embed = dot(slot[:TT, :], patch_weight[...])
        tokens[:, :PD] = embed[:, :PD] + dot(rim_lift[...], slot[TT : TT + RIM, :]) + place[:, :PD]
        tokens[:, PD:] = embed[:, PD:] + dot(rim_lift[...], rest) + place[:, PD:]
        attend(
            tokens, normed, packed, mixed, gain_attn, qkv_weight, out_weight,
            lambda: weights.first(k, 2), lambda: weights.first(k, 3),
        )
        answer = classify(tokens, normed, gain_head, head)

        def store(way, at):
            answers[way][at] = answer

        each_slot(k, store)
        return carry

    lax.fori_loop(0, count, work, jnp.int32(0))


def merge_kernel(flags, base, *refs):
    returned = refs[: len(SEND)]
    logits, chosen = refs[len(SEND) :]
    keep, away = list_flagged(flags, chosen)
    logits[...] = base[...]
    for s in range(len(SLOTS)):

        @pl.when(s < away)
        def _():
            way, at = SLOTS[s]
            logits[chosen[keep + s]] = returned[way][at]


def vmem():
    return pl.BlockSpec(memory_space=pltpu.VMEM)


def smem():
    return pl.BlockSpec(memory_space=pltpu.SMEM)


def hbm():
    return pl.BlockSpec(memory_space=pl.ANY)


def block_scratch(rows):
    return [
        pltpu.VMEM((rows, D), F32),
        pltpu.VMEM((rows, D), BF),
        pltpu.VMEM((rows, 3 * D), BF),
        pltpu.VMEM((rows, D), BF),
    ]


def weight_scratch(*more):
    return [
        pltpu.VMEM((PD, D), BF),
        pltpu.VMEM((TT, D), BF),
        pltpu.VMEM((D, 3 * D), BF),
        pltpu.VMEM((D, D), BF),
        *more,
        pltpu.VMEM((D, LANES), BF),
        pltpu.SemaphoreType.DMA((4 + len(more),)),
    ]


def glance(coarse_pixels, small, large, join_weight):
    rows = CR * CC
    return pl.pallas_call(
        glance_kernel,
        out_shape=jax.ShapeDtypeStruct((CR, CC, JW), BF),
        in_specs=[vmem()] * 4 + [hbm()] * 5,
        out_specs=vmem(),
        scratch_shapes=weight_scratch(pltpu.VMEM((D, D), BF)) + block_scratch(rows),
        compiler_params=params(),
        name="glance",
    )(coarse_pixels, *small, *large, join_weight)


def tile_cost(tiles):
    return pl.CostEstimate(flops=tiles * 3_500_000_000, bytes_accessed=12_000_000, transcendentals=0)


def params():
    return pltpu.CompilerParams(vmem_limit_bytes=VMEM_LIMIT)


def chosen_scratch():
    return pltpu.SMEM((TILES,), jnp.int32)


def pack(flags, pixels, joined, up, down, left, right, pick, rim_pick):
    return pl.pallas_call(
        pack_kernel,
        out_shape=[jax.ShapeDtypeStruct((TR, RIM_K, JW), BF)]
        + [jax.ShapeDtypeStruct((n, SLOT_ROWS, PD), BF) for n in SEND],
        in_specs=[smem(), hbm()] + [vmem()] * 7,
        out_specs=[vmem()] + [hbm()] * len(SEND),
        scratch_shapes=[
            chosen_scratch(),
            pltpu.VMEM((len(SLOTS), SLOT_ROWS, PD), BF),
            pltpu.SemaphoreType.DMA((len(SLOTS),)),
            pltpu.SemaphoreType.DMA((len(SLOTS),)),
        ],
        compiler_params=params(),
        name="pack",
    )(flags, pixels, joined, up, down, left, right, pick, rim_pick)


def focus_local(flags, pixels, rims, lift, small, large):
    return pl.pallas_call(
        local_kernel,
        out_shape=jax.ShapeDtypeStruct((TILES, CLASSES, TT), BF),
        in_specs=[smem(), hbm()] + [vmem()] * 5 + [hbm()] * 4,
        out_specs=vmem(),
        scratch_shapes=[
            chosen_scratch(),
            pltpu.VMEM((2, TT, PD), BF),
            pltpu.SemaphoreType.DMA((2,)),
        ]
        + weight_scratch()
        + block_scratch(TT),
        compiler_params=params(),
        cost_estimate=tile_cost(9),
        name="focus_local",
    )(flags, pixels, rims, lift, *small, *large)


def focus_remote(got, base, rim_lift, small, large):
    return pl.pallas_call(
        remote_kernel,
        out_shape=[jax.ShapeDtypeStruct((n, CLASSES, TT), BF) for n in SEND],
        in_specs=[hbm()] * (len(SEND) + 1) + [vmem()] * 4 + [hbm()] * 4,
        out_specs=[vmem()] * len(SEND),
        scratch_shapes=[
            pltpu.SMEM((len(SLOTS),), jnp.int32),
            pltpu.VMEM((len(SLOTS), 16, PD), BF),
            pltpu.VMEM((2, SLOT_ROWS, PD), BF),
            pltpu.SemaphoreType.DMA((len(SLOTS),)),
            pltpu.SemaphoreType.DMA((2,)),
        ]
        + weight_scratch()
        + block_scratch(TT),
        compiler_params=params(),
        cost_estimate=tile_cost(4),
        name="focus_remote",
    )(*got, base, rim_lift, *small, *large)


def merge(flags, base, returned):
    return pl.pallas_call(
        merge_kernel,
        out_shape=jax.ShapeDtypeStruct((TILES, CLASSES, TT), BF),
        in_specs=[smem()] + [vmem()] * (1 + len(SEND)),
        out_specs=vmem(),
        scratch_shapes=[chosen_scratch()],
        compiler_params=params(),
        name="merge",
    )(flags, base, *returned)


def routes():
    wide = lax.axis_size("wide")
    narrow = lax.axis_size("narrow")
    side = int(np.sqrt(wide))

    def along_x(step):
        return "wide", [(i, (i // side + step) % side * side + i % side) for i in range(wide)]

    def along_y(step):
        return "wide", [(i, i // side * side + (i % side + step) % side) for i in range(wide)]

    return [along_x(1), along_x(-1), along_y(1), along_y(-1), ("narrow", [(i, i ^ 1) for i in range(narrow)])]


def shifted(x, axis, step):
    count = lax.axis_size(axis)
    pairs = [(i, i + step) for i in range(count) if 0 <= i + step < count]
    return lax.ppermute(x, axis, pairs)


def borders(joined):
    wide_pos = lax.axis_index("wide")
    wide_end = lax.axis_size("wide") - 1
    narrow_pos = lax.axis_index("narrow")
    narrow_end = lax.axis_size("narrow") - 1
    up = jnp.where(wide_pos == 0, joined[0], shifted(joined[-1], "wide", 1))
    down = jnp.where(wide_pos == wide_end, joined[-1], shifted(joined[0], "wide", -1))
    blank = jnp.zeros((32 - CR - 2, JW), BF)
    first = jnp.concatenate([up[:1], joined[:, 0], down[:1], blank], axis=0)
    last = jnp.concatenate([up[-1:], joined[:, -1], down[-1:], blank], axis=0)
    left = jnp.where(narrow_pos == 0, first, shifted(last, "narrow", 1))
    right = jnp.where(narrow_pos == narrow_end, last, shifted(first, "narrow", -1))
    return up, down, left, right


def per_device(
    pixels,
    coarse_pixels,
    unsure,
    patch_weight,
    position,
    qkv_weight,
    out_weight,
    join_weight,
    gain_attn,
    gain_head,
    head_weight,
):
    tile_rows, tile_cols = unsure.shape
    flags = unsure.reshape(-1)
    gain_attn = gain_attn.reshape(1, D)
    gain_head = gain_head.reshape(1, D)
    small = (gain_attn, gain_head, head_weight.T)
    large = (patch_weight, position, qkv_weight, out_weight)
    lift = jnp.asarray(lift_tables(), BF)
    pick = jnp.asarray(side_tables(), BF)
    joined = glance(coarse_pixels, small, large, join_weight)
    up, down, left, right = borders(joined)
    rim_pick, rim_lift = (jnp.asarray(t, BF) for t in rim_tables())
    flat_pixels = pixels.reshape(TILES, TT, PD)
    flat_joined = joined.reshape(CR * CC, JW)
    rims, *sends = pack(flags, flat_pixels, flat_joined, up, down, left, right, pick, rim_pick)
    ways = routes()
    got = [lax.ppermute(block, axis, pairs) for block, (axis, pairs) in zip(sends, ways)]
    base = focus_local(flags, flat_pixels, rims, lift, small, large)
    answers = focus_remote(got, base, rim_lift, small, large)
    returned = [
        lax.ppermute(block, axis, [(b, a) for a, b in pairs]) for block, (axis, pairs) in zip(answers, ways)
    ]
    logits = merge(flags, base, returned)
    return logits.reshape(tile_rows, tile_cols, CLASSES, TT)


def solution(mesh):
    return jax.shard_map(
        per_device,
        mesh=mesh,
        in_specs=(
            P("wide", "narrow", None, None),
            P("wide", "narrow", None),
            P("wide", "narrow"),
            P(),
            P(),
            P(),
            P(),
            P(),
            P(),
            P(),
            P(),
        ),
        out_specs=P("wide", "narrow", None, None),
        check_vma=False,
    )
```

```python
import functools

import jax
import jax.numpy as jnp
import numpy as np
from jax import lax
from jax.experimental import pallas as pl
from jax.experimental.pallas import tpu as pltpu
from jax.sharding import PartitionSpec as P

D = 1024
HEADS = 16
HD = 64
PD = 768
CLASSES = 16
TS = 16
TT = 256
CS = 4
EPS = 1e-06
LOG2E = 1.4426950408889634
GROUP = 256
GROUP_HEADS = GROUP // HD
LANES = 128
JW = D + LANES
RIM_K = 256
TR = 4
TC = 8
TILES = TR * TC
CR = TR * CS
CC = TC * CS
KEEP = 7
SEND = (3, 3, 3, 3, 2)
SLOTS = ((4, 0), (0, 0), (2, 0), (1, 0), (3, 0), (4, 1), (0, 1), (2, 1), (1, 1), (3, 1), (0, 2), (2, 2), (1, 2), (3, 2))
RIM = 48
SLOT_ROWS = TT + RIM + 16
BF = jnp.bfloat16
F32 = jnp.float32
NT = (((1,), (1,)), ((), ()))
VMEM_LIMIT = 60 * 1024 * 1024


def interp_table():
    table = np.zeros((TS, CS + 2), np.float64)
    for p in range(TS):
        c = (2 * p - 3) / 8
        i = int(np.floor(c))
        table[p, i + 1] = 1 - (c - i)
        table[p, i + 2] = c - i
    return table


def rim_slots():
    slots = np.zeros((CS + 2, CC + 2), np.int64)
    for i in range(CS + 2):
        for c in range(1, CC + 1):
            slots[i, c] = i * CC + c - 1
        slots[i, 0] = (CS + 2) * CC + i
        slots[i, CC + 1] = (CS + 2) * CC + 8 + i
    return slots


def lift_tables():
    table = interp_table()
    slots = rim_slots()
    lift = np.zeros((TC, TT, RIM_K), np.float32)
    for b in range(TC):
        for i in range(CS + 2):
            for j in range(CS + 2):
                lift[b, :, slots[i, b * CS + j]] += np.outer(table[:, i], table[:, j]).reshape(-1)
    return lift


def side_tables():
    pick = np.zeros((2, TR, 16, 32), np.float32)
    for a in range(TR):
        for i in range(CS + 2):
            row = a * CS + i
            at = CR if row == 0 else CR + 1 if row == CR + 1 else row - 1
            pick[0, a, i, at] = 1
            pick[1, a, 8 + i, at] = 1
    return pick


def rim_tables():
    table = interp_table()
    slots = rim_slots()
    pick = np.zeros((TC, RIM, RIM_K), np.float32)
    lift = np.zeros((TT, RIM), np.float32)
    for i in range(CS + 2):
        for j in range(CS + 2):
            r = i * (CS + 2) + j
            lift[:, r] = np.outer(table[:, i], table[:, j]).reshape(-1)
            for b in range(TC):
                pick[b, r, slots[i, b * CS + j]] = 1
    return pick, lift


def dot(a, b):
    return jnp.dot(a, b, preferred_element_type=F32)


def dot_nt(a, b):
    return lax.dot_general(a, b, NT, preferred_element_type=F32)


def layer_norm(values, gain):
    center = values - jnp.mean(values, axis=-1, keepdims=True)
    spread = jnp.mean(center * center, axis=-1, keepdims=True)
    return center * lax.rsqrt(spread + EPS) * gain


def attend(tokens, normed, packed, mixed, gain_attn, qkv_weight, out_weight, need_qkv, need_out):
    count = tokens.shape[0] // TT
    normed[...] = layer_norm(tokens[...], gain_attn[...]).astype(BF)
    lane_head = lax.broadcasted_iota(jnp.int32, (TT, GROUP), 1) // HD
    need_qkv()
    for g in range(HEADS // GROUP_HEADS):
        for part in range(3):
            cols = slice(part * D + g * GROUP, part * D + (g + 1) * GROUP)
            packed[:, cols] = dot(normed[...], qkv_weight[:, cols]).astype(BF)
    for w in range(count):
        rows = slice(w * TT, (w + 1) * TT)
        for g in range(HEADS // GROUP_HEADS):
            queries = packed[rows, g * GROUP : (g + 1) * GROUP]
            keys = packed[rows, D + g * GROUP : D + (g + 1) * GROUP]
            values = packed[rows, 2 * D + g * GROUP : 2 * D + (g + 1) * GROUP]
            total = None
            norms = None
            for h in range(GROUP_HEADS):
                mine = lane_head == h
                scores = dot_nt(jnp.where(mine, queries, jnp.zeros_like(queries)), keys)
                top = jnp.max(scores, axis=-1, keepdims=True)
                weights = jnp.exp2((scores - top) * (HD ** (-0.5) * LOG2E))
                norm = 1.0 / jnp.sum(weights, axis=-1, keepdims=True)
                norms = norm if norms is None else jnp.where(lane_head >= h, norm, norms)
                term = dot(weights.astype(BF), jnp.where(mine, values, jnp.zeros_like(values)))
                total = term if total is None else total + term
            mixed[rows, g * GROUP : (g + 1) * GROUP] = (total * norms).astype(BF)
    need_out()
    for n in range(D // GROUP):
        cols = slice(n * GROUP, (n + 1) * GROUP)
        tokens[:, cols] = tokens[:, cols] + dot(mixed[...], out_weight[:, cols])


class Weights:
    def __init__(self, sources, scratch, sem):
        self.refs = scratch
        self.copies = [pltpu.make_async_copy(a, b, sem.at[i]) for i, (a, b) in enumerate(zip(sources, scratch))]

    def start(self):
        for copy in self.copies:
            copy.start()

    def need(self, *which):
        for i in which:
            self.copies[i].wait()

    def first(self, k, *which):
        @pl.when(k == 0)
        def _():
            self.need(*which)


def spread_head(head_rows, head):
    rows = head_rows[...].astype(F32)
    rows = jnp.concatenate([rows, rows, jnp.zeros((LANES - 2 * CLASSES, D), F32)], axis=0)
    head[...] = jnp.transpose(rows).astype(BF)


def glance_kernel(
    coarse, gain_attn, gain_head, head_rows, patch_hbm, position_hbm, qkv_hbm, out_hbm, join_hbm,
    joined, top, bottom, first, last, c00, c01, c10, c11,
    patch_weight, position, qkv_weight, out_weight, join_weight, head, sem, tokens, normed, packed, mixed,
):
    weights = Weights(
        [patch_hbm, position_hbm, qkv_hbm, out_hbm, join_hbm],
        [patch_weight, position, qkv_weight, out_weight, join_weight],
        sem,
    )
    weights.start()
    spread_head(head_rows, head)
    weights.need(0, 1)
    windows = CC // TS
    for w in range(windows):
        rows = slice(w * TT, (w + 1) * TT)
        cells = coarse[:, w * TS : (w + 1) * TS, :].reshape(TT, PD)
        tokens[rows, :] = dot(cells, patch_weight[...]) + position[...].astype(F32)
    attend(
        tokens, normed, packed, mixed, gain_attn, qkv_weight, out_weight, lambda: weights.need(2), lambda: weights.need(3)
    )
    features = tokens[...].astype(BF)
    normed[...] = layer_norm(features.astype(F32), gain_head[...]).astype(BF)
    mixed[...] = features
    logits = dot(normed[...], head[...])
    high = logits.astype(BF)
    low = (logits - high.astype(F32)).astype(BF)
    lane = lax.broadcasted_iota(jnp.int32, high.shape, 1)
    both = jnp.where(lane < CLASSES, high, low)
    weights.need(4)
    lifted = dot(mixed[...], join_weight[...]).astype(BF)
    for w in range(windows):
        rows = slice(w * TT, (w + 1) * TT)
        cols = slice(w * TS, (w + 1) * TS)
        joined[:, cols, :D] = lifted[rows].reshape(TS, TS, D)
        joined[:, cols, D:] = both[rows].reshape(TS, TS, LANES)
    top[...] = joined[0]
    bottom[...] = joined[CR - 1]
    c00[...] = joined[0, :16]
    c01[...] = joined[0, CC - 16 :]
    c10[...] = joined[CR - 1, :16]
    c11[...] = joined[CR - 1, CC - 16 :]
    first[...] = jnp.concatenate([joined[r, :16].astype(F32)[:1] for r in range(CR)], axis=0).astype(BF)
    last[...] = jnp.concatenate([joined[r, CC - 16 :].astype(F32)[15:] for r in range(CR)], axis=0).astype(BF)


def list_flagged(flags, chosen):
    def mark(t, count):
        @pl.when(flags[t] == 1)
        def _():
            chosen[count] = t

        return count + flags[t]

    count = lax.fori_loop(0, TILES, mark, jnp.int32(0))
    away = jnp.clip(count - KEEP, 0, len(SLOTS))
    return count - away, away


def pack_kernel(
    wide_end, narrow_end, place, flags, pixels, joined, top, bottom, first, last, up, down, left, right, ul, ur, dl, dr,
    pick, rim_pick, rims, *refs,
):
    sends = refs[: len(SEND)]
    chosen, stage, in_sem, out_sem, sides = refs[len(SEND) :]
    wide_pos = place[0]
    narrow_pos = place[1]
    keep, away = list_flagged(flags, chosen)

    def pixel_copy(s):
        return pltpu.make_async_copy(pixels.at[chosen[keep + s]], stage.at[s, pl.ds(0, TT)], in_sem.at[s])

    def whole_copy(s):
        way, at = SLOTS[s]
        return pltpu.make_async_copy(stage.at[s], sends[way].at[at], out_sem.at[s])

    def tail_copy(s):
        way, at = SLOTS[s]
        rows = pl.ds(TT + RIM - 16, 16)
        return pltpu.make_async_copy(stage.at[s, rows], sends[way].at[at, rows], out_sem.at[s])

    for s in range(len(SLOTS)):

        @pl.when(s < away)
        def _():
            pixel_copy(s).start()

    def pick_side(at_edge, own, got):
        return jnp.where(at_edge, own.astype(F32), got.astype(F32))

    over = pick_side(wide_pos == 0, top[...], up[...])
    under = pick_side(wide_pos == wide_end, bottom[...], down[...])
    row = lax.broadcasted_iota(jnp.int32, (16, JW), 0)
    columns = (
        (narrow_pos == 0, first, left, 0, ul, dl, 15),
        (narrow_pos == narrow_end, last, right, CC - 1, ur, dr, 0),
    )
    for side, (at_edge, own, got, end, high, low, at) in enumerate(columns):
        cells = pick_side(at_edge, own[...], got[...])
        corner = pick_side(at_edge, over[end : end + 1], high[...].astype(F32)[at : at + 1])
        corner = pick_side(wide_pos == 0, cells[:1], corner)
        foot = pick_side(at_edge, under[end : end + 1], low[...].astype(F32)[at : at + 1])
        foot = pick_side(wide_pos == wide_end, cells[CR - 1 :], foot)
        sides[side, :CR, :] = cells.astype(BF)
        sides[side, CR:, :] = jnp.where(row == 0, corner, jnp.where(row == 1, foot, 0.0)).astype(BF)
    over = over.astype(BF)
    under = under.astype(BF)
    for a in range(TR):
        for i in range(CS + 2):
            row = a * CS + i
            if row == 0:
                cells = over
            elif row == CR + 1:
                cells = under
            else:
                cells = joined[(row - 1) * CC : row * CC, :]
            rims[a, i * CC : (i + 1) * CC, :] = cells
        edge = (CS + 2) * CC
        block = dot(pick[0, a], sides[0]) + dot(pick[1, a], sides[1])
        rims[a, edge : edge + 16, :] = block.astype(BF)
        rims[a, edge + 16 :, :] = jnp.zeros((RIM_K - edge - 16, JW), BF)
    for s in range(len(SLOTS)):

        @pl.when(s < away)
        def _():
            tile = chosen[keep + s]
            rim = dot(rim_pick[tile % TC], rims[tile // TC, :, :D])
            row = lax.broadcasted_iota(jnp.int32, rim.shape, 0)
            rim = jnp.where(row == RIM - 1, 1.0, rim).astype(BF)
            stage[s, TT : TT + RIM, :] = rim[:, :PD]
            for part in range(RIM // 16):
                cols = slice(part * GROUP, (part + 1) * GROUP)
                stage[s, TT + RIM :, cols] = rim[part * 16 : (part + 1) * 16, PD:]
            pixel_copy(s).wait()
            whole_copy(s).start()

        @pl.when(s >= away)
        def _():
            stage[s, TT + RIM - 16 : TT + RIM, :] = jnp.zeros((16, PD), BF)
            tail_copy(s).start()

    for s in range(len(SLOTS)):

        @pl.when(s < away)
        def _():
            whole_copy(s).wait()

        @pl.when(s >= away)
        def _():
            tail_copy(s).wait()


def classify(tokens, normed, gain_head, head):
    normed[...] = layer_norm(tokens[...], gain_head[...]).astype(BF)
    answer = jnp.transpose(dot(normed[...], head[...]))
    return answer[:CLASSES].astype(BF)


def local_kernel(
    flags, pixels, rims, lift, gain_attn, gain_head, head_rows, patch_hbm, position_hbm, qkv_hbm, out_hbm,
    logits, chosen, buffer, sem, patch_weight, position, qkv_weight, out_weight, head, weight_sem, tokens, normed, packed, mixed,
):
    weights = Weights(
        [patch_hbm, position_hbm, qkv_hbm, out_hbm], [patch_weight, position, qkv_weight, out_weight], weight_sem
    )
    weights.start()
    keep, _ = list_flagged(flags, chosen)

    def fetch(k):
        return pltpu.make_async_copy(pixels.at[chosen[k]], buffer.at[k % 2], sem.at[k % 2])

    @pl.when(keep > 0)
    def _():
        fetch(0).start()

    spread_head(head_rows, head)
    coarse = []
    for a in range(TR):
        turned = jnp.transpose(rims[a, :, D:].astype(F32))
        coarse.append(turned[: 2 * CLASSES])
    coarse = jnp.concatenate(coarse, axis=0).astype(BF)
    for b in range(TC):
        fine = dot_nt(coarse, lift[b])
        for a in range(TR):
            at = a * 2 * CLASSES
            logits[a * TC + b] = (fine[at : at + CLASSES] + fine[at + CLASSES : at + 2 * CLASSES]).astype(BF)

    def work(k, carry):
        fetch(k).wait()

        @pl.when(k + 1 < keep)
        def _():
            fetch(k + 1).start()

        weights.first(k, 0, 1)
        tile = chosen[k]
        embed = dot(buffer[k % 2], patch_weight[...])
        embed = embed + dot(lift[tile % TC], rims[tile // TC, :, :D])
        tokens[...] = embed + position[...].astype(F32)
        attend(
            tokens, normed, packed, mixed, gain_attn, qkv_weight, out_weight,
            lambda: weights.first(k, 2), lambda: weights.first(k, 3),
        )
        logits[tile] = classify(tokens, normed, gain_head, head)
        return carry

    lax.fori_loop(0, keep, work, jnp.int32(0))

    @pl.when(keep == 0)
    def _():
        weights.need(0, 1, 2, 3)


def remote_kernel(*refs):
    ways = len(SEND)
    got = refs[:ways]
    refs = refs[1:]
    rim_lift, gain_attn, gain_head, head_rows = refs[ways : ways + 4]
    sources = refs[ways + 4 : ways + 8]
    answers = refs[ways + 8 : 2 * ways + 8]
    filled, flag_rows, buffer, flag_sem, sem = refs[2 * ways + 8 : 2 * ways + 13]
    held = refs[2 * ways + 13 : 2 * ways + 17]
    head, weight_sem, tokens, normed, packed, mixed = refs[2 * ways + 17 :]
    patch_weight, position, qkv_weight, out_weight = held
    weights = Weights(sources, held, weight_sem)

    def flag_copy(s):
        way, at = SLOTS[s]
        return pltpu.make_async_copy(got[way].at[at, pl.ds(TT + RIM - 16, 16)], flag_rows.at[s], flag_sem.at[s])

    for s in range(len(SLOTS)):
        flag_copy(s).start()
    count = jnp.int32(0)
    for s in range(len(SLOTS)):
        flag_copy(s).wait()
        here = (jnp.max(flag_rows[s, :, :LANES].astype(F32)[15:16]) > 0.5).astype(jnp.int32)

        @pl.when(here == 1)
        def _():
            filled[count] = s

        count = count + here

    def each_slot(k, then):
        for s in range(len(SLOTS)):

            @pl.when(filled[k] == s)
            def _():
                then(*SLOTS[s])

    def fetch(k, way, at):
        return pltpu.make_async_copy(got[way].at[at], buffer.at[k % 2], sem.at[k % 2])

    @pl.when(count > 0)
    def _():
        each_slot(0, lambda way, at: fetch(0, way, at).start())
        weights.start()
        spread_head(head_rows, head)

    def work(k, carry):
        fetch(k, 0, 0).wait()

        @pl.when(k + 1 < count)
        def _():
            each_slot(k + 1, lambda way, at: fetch(k + 1, way, at).start())

        weights.first(k, 0, 1)
        slot = buffer.at[k % 2]
        tail = slot[TT + RIM :, :]
        rest = jnp.concatenate([tail[:, part * GROUP : (part + 1) * GROUP] for part in range(RIM // 16)], axis=0)
        place = position[...].astype(F32)
        embed = dot(slot[:TT, :], patch_weight[...])
        tokens[:, :PD] = embed[:, :PD] + dot(rim_lift[...], slot[TT : TT + RIM, :]) + place[:, :PD]
        tokens[:, PD:] = embed[:, PD:] + dot(rim_lift[...], rest) + place[:, PD:]
        attend(
            tokens, normed, packed, mixed, gain_attn, qkv_weight, out_weight,
            lambda: weights.first(k, 2), lambda: weights.first(k, 3),
        )
        answer = classify(tokens, normed, gain_head, head)

        def store(way, at):
            answers[way][at] = answer

        each_slot(k, store)
        return carry

    lax.fori_loop(0, count, work, jnp.int32(0))


def merge_kernel(flags, base, *refs):
    returned = refs[: len(SEND)]
    logits, chosen = refs[len(SEND) :]
    keep, away = list_flagged(flags, chosen)
    logits[...] = base[...]
    for s in range(len(SLOTS)):

        @pl.when(s < away)
        def _():
            way, at = SLOTS[s]
            logits[chosen[keep + s]] = returned[way][at]


def vmem():
    return pl.BlockSpec(memory_space=pltpu.VMEM)


def smem():
    return pl.BlockSpec(memory_space=pltpu.SMEM)


def hbm():
    return pl.BlockSpec(memory_space=pl.ANY)


def block_scratch(rows):
    return [
        pltpu.VMEM((rows, D), F32),
        pltpu.VMEM((rows, D), BF),
        pltpu.VMEM((rows, 3 * D), BF),
        pltpu.VMEM((rows, D), BF),
    ]


def weight_scratch(*more):
    return [
        pltpu.VMEM((PD, D), BF),
        pltpu.VMEM((TT, D), BF),
        pltpu.VMEM((D, 3 * D), BF),
        pltpu.VMEM((D, D), BF),
        *more,
        pltpu.VMEM((D, LANES), BF),
        pltpu.SemaphoreType.DMA((4 + len(more),)),
    ]


def glance(coarse_pixels, small, large, join_weight):
    rows = CR * CC
    return pl.pallas_call(
        glance_kernel,
        out_shape=[jax.ShapeDtypeStruct((CR, CC, JW), BF)]
        + [jax.ShapeDtypeStruct((CC, JW), BF)] * 2
        + [jax.ShapeDtypeStruct((16, JW), BF)] * 6,
        in_specs=[vmem()] * 4 + [hbm()] * 5,
        out_specs=[vmem()] * 9,
        scratch_shapes=weight_scratch(pltpu.VMEM((D, D), BF)) + block_scratch(rows),
        compiler_params=params(),
        name="glance",
    )(coarse_pixels, *small, *large, join_weight)


def tile_cost(tiles):
    return pl.CostEstimate(flops=tiles * 3_500_000_000, bytes_accessed=12_000_000, transcendentals=0)


def params():
    return pltpu.CompilerParams(vmem_limit_bytes=VMEM_LIMIT)


def chosen_scratch():
    return pltpu.SMEM((TILES,), jnp.int32)


def pack(place, flags, pixels, joined, *cells):
    return pl.pallas_call(
        functools.partial(pack_kernel, lax.axis_size("wide") - 1, lax.axis_size("narrow") - 1),
        out_shape=[jax.ShapeDtypeStruct((TR, RIM_K, JW), BF)]
        + [jax.ShapeDtypeStruct((n, SLOT_ROWS, PD), BF) for n in SEND],
        in_specs=[smem(), smem(), hbm()] + [vmem()] * (1 + len(cells)),
        out_specs=[vmem()] + [hbm()] * len(SEND),
        scratch_shapes=[
            chosen_scratch(),
            pltpu.VMEM((len(SLOTS), SLOT_ROWS, PD), BF),
            pltpu.SemaphoreType.DMA((len(SLOTS),)),
            pltpu.SemaphoreType.DMA((len(SLOTS),)),
            pltpu.VMEM((2, 32, JW), BF),
        ],
        compiler_params=params(),
        name="pack",
    )(place, flags, pixels, joined, *cells)


def focus_local(flags, pixels, rims, lift, small, large):
    return pl.pallas_call(
        local_kernel,
        out_shape=jax.ShapeDtypeStruct((TILES, CLASSES, TT), BF),
        in_specs=[smem(), hbm()] + [vmem()] * 5 + [hbm()] * 4,
        out_specs=vmem(),
        scratch_shapes=[
            chosen_scratch(),
            pltpu.VMEM((2, TT, PD), BF),
            pltpu.SemaphoreType.DMA((2,)),
        ]
        + weight_scratch()
        + block_scratch(TT),
        compiler_params=params(),
        cost_estimate=tile_cost(9),
        name="focus_local",
    )(flags, pixels, rims, lift, *small, *large)


def focus_remote(got, base, rim_lift, small, large):
    return pl.pallas_call(
        remote_kernel,
        out_shape=[jax.ShapeDtypeStruct((n, CLASSES, TT), BF) for n in SEND],
        in_specs=[hbm()] * (len(SEND) + 1) + [vmem()] * 4 + [hbm()] * 4,
        out_specs=[vmem()] * len(SEND),
        scratch_shapes=[
            pltpu.SMEM((len(SLOTS),), jnp.int32),
            pltpu.VMEM((len(SLOTS), 16, PD), BF),
            pltpu.VMEM((2, SLOT_ROWS, PD), BF),
            pltpu.SemaphoreType.DMA((len(SLOTS),)),
            pltpu.SemaphoreType.DMA((2,)),
        ]
        + weight_scratch()
        + block_scratch(TT),
        compiler_params=params(),
        cost_estimate=tile_cost(4),
        name="focus_remote",
    )(*got, base, rim_lift, *small, *large)


def merge(flags, base, returned):
    return pl.pallas_call(
        merge_kernel,
        out_shape=jax.ShapeDtypeStruct((TILES, CLASSES, TT), BF),
        in_specs=[smem()] + [vmem()] * (1 + len(SEND)),
        out_specs=vmem(),
        scratch_shapes=[chosen_scratch()],
        compiler_params=params(),
        name="merge",
    )(flags, base, *returned)


def routes():
    wide = lax.axis_size("wide")
    narrow = lax.axis_size("narrow")
    side = int(np.sqrt(wide))

    def along_x(step):
        return "wide", [(i, (i // side + step) % side * side + i % side) for i in range(wide)]

    def along_y(step):
        return "wide", [(i, i // side * side + (i % side + step) % side) for i in range(wide)]

    return [along_x(1), along_x(-1), along_y(1), along_y(-1), ("narrow", [(i, i ^ 1) for i in range(narrow)])]


def shifted(x, down, across):
    wide = lax.axis_size("wide")
    narrow = lax.axis_size("narrow")
    pairs = [
        (w * narrow + n, (w + down) * narrow + n + across)
        for w in range(wide)
        for n in range(narrow)
        if 0 <= w + down < wide and 0 <= n + across < narrow
    ]
    return lax.ppermute(x, ("wide", "narrow"), pairs)


def per_device(
    pixels,
    coarse_pixels,
    unsure,
    patch_weight,
    position,
    qkv_weight,
    out_weight,
    join_weight,
    gain_attn,
    gain_head,
    head_weight,
):
    tile_rows, tile_cols = unsure.shape
    flags = unsure.reshape(-1)
    gain_attn = gain_attn.reshape(1, D)
    gain_head = gain_head.reshape(1, D)
    small = (gain_attn, gain_head, head_weight.T)
    large = (patch_weight, position, qkv_weight, out_weight)
    lift = jnp.asarray(lift_tables(), BF)
    pick = jnp.asarray(side_tables(), BF)
    joined, top, bottom, first, last, c00, c01, c10, c11 = glance(coarse_pixels, small, large, join_weight)
    borders = [
        shifted(bottom, 1, 0),
        shifted(top, -1, 0),
        shifted(last, 0, 1),
        shifted(first, 0, -1),
        shifted(c11, 1, 1),
        shifted(c10, 1, -1),
        shifted(c01, -1, 1),
        shifted(c00, -1, -1),
    ]
    place = jnp.stack([lax.axis_index("wide"), lax.axis_index("narrow")]).astype(jnp.int32)
    rim_pick, rim_lift = (jnp.asarray(t, BF) for t in rim_tables())
    flat_pixels = pixels.reshape(TILES, TT, PD)
    flat_joined = joined.reshape(CR * CC, JW)
    rims, *sends = pack(
        place, flags, flat_pixels, flat_joined, top, bottom, first, last, *borders, pick, rim_pick
    )
    ways = routes()
    got = [lax.ppermute(block, axis, pairs) for block, (axis, pairs) in zip(sends, ways)]
    base = focus_local(flags, flat_pixels, rims, lift, small, large)
    answers = focus_remote(got, base, rim_lift, small, large)
    returned = [
        lax.ppermute(block, axis, [(b, a) for a, b in pairs]) for block, (axis, pairs) in zip(answers, ways)
    ]
    logits = merge(flags, base, returned)
    return logits.reshape(tile_rows, tile_cols, CLASSES, TT)


def solution(mesh):
    return jax.shard_map(
        per_device,
        mesh=mesh,
        in_specs=(
            P("wide", "narrow", None, None),
            P("wide", "narrow", None),
            P("wide", "narrow"),
            P(),
            P(),
            P(),
            P(),
            P(),
            P(),
            P(),
            P(),
        ),
        out_specs=P("wide", "narrow", None, None),
        check_vma=False,
    )
```

```python
import functools

import jax
import jax.numpy as jnp
import numpy as np
from jax import lax
from jax.experimental import pallas as pl
from jax.experimental.pallas import tpu as pltpu
from jax.sharding import PartitionSpec as P

D = 1024
HEADS = 16
HD = 64
PD = 768
CLASSES = 16
TS = 16
TT = 256
CS = 4
EPS = 1e-06
LOG2E = 1.4426950408889634
GROUP = 256
GROUP_HEADS = GROUP // HD
LANES = 128
JW = D + LANES
RIM_K = 256
TR = 4
TC = 8
TILES = TR * TC
CR = TR * CS
CC = TC * CS
KEEP = 7
SEND = (4, 4, 4, 4)
SLOTS = tuple((way, at) for at in range(4) for way in (0, 2, 1, 3))
RIM = 48
SLOT_ROWS = TT + RIM + 16
BF = jnp.bfloat16
F32 = jnp.float32
NT = (((1,), (1,)), ((), ()))
VMEM_LIMIT = 60 * 1024 * 1024


def interp_table():
    table = np.zeros((TS, CS + 2), np.float64)
    for p in range(TS):
        c = (2 * p - 3) / 8
        i = int(np.floor(c))
        table[p, i + 1] = 1 - (c - i)
        table[p, i + 2] = c - i
    return table


def rim_slots():
    slots = np.zeros((CS + 2, CC + 2), np.int64)
    for i in range(CS + 2):
        for c in range(1, CC + 1):
            slots[i, c] = i * CC + c - 1
        slots[i, 0] = (CS + 2) * CC + i
        slots[i, CC + 1] = (CS + 2) * CC + 8 + i
    return slots


def lift_tables():
    table = interp_table()
    slots = rim_slots()
    lift = np.zeros((TC, TT, RIM_K), np.float32)
    for b in range(TC):
        for i in range(CS + 2):
            for j in range(CS + 2):
                lift[b, :, slots[i, b * CS + j]] += np.outer(table[:, i], table[:, j]).reshape(-1)
    return lift


def side_tables():
    pick = np.zeros((2, TR, 16, 32), np.float32)
    for a in range(TR):
        for i in range(CS + 2):
            row = a * CS + i
            at = CR if row == 0 else CR + 1 if row == CR + 1 else row - 1
            pick[0, a, i, at] = 1
            pick[1, a, 8 + i, at] = 1
    return pick


def rim_tables():
    table = interp_table()
    slots = rim_slots()
    pick = np.zeros((TC, RIM, RIM_K), np.float32)
    lift = np.zeros((TT, RIM), np.float32)
    for i in range(CS + 2):
        for j in range(CS + 2):
            r = i * (CS + 2) + j
            lift[:, r] = np.outer(table[:, i], table[:, j]).reshape(-1)
            for b in range(TC):
                pick[b, r, slots[i, b * CS + j]] = 1
    return pick, lift


def dot(a, b):
    return jnp.dot(a, b, preferred_element_type=F32)


def dot_nt(a, b):
    return lax.dot_general(a, b, NT, preferred_element_type=F32)


def layer_norm(values, gain):
    center = values - jnp.mean(values, axis=-1, keepdims=True)
    spread = jnp.mean(center * center, axis=-1, keepdims=True)
    return center * lax.rsqrt(spread + EPS) * gain


def attend(tokens, normed, packed, mixed, gain_attn, qkv_weight, out_weight, need_qkv, need_out):
    count = tokens.shape[0] // TT
    normed[...] = layer_norm(tokens[...], gain_attn[...]).astype(BF)
    lane_head = lax.broadcasted_iota(jnp.int32, (TT, GROUP), 1) // HD
    need_qkv()
    for g in range(HEADS // GROUP_HEADS):
        for part in range(3):
            cols = slice(part * D + g * GROUP, part * D + (g + 1) * GROUP)
            packed[:, cols] = dot(normed[...], qkv_weight[:, cols]).astype(BF)
    for w in range(count):
        rows = slice(w * TT, (w + 1) * TT)
        for g in range(HEADS // GROUP_HEADS):
            queries = packed[rows, g * GROUP : (g + 1) * GROUP]
            keys = packed[rows, D + g * GROUP : D + (g + 1) * GROUP]
            values = packed[rows, 2 * D + g * GROUP : 2 * D + (g + 1) * GROUP]
            total = None
            norms = None
            for h in range(GROUP_HEADS):
                mine = lane_head == h
                scores = dot_nt(jnp.where(mine, queries, jnp.zeros_like(queries)), keys)
                top = jnp.max(scores, axis=-1, keepdims=True)
                weights = jnp.exp2((scores - top) * (HD ** (-0.5) * LOG2E))
                norm = 1.0 / jnp.sum(weights, axis=-1, keepdims=True)
                norms = norm if norms is None else jnp.where(lane_head >= h, norm, norms)
                term = dot(weights.astype(BF), jnp.where(mine, values, jnp.zeros_like(values)))
                total = term if total is None else total + term
            mixed[rows, g * GROUP : (g + 1) * GROUP] = (total * norms).astype(BF)
    need_out()
    for n in range(D // GROUP):
        cols = slice(n * GROUP, (n + 1) * GROUP)
        tokens[:, cols] = tokens[:, cols] + dot(mixed[...], out_weight[:, cols])


class Weights:
    def __init__(self, sources, scratch, sem):
        self.refs = scratch
        self.copies = [pltpu.make_async_copy(a, b, sem.at[i]) for i, (a, b) in enumerate(zip(sources, scratch))]

    def start(self):
        for copy in self.copies:
            copy.start()

    def need(self, *which):
        for i in which:
            self.copies[i].wait()


def spread_head(head_rows, head):
    rows = head_rows[...].astype(F32)
    rows = jnp.concatenate([rows, rows, jnp.zeros((LANES - 2 * CLASSES, D), F32)], axis=0)
    head[...] = jnp.transpose(rows).astype(BF)


def glance_kernel(
    coarse, gain_attn, gain_head, head_rows, patch_hbm, position_hbm, qkv_hbm, out_hbm, join_hbm,
    joined, top, bottom, first, last,
    patch_weight, position, qkv_weight, out_weight, join_weight, head, sem, tokens, normed, packed, mixed,
):
    weights = Weights(
        [patch_hbm, position_hbm, qkv_hbm, out_hbm, join_hbm],
        [patch_weight, position, qkv_weight, out_weight, join_weight],
        sem,
    )
    weights.start()
    spread_head(head_rows, head)
    weights.need(0, 1)
    windows = CC // TS
    for w in range(windows):
        rows = slice(w * TT, (w + 1) * TT)
        cells = coarse[:, w * TS : (w + 1) * TS, :].reshape(TT, PD)
        tokens[rows, :] = dot(cells, patch_weight[...]) + position[...].astype(F32)
    attend(
        tokens, normed, packed, mixed, gain_attn, qkv_weight, out_weight, lambda: weights.need(2), lambda: weights.need(3)
    )
    features = tokens[...].astype(BF)
    normed[...] = layer_norm(features.astype(F32), gain_head[...]).astype(BF)
    mixed[...] = features
    logits = dot(normed[...], head[...])
    high = logits.astype(BF)
    low = (logits - high.astype(F32)).astype(BF)
    lane = lax.broadcasted_iota(jnp.int32, high.shape, 1)
    both = jnp.where(lane < CLASSES, high, low)
    weights.need(4)
    lifted = dot(mixed[...], join_weight[...]).astype(BF)
    for w in range(windows):
        rows = slice(w * TT, (w + 1) * TT)
        cols = slice(w * TS, (w + 1) * TS)
        joined[:, cols, :D] = lifted[rows].reshape(TS, TS, D)
        joined[:, cols, D:] = both[rows].reshape(TS, TS, LANES)
    top[...] = joined[0]
    bottom[...] = joined[CR - 1]
    blank = jnp.zeros((16, JW), F32)
    first[...] = jnp.concatenate([joined[r, :16].astype(F32)[:1] for r in range(CR)] + [blank], axis=0).astype(BF)
    last[...] = jnp.concatenate([joined[r, CC - 16 :].astype(F32)[15:] for r in range(CR)] + [blank], axis=0).astype(BF)


def list_flagged(flags, chosen):
    def mark(t, count):
        @pl.when(flags[t] == 1)
        def _():
            chosen[count] = t

        return count + flags[t]

    count = lax.fori_loop(0, TILES, mark, jnp.int32(0))
    away = jnp.clip(count - KEEP, 0, len(SLOTS))
    return count - away, away


def pack_kernel(
    wide_end, narrow_end, place, flags, pixels, joined, top, bottom, first, last, up, down, left, right,
    pick, rim_pick, rims, *refs,
):
    sends = refs[: len(SEND)]
    chosen, stage, in_sem, out_sem, sides = refs[len(SEND) :]
    wide_pos = place[0]
    narrow_pos = place[1]
    keep, away = list_flagged(flags, chosen)

    def pixel_copy(s):
        return pltpu.make_async_copy(pixels.at[chosen[keep + s]], stage.at[s, pl.ds(0, TT)], in_sem.at[s])

    def whole_copy(s):
        way, at = SLOTS[s]
        return pltpu.make_async_copy(stage.at[s], sends[way].at[at], out_sem.at[s])

    def tail_copy(s):
        way, at = SLOTS[s]
        rows = pl.ds(TT + RIM - 16, 16)
        return pltpu.make_async_copy(stage.at[s, rows], sends[way].at[at, rows], out_sem.at[s])

    for s in range(len(SLOTS)):

        @pl.when(s < away)
        def _():
            pixel_copy(s).start()

    def pick_side(at_edge, own, got):
        return jnp.where(at_edge, own.astype(F32), got.astype(F32))

    over = pick_side(wide_pos == 0, top[...], up[...]).astype(BF)
    under = pick_side(wide_pos == wide_end, bottom[...], down[...]).astype(BF)
    sides[0] = pick_side(narrow_pos == 0, first[...], left[...]).astype(BF)
    sides[1] = pick_side(narrow_pos == narrow_end, last[...], right[...]).astype(BF)
    for a in range(TR):
        for i in range(CS + 2):
            row = a * CS + i
            if row == 0:
                cells = over
            elif row == CR + 1:
                cells = under
            else:
                cells = joined[(row - 1) * CC : row * CC, :]
            rims[a, i * CC : (i + 1) * CC, :] = cells
        edge = (CS + 2) * CC
        block = dot(pick[0, a], sides[0]) + dot(pick[1, a], sides[1])
        rims[a, edge : edge + 16, :] = block.astype(BF)
        rims[a, edge + 16 :, :] = jnp.zeros((RIM_K - edge - 16, JW), BF)
    for s in range(len(SLOTS)):

        @pl.when(s < away)
        def _():
            tile = chosen[keep + s]
            rim = dot(rim_pick[tile % TC], rims[tile // TC, :, :D])
            row = lax.broadcasted_iota(jnp.int32, rim.shape, 0)
            rim = jnp.where(row == RIM - 1, 1.0, rim).astype(BF)
            stage[s, TT : TT + RIM, :] = rim[:, :PD]
            for part in range(RIM // 16):
                cols = slice(part * GROUP, (part + 1) * GROUP)
                stage[s, TT + RIM :, cols] = rim[part * 16 : (part + 1) * 16, PD:]
            pixel_copy(s).wait()
            whole_copy(s).start()

        @pl.when(s >= away)
        def _():
            stage[s, TT + RIM - 16 : TT + RIM, :] = jnp.zeros((16, PD), BF)
            tail_copy(s).start()

    for s in range(len(SLOTS)):

        @pl.when(s < away)
        def _():
            whole_copy(s).wait()

        @pl.when(s >= away)
        def _():
            tail_copy(s).wait()


def classify(tokens, normed, gain_head, head):
    normed[...] = layer_norm(tokens[...], gain_head[...]).astype(BF)
    answer = jnp.transpose(dot(normed[...], head[...]))
    return answer[:CLASSES].astype(BF)


def local_kernel(
    flags, pixels, rims, lift, gain_attn, gain_head, head_rows, patch_hbm, position_hbm, qkv_hbm, out_hbm,
    logits, chosen, buffer, sem, patch_weight, position, qkv_weight, out_weight, head, weight_sem, tokens, normed, packed, mixed,
):
    weights = Weights(
        [patch_hbm, position_hbm, qkv_hbm, out_hbm], [patch_weight, position, qkv_weight, out_weight], weight_sem
    )
    weights.start()
    keep, _ = list_flagged(flags, chosen)

    def fetch(k):
        return pltpu.make_async_copy(pixels.at[chosen[k]], buffer.at[k % 2], sem.at[k % 2])

    @pl.when(keep > 0)
    def _():
        fetch(0).start()

    spread_head(head_rows, head)
    coarse = []
    for a in range(TR):
        turned = jnp.transpose(rims[a, :, D:].astype(F32))
        coarse.append(turned[: 2 * CLASSES])
    coarse = jnp.concatenate(coarse, axis=0).astype(BF)
    for b in range(TC):
        fine = dot_nt(coarse, lift[b])
        for a in range(TR):
            at = a * 2 * CLASSES
            logits[a * TC + b] = (fine[at : at + CLASSES] + fine[at + CLASSES : at + 2 * CLASSES]).astype(BF)

    def work(k, carry, need=lambda *which: None):
        fetch(k).wait()

        @pl.when(k + 1 < keep)
        def _():
            fetch(k + 1).start()

        need(0, 1)
        tile = chosen[k]
        embed = dot(buffer[k % 2], patch_weight[...])
        embed = embed + dot(lift[tile % TC], rims[tile // TC, :, :D])
        tokens[...] = embed + position[...].astype(F32)
        attend(
            tokens, normed, packed, mixed, gain_attn, qkv_weight, out_weight,
            lambda: need(2), lambda: need(3),
        )
        logits[tile] = classify(tokens, normed, gain_head, head)
        return carry

    @pl.when(keep > 0)
    def _():
        work(jnp.int32(0), None, weights.need)

    lax.fori_loop(1, keep, work, jnp.int32(0))

    @pl.when(keep == 0)
    def _():
        weights.need(0, 1, 2, 3)


def remote_kernel(*refs):
    ways = len(SEND)
    got = refs[:ways]
    refs = refs[1:]
    rim_lift, gain_attn, gain_head, head_rows = refs[ways : ways + 4]
    sources = refs[ways + 4 : ways + 8]
    answers = refs[ways + 8 : 2 * ways + 8]
    filled, flag_rows, buffer, flag_sem, sem = refs[2 * ways + 8 : 2 * ways + 13]
    held = refs[2 * ways + 13 : 2 * ways + 17]
    head, weight_sem, tokens, normed, packed, mixed = refs[2 * ways + 17 :]
    patch_weight, position, qkv_weight, out_weight = held
    weights = Weights(sources, held, weight_sem)

    def flag_copy(s):
        way, at = SLOTS[s]
        return pltpu.make_async_copy(got[way].at[at, pl.ds(TT + RIM - 16, 16)], flag_rows.at[s], flag_sem.at[s])

    for s in range(len(SLOTS)):
        flag_copy(s).start()
    count = jnp.int32(0)
    for s in range(len(SLOTS)):
        flag_copy(s).wait()
        here = (jnp.max(flag_rows[s, :, :LANES].astype(F32)[15:16]) > 0.5).astype(jnp.int32)

        @pl.when(here == 1)
        def _():
            filled[count] = s

        count = count + here

    def each_slot(k, then):
        for s in range(len(SLOTS)):

            @pl.when(filled[k] == s)
            def _():
                then(*SLOTS[s])

    def fetch(k, way, at):
        return pltpu.make_async_copy(got[way].at[at], buffer.at[k % 2], sem.at[k % 2])

    @pl.when(count > 0)
    def _():
        each_slot(0, lambda way, at: fetch(0, way, at).start())
        weights.start()
        spread_head(head_rows, head)

    def work(k, carry, need=lambda *which: None):
        fetch(k, 0, 0).wait()

        @pl.when(k + 1 < count)
        def _():
            each_slot(k + 1, lambda way, at: fetch(k + 1, way, at).start())

        need(0, 1)
        slot = buffer.at[k % 2]
        tail = slot[TT + RIM :, :]
        rest = jnp.concatenate([tail[:, part * GROUP : (part + 1) * GROUP] for part in range(RIM // 16)], axis=0)
        place = position[...].astype(F32)
        embed = dot(slot[:TT, :], patch_weight[...])
        tokens[:, :PD] = embed[:, :PD] + dot(rim_lift[...], slot[TT : TT + RIM, :]) + place[:, :PD]
        tokens[:, PD:] = embed[:, PD:] + dot(rim_lift[...], rest) + place[:, PD:]
        attend(
            tokens, normed, packed, mixed, gain_attn, qkv_weight, out_weight,
            lambda: need(2), lambda: need(3),
        )
        answer = classify(tokens, normed, gain_head, head)

        def store(way, at):
            answers[way][at] = answer

        each_slot(k, store)
        return carry

    @pl.when(count > 0)
    def _():
        work(jnp.int32(0), None, weights.need)

    lax.fori_loop(1, count, work, jnp.int32(0))


def merge_kernel(flags, base, *refs):
    returned = refs[: len(SEND)]
    logits, chosen = refs[len(SEND) :]
    keep, away = list_flagged(flags, chosen)
    logits[...] = base[...]
    for s in range(len(SLOTS)):

        @pl.when(s < away)
        def _():
            way, at = SLOTS[s]
            logits[chosen[keep + s]] = returned[way][at]


def vmem():
    return pl.BlockSpec(memory_space=pltpu.VMEM)


def smem():
    return pl.BlockSpec(memory_space=pltpu.SMEM)


def hbm():
    return pl.BlockSpec(memory_space=pl.ANY)


def block_scratch(rows):
    return [
        pltpu.VMEM((rows, D), F32),
        pltpu.VMEM((rows, D), BF),
        pltpu.VMEM((rows, 3 * D), BF),
        pltpu.VMEM((rows, D), BF),
    ]


def weight_scratch(*more):
    return [
        pltpu.VMEM((PD, D), BF),
        pltpu.VMEM((TT, D), BF),
        pltpu.VMEM((D, 3 * D), BF),
        pltpu.VMEM((D, D), BF),
        *more,
        pltpu.VMEM((D, LANES), BF),
        pltpu.SemaphoreType.DMA((4 + len(more),)),
    ]


def glance(coarse_pixels, small, large, join_weight):
    rows = CR * CC
    return pl.pallas_call(
        glance_kernel,
        out_shape=[jax.ShapeDtypeStruct((CR, CC, JW), BF)]
        + [jax.ShapeDtypeStruct((CC, JW), BF)] * 4,
        in_specs=[vmem()] * 4 + [hbm()] * 5,
        out_specs=[vmem()] * 5,
        scratch_shapes=weight_scratch(pltpu.VMEM((D, D), BF)) + block_scratch(rows),
        compiler_params=params(),
        name="glance",
    )(coarse_pixels, *small, *large, join_weight)


def tile_cost(tiles):
    return pl.CostEstimate(flops=tiles * 3_500_000_000, bytes_accessed=12_000_000, transcendentals=0)


def params():
    return pltpu.CompilerParams(vmem_limit_bytes=VMEM_LIMIT)


def chosen_scratch():
    return pltpu.SMEM((TILES,), jnp.int32)


def pack(place, flags, pixels, joined, *cells):
    return pl.pallas_call(
        functools.partial(pack_kernel, lax.axis_size("wide") - 1, lax.axis_size("narrow") - 1),
        out_shape=[jax.ShapeDtypeStruct((TR, RIM_K, JW), BF)]
        + [jax.ShapeDtypeStruct((n, SLOT_ROWS, PD), BF) for n in SEND],
        in_specs=[smem(), smem(), hbm()] + [vmem()] * (1 + len(cells)),
        out_specs=[vmem()] + [hbm()] * len(SEND),
        scratch_shapes=[
            chosen_scratch(),
            pltpu.VMEM((len(SLOTS), SLOT_ROWS, PD), BF),
            pltpu.SemaphoreType.DMA((len(SLOTS),)),
            pltpu.SemaphoreType.DMA((len(SLOTS),)),
            pltpu.VMEM((2, 32, JW), BF),
        ],
        compiler_params=params(),
        name="pack",
    )(place, flags, pixels, joined, *cells)


def focus_local(flags, pixels, rims, lift, small, large):
    return pl.pallas_call(
        local_kernel,
        out_shape=jax.ShapeDtypeStruct((TILES, CLASSES, TT), BF),
        in_specs=[smem(), hbm()] + [vmem()] * 5 + [hbm()] * 4,
        out_specs=vmem(),
        scratch_shapes=[
            chosen_scratch(),
            pltpu.VMEM((2, TT, PD), BF),
            pltpu.SemaphoreType.DMA((2,)),
        ]
        + weight_scratch()
        + block_scratch(TT),
        compiler_params=params(),
        cost_estimate=tile_cost(9),
        name="focus_local",
    )(flags, pixels, rims, lift, *small, *large)


def focus_remote(got, base, rim_lift, small, large):
    return pl.pallas_call(
        remote_kernel,
        out_shape=[jax.ShapeDtypeStruct((n, CLASSES, TT), BF) for n in SEND],
        in_specs=[hbm()] * (len(SEND) + 1) + [vmem()] * 4 + [hbm()] * 4,
        out_specs=[vmem()] * len(SEND),
        scratch_shapes=[
            pltpu.SMEM((len(SLOTS),), jnp.int32),
            pltpu.VMEM((len(SLOTS), 16, PD), BF),
            pltpu.VMEM((2, SLOT_ROWS, PD), BF),
            pltpu.SemaphoreType.DMA((len(SLOTS),)),
            pltpu.SemaphoreType.DMA((2,)),
        ]
        + weight_scratch()
        + block_scratch(TT),
        compiler_params=params(),
        cost_estimate=tile_cost(4),
        name="focus_remote",
    )(*got, base, rim_lift, *small, *large)


def merge(flags, base, returned):
    return pl.pallas_call(
        merge_kernel,
        out_shape=jax.ShapeDtypeStruct((TILES, CLASSES, TT), BF),
        in_specs=[smem()] + [vmem()] * (1 + len(SEND)),
        out_specs=vmem(),
        scratch_shapes=[chosen_scratch()],
        compiler_params=params(),
        name="merge",
    )(flags, base, *returned)


def routes():
    wide = lax.axis_size("wide")
    side = int(np.sqrt(wide))

    def along_x(step):
        return "wide", [(i, (i // side + step) % side * side + i % side) for i in range(wide)]

    def along_y(step):
        return "wide", [(i, i // side * side + (i % side + step) % side) for i in range(wide)]

    return [along_x(1), along_x(-1), along_y(1), along_y(-1)]


def shifted(x, axis, step):
    count = lax.axis_size(axis)
    pairs = [(i, i + step) for i in range(count) if 0 <= i + step < count]
    return lax.ppermute(x, axis, pairs)


def cornered(column, above, below):
    blank = jnp.zeros((32 - CR - 2, JW), BF)
    return jnp.concatenate([column[:CR], above, below, blank], axis=0)


def per_device(
    pixels,
    coarse_pixels,
    unsure,
    patch_weight,
    position,
    qkv_weight,
    out_weight,
    join_weight,
    gain_attn,
    gain_head,
    head_weight,
):
    tile_rows, tile_cols = unsure.shape
    flags = unsure.reshape(-1)
    gain_attn = gain_attn.reshape(1, D)
    gain_head = gain_head.reshape(1, D)
    small = (gain_attn, gain_head, head_weight.T)
    large = (patch_weight, position, qkv_weight, out_weight)
    lift = jnp.asarray(lift_tables(), BF)
    pick = jnp.asarray(side_tables(), BF)
    joined, top, bottom, first, last = glance(coarse_pixels, small, large, join_weight)
    up = shifted(bottom, "wide", 1)
    down = shifted(top, "wide", -1)
    wide_pos = lax.axis_index("wide")
    first_row = wide_pos == 0
    last_row = wide_pos == lax.axis_size("wide") - 1
    first = cornered(first, jnp.where(first_row, top[:1], up[:1]), jnp.where(last_row, bottom[:1], down[:1]))
    last = cornered(last, jnp.where(first_row, top[-1:], up[-1:]), jnp.where(last_row, bottom[-1:], down[-1:]))
    borders = [up, down, shifted(last, "narrow", 1), shifted(first, "narrow", -1)]
    place = jnp.stack([lax.axis_index("wide"), lax.axis_index("narrow")]).astype(jnp.int32)
    rim_pick, rim_lift = (jnp.asarray(t, BF) for t in rim_tables())
    flat_pixels = pixels.reshape(TILES, TT, PD)
    flat_joined = joined.reshape(CR * CC, JW)
    rims, *sends = pack(
        place, flags, flat_pixels, flat_joined, top, bottom, first, last, *borders, pick, rim_pick
    )
    ways = routes()
    got = [lax.ppermute(block, axis, pairs) for block, (axis, pairs) in zip(sends, ways)]
    base = focus_local(flags, flat_pixels, rims, lift, small, large)
    answers = focus_remote(got, base, rim_lift, small, large)
    returned = [
        lax.ppermute(block, axis, [(b, a) for a, b in pairs]) for block, (axis, pairs) in zip(answers, ways)
    ]
    logits = merge(flags, base, returned)
    return logits.reshape(tile_rows, tile_cols, CLASSES, TT)


def solution(mesh):
    return jax.shard_map(
        per_device,
        mesh=mesh,
        in_specs=(
            P("wide", "narrow", None, None),
            P("wide", "narrow", None),
            P("wide", "narrow"),
            P(),
            P(),
            P(),
            P(),
            P(),
            P(),
            P(),
            P(),
        ),
        out_specs=P("wide", "narrow", None, None),
        check_vma=False,
    )
```

```python
import functools

import jax
import jax.numpy as jnp
import numpy as np
from jax import lax
from jax.experimental import pallas as pl
from jax.experimental.pallas import tpu as pltpu
from jax.sharding import PartitionSpec as P

D = 1024
HEADS = 16
HD = 64
PD = 768
CLASSES = 16
TS = 16
TT = 256
CS = 4
EPS = 1e-06
LOG2E = 1.4426950408889634
GROUP = 256
GROUP_HEADS = GROUP // HD
LANES = 128
JW = D + LANES
RIM_K = 256
TR = 4
TC = 8
TILES = TR * TC
CR = TR * CS
CC = TC * CS
KEEP = 7
SEND = (4, 4, 4, 4)
SLOTS = tuple((way, at) for at in range(4) for way in (0, 2, 1, 3))
RIM = 48
SLOT_ROWS = TT + RIM + 16
BF = jnp.bfloat16
F32 = jnp.float32
NT = (((1,), (1,)), ((), ()))
MIB = 1024 * 1024


def interp_table():
    table = np.zeros((TS, CS + 2), np.float64)
    for p in range(TS):
        c = (2 * p - 3) / 8
        i = int(np.floor(c))
        table[p, i + 1] = 1 - (c - i)
        table[p, i + 2] = c - i
    return table


def rim_slots():
    slots = np.zeros((CS + 2, CC + 2), np.int64)
    for i in range(CS + 2):
        for c in range(1, CC + 1):
            slots[i, c] = i * CC + c - 1
        slots[i, 0] = (CS + 2) * CC + i
        slots[i, CC + 1] = (CS + 2) * CC + 8 + i
    return slots


def lift_tables():
    table = interp_table()
    slots = rim_slots()
    lift = np.zeros((TC, TT, RIM_K), np.float32)
    for b in range(TC):
        for i in range(CS + 2):
            for j in range(CS + 2):
                lift[b, :, slots[i, b * CS + j]] += np.outer(table[:, i], table[:, j]).reshape(-1)
    return lift


def side_tables():
    pick = np.zeros((2, TR, 16, 32), np.float32)
    for a in range(TR):
        for i in range(CS + 2):
            row = a * CS + i
            at = CR if row == 0 else CR + 1 if row == CR + 1 else row - 1
            pick[0, a, i, at] = 1
            pick[1, a, 8 + i, at] = 1
    return pick


def rim_tables():
    table = interp_table()
    slots = rim_slots()
    pick = np.zeros((TC, RIM, RIM_K), np.float32)
    lift = np.zeros((TT, RIM), np.float32)
    for i in range(CS + 2):
        for j in range(CS + 2):
            r = i * (CS + 2) + j
            lift[:, r] = np.outer(table[:, i], table[:, j]).reshape(-1)
            for b in range(TC):
                pick[b, r, slots[i, b * CS + j]] = 1
    return pick, lift


def dot(a, b):
    return jnp.dot(a, b, preferred_element_type=F32)


def dot_nt(a, b):
    return lax.dot_general(a, b, NT, preferred_element_type=F32)


def layer_norm(values, gain):
    center = values - jnp.mean(values, axis=-1, keepdims=True)
    spread = jnp.mean(center * center, axis=-1, keepdims=True)
    return center * lax.rsqrt(spread + EPS) * gain


def attend(tokens, normed, packed, mixed, gain_attn, qkv_weight, out_weight, need_qkv, need_out):
    count = tokens.shape[0] // TT
    normed[...] = layer_norm(tokens[...], gain_attn[...]).astype(BF)
    lane_head = lax.broadcasted_iota(jnp.int32, (TT, GROUP), 1) // HD
    need_qkv()
    for g in range(HEADS // GROUP_HEADS):
        for part in range(3):
            cols = slice(part * D + g * GROUP, part * D + (g + 1) * GROUP)
            packed[:, cols] = dot(normed[...], qkv_weight[:, cols]).astype(BF)
    for w in range(count):
        rows = slice(w * TT, (w + 1) * TT)
        for g in range(HEADS // GROUP_HEADS):
            queries = packed[rows, g * GROUP : (g + 1) * GROUP]
            keys = packed[rows, D + g * GROUP : D + (g + 1) * GROUP]
            values = packed[rows, 2 * D + g * GROUP : 2 * D + (g + 1) * GROUP]
            total = None
            norms = None
            for h in range(GROUP_HEADS):
                mine = lane_head == h
                scores = dot_nt(jnp.where(mine, queries, jnp.zeros_like(queries)), keys)
                top = jnp.max(scores, axis=-1, keepdims=True)
                weights = jnp.exp2((scores - top) * (HD ** (-0.5) * LOG2E))
                norm = 1.0 / jnp.sum(weights, axis=-1, keepdims=True)
                norms = norm if norms is None else jnp.where(lane_head >= h, norm, norms)
                term = dot(weights.astype(BF), jnp.where(mine, values, jnp.zeros_like(values)))
                total = term if total is None else total + term
            mixed[rows, g * GROUP : (g + 1) * GROUP] = (total * norms).astype(BF)
    need_out()
    for n in range(D // GROUP):
        cols = slice(n * GROUP, (n + 1) * GROUP)
        tokens[:, cols] = tokens[:, cols] + dot(mixed[...], out_weight[:, cols])


class Weights:
    def __init__(self, sources, scratch, sem):
        self.refs = scratch
        self.copies = [pltpu.make_async_copy(a, b, sem.at[i]) for i, (a, b) in enumerate(zip(sources, scratch))]

    def start(self, *which):
        for i in which:
            self.copies[i].start()

    def need(self, *which):
        for i in which:
            self.copies[i].wait()


def spread_head(head_rows, head):
    rows = head_rows[...].astype(F32)
    rows = jnp.concatenate([rows, rows, jnp.zeros((LANES - 2 * CLASSES, D), F32)], axis=0)
    head[...] = jnp.transpose(rows).astype(BF)


def glance_kernel(
    coarse, gain_attn, gain_head, head_rows, patch_hbm, position_hbm, qkv_hbm, out_hbm, join_hbm,
    joined, top, bottom, first, last,
    patch_weight, position, qkv_weight, out_weight, join_weight, head, sem, tokens, normed, packed, mixed,
):
    weights = Weights(
        [patch_hbm, position_hbm, qkv_hbm, out_hbm, join_hbm],
        [patch_weight, position, qkv_weight, out_weight, join_weight],
        sem,
    )
    weights.start(0, 1, 2, 3, 4)
    spread_head(head_rows, head)
    weights.need(0, 1)
    windows = CC // TS
    for w in range(windows):
        rows = slice(w * TT, (w + 1) * TT)
        cells = coarse[:, w * TS : (w + 1) * TS, :].reshape(TT, PD)
        tokens[rows, :] = dot(cells, patch_weight[...]) + position[...].astype(F32)
    attend(
        tokens, normed, packed, mixed, gain_attn, qkv_weight, out_weight, lambda: weights.need(2), lambda: weights.need(3)
    )
    features = tokens[...].astype(BF)
    normed[...] = layer_norm(features.astype(F32), gain_head[...]).astype(BF)
    mixed[...] = features
    logits = dot(normed[...], head[...])
    high = logits.astype(BF)
    low = (logits - high.astype(F32)).astype(BF)
    lane = lax.broadcasted_iota(jnp.int32, high.shape, 1)
    both = jnp.where(lane < CLASSES, high, low)
    weights.need(4)
    lifted = dot(mixed[...], join_weight[...]).astype(BF)
    for w in range(windows):
        rows = slice(w * TT, (w + 1) * TT)
        cols = slice(w * TS, (w + 1) * TS)
        joined[:, cols, :D] = lifted[rows].reshape(TS, TS, D)
        joined[:, cols, D:] = both[rows].reshape(TS, TS, LANES)
    top[...] = joined[0]
    bottom[...] = joined[CR - 1]
    blank = jnp.zeros((16, JW), F32)
    first[...] = jnp.concatenate([joined[r, :16].astype(F32)[:1] for r in range(CR)] + [blank], axis=0).astype(BF)
    last[...] = jnp.concatenate([joined[r, CC - 16 :].astype(F32)[15:] for r in range(CR)] + [blank], axis=0).astype(BF)


def list_flagged(flags, chosen):
    def mark(t, count):
        @pl.when(flags[t] == 1)
        def _():
            chosen[count] = t

        return count + flags[t]

    count = lax.fori_loop(0, TILES, mark, jnp.int32(0))
    away = jnp.clip(count - KEEP, 0, len(SLOTS))
    return count - away, away


def pack_kernel(
    wide_end, narrow_end, place, flags, pixels, joined, top, bottom, first, last, up, down, left, right,
    pick, rim_pick, rims, *refs,
):
    sends = refs[: len(SEND)]
    chosen, stage, in_sem, out_sem, sides = refs[len(SEND) :]
    wide_pos = place[0]
    narrow_pos = place[1]
    keep, away = list_flagged(flags, chosen)

    def pixel_copy(s):
        return pltpu.make_async_copy(pixels.at[chosen[keep + s]], stage.at[s, pl.ds(0, TT)], in_sem.at[s])

    def whole_copy(s):
        way, at = SLOTS[s]
        return pltpu.make_async_copy(stage.at[s], sends[way].at[at], out_sem.at[s])

    def tail_copy(s):
        way, at = SLOTS[s]
        rows = pl.ds(TT + RIM - 16, 16)
        return pltpu.make_async_copy(stage.at[s, rows], sends[way].at[at, rows], out_sem.at[s])

    for s in range(len(SLOTS)):

        @pl.when(s < away)
        def _():
            pixel_copy(s).start()

    def pick_side(at_edge, own, got):
        return jnp.where(at_edge, own.astype(F32), got.astype(F32))

    over = pick_side(wide_pos == 0, top[...], up[...]).astype(BF)
    under = pick_side(wide_pos == wide_end, bottom[...], down[...]).astype(BF)
    sides[0] = pick_side(narrow_pos == 0, first[...], left[...]).astype(BF)
    sides[1] = pick_side(narrow_pos == narrow_end, last[...], right[...]).astype(BF)
    for a in range(TR):
        for i in range(CS + 2):
            row = a * CS + i
            if row == 0:
                cells = over
            elif row == CR + 1:
                cells = under
            else:
                cells = joined[(row - 1) * CC : row * CC, :]
            rims[a, i * CC : (i + 1) * CC, :] = cells
        edge = (CS + 2) * CC
        block = dot(pick[0, a], sides[0]) + dot(pick[1, a], sides[1])
        rims[a, edge : edge + 16, :] = block.astype(BF)
        rims[a, edge + 16 :, :] = jnp.zeros((RIM_K - edge - 16, JW), BF)
    for s in range(len(SLOTS)):

        @pl.when(s < away)
        def _():
            tile = chosen[keep + s]
            rim = dot(rim_pick[tile % TC], rims[tile // TC, :, :D])
            row = lax.broadcasted_iota(jnp.int32, rim.shape, 0)
            rim = jnp.where(row == RIM - 1, 1.0, rim).astype(BF)
            stage[s, TT : TT + RIM, :] = rim[:, :PD]
            for part in range(RIM // 16):
                cols = slice(part * GROUP, (part + 1) * GROUP)
                stage[s, TT + RIM :, cols] = rim[part * 16 : (part + 1) * 16, PD:]
            pixel_copy(s).wait()
            whole_copy(s).start()

        @pl.when(s >= away)
        def _():
            stage[s, TT + RIM - 16 : TT + RIM, :] = jnp.zeros((16, PD), BF)
            tail_copy(s).start()

    for s in range(len(SLOTS)):

        @pl.when(s < away)
        def _():
            whole_copy(s).wait()

        @pl.when(s >= away)
        def _():
            tail_copy(s).wait()


def run_tiles(count, fetch, wait, embed, finish, weights, gain_attn, gain_head, head, block):
    _, _, qkv_weight, out_weight = weights.refs

    def body(k, size, need):
        for t in range(size):
            wait(k + t)
        for t in range(size, size + 2):

            @pl.when(k + t < count)
            def _():
                fetch(k + t)

        tokens, normed, packed, mixed = (ref.at[pl.ds(0, size * TT)] for ref in block)
        need(0, 1)
        for t in range(size):
            embed(k + t, tokens.at[pl.ds(t * TT, TT)])
        attend(
            tokens, normed, packed, mixed, gain_attn, qkv_weight, out_weight, lambda: need(2), lambda: need(3)
        )
        normed[...] = layer_norm(tokens[...], gain_head[...]).astype(BF)
        answer = dot(normed[...], head[...])
        for t in range(size):
            finish(k + t, jnp.transpose(answer[t * TT : (t + 1) * TT])[:CLASSES].astype(BF))

    odd = count % 2

    @pl.when(odd == 1)
    def _():
        body(jnp.int32(0), 1, weights.need)

    @pl.when((odd == 0) & (count > 0))
    def _():
        body(jnp.int32(0), 2, weights.need)

    def pair(i, carry):
        body(2 - odd + 2 * i, 2, lambda *which: None)
        return carry

    lax.fori_loop(0, (count - 2 + odd) // 2, pair, jnp.int32(0))


def local_kernel(
    flags, pixels, rims, lift, gain_attn, gain_head, head_rows, patch_hbm, position_hbm, qkv_hbm, out_hbm,
    logits, chosen, buffer, sem, patch_weight, position, qkv_weight, out_weight, head, weight_sem, *block,
):
    weights = Weights(
        [patch_hbm, position_hbm, qkv_hbm, out_hbm], [patch_weight, position, qkv_weight, out_weight], weight_sem
    )
    weights.start(0, 1)
    keep, _ = list_flagged(flags, chosen)

    def copy(k):
        return pltpu.make_async_copy(pixels.at[chosen[k]], buffer.at[k % 4], sem.at[k % 4])

    @pl.when(keep > 0)
    def _():
        copy(0).start()

    @pl.when((keep > 0) & (keep % 2 == 0))
    def _():
        copy(1).start()

    weights.start(2, 3)
    spread_head(head_rows, head)
    coarse = []
    for a in range(TR):
        turned = jnp.transpose(rims[a, :, D:].astype(F32))
        coarse.append(turned[: 2 * CLASSES])
    coarse = jnp.concatenate(coarse, axis=0).astype(BF)
    for b in range(TC):
        fine = dot_nt(coarse, lift[b])
        for a in range(TR):
            at = a * 2 * CLASSES
            logits[a * TC + b] = (fine[at : at + CLASSES] + fine[at + CLASSES : at + 2 * CLASSES]).astype(BF)

    def embed(k, tokens):
        tile = chosen[k]
        cells = dot(buffer[k % 4], patch_weight[...])
        cells = cells + dot(lift[tile % TC], rims[tile // TC, :, :D])
        tokens[...] = cells + position[...].astype(F32)

    def finish(k, answer):
        logits[chosen[k]] = answer

    run_tiles(
        keep, lambda k: copy(k).start(), lambda k: copy(k).wait(), embed, finish, weights, gain_attn, gain_head, head, block
    )

    @pl.when(keep == 0)
    def _():
        weights.need(0, 1, 2, 3)


def remote_kernel(*refs):
    ways = len(SEND)
    got = refs[:ways]
    refs = refs[1:]
    rim_lift, gain_attn, gain_head, head_rows = refs[ways : ways + 4]
    sources = refs[ways + 4 : ways + 8]
    answers = refs[ways + 8 : 2 * ways + 8]
    filled, flag_rows, buffer, flag_sem, sem = refs[2 * ways + 8 : 2 * ways + 13]
    held = refs[2 * ways + 13 : 2 * ways + 17]
    head, weight_sem = refs[2 * ways + 17 : 2 * ways + 19]
    block = refs[2 * ways + 19 :]
    patch_weight, position = held[:2]
    weights = Weights(sources, held, weight_sem)

    def flag_copy(s):
        way, at = SLOTS[s]
        return pltpu.make_async_copy(got[way].at[at, pl.ds(TT + RIM - 16, 16)], flag_rows.at[s], flag_sem.at[s])

    for s in range(len(SLOTS)):
        flag_copy(s).start()
    count = jnp.int32(0)
    for s in range(len(SLOTS)):
        flag_copy(s).wait()
        here = (jnp.max(flag_rows[s, :, :LANES].astype(F32)[15:16]) > 0.5).astype(jnp.int32)

        @pl.when(here == 1)
        def _():
            filled[count] = s

        count = count + here

    def each_slot(k, then):
        for s in range(len(SLOTS)):

            @pl.when(filled[k] == s)
            def _():
                then(*SLOTS[s])

    def copy(k, way, at):
        return pltpu.make_async_copy(got[way].at[at], buffer.at[k % 4], sem.at[k % 4])

    def fetch(k):
        each_slot(k, lambda way, at: copy(k, way, at).start())

    @pl.when(count > 0)
    def _():
        fetch(0)

    @pl.when((count > 0) & (count % 2 == 0))
    def _():
        fetch(1)

    @pl.when(count > 0)
    def _():
        weights.start(0, 1, 2, 3)
        spread_head(head_rows, head)

    def embed(k, tokens):
        slot = buffer.at[k % 4]
        tail = slot[TT + RIM :, :]
        rest = jnp.concatenate([tail[:, part * GROUP : (part + 1) * GROUP] for part in range(RIM // 16)], axis=0)
        place = position[...].astype(F32)
        cells = dot(slot[:TT, :], patch_weight[...])
        tokens[:, :PD] = cells[:, :PD] + dot(rim_lift[...], slot[TT : TT + RIM, :]) + place[:, :PD]
        tokens[:, PD:] = cells[:, PD:] + dot(rim_lift[...], rest) + place[:, PD:]

    def finish(k, answer):
        def store(way, at):
            answers[way][at] = answer

        each_slot(k, store)

    run_tiles(count, fetch, lambda k: copy(k, 0, 0).wait(), embed, finish, weights, gain_attn, gain_head, head, block)


def merge_kernel(flags, base, *refs):
    returned = refs[: len(SEND)]
    logits, chosen = refs[len(SEND) :]
    keep, away = list_flagged(flags, chosen)
    logits[...] = base[...]
    for s in range(len(SLOTS)):

        @pl.when(s < away)
        def _():
            way, at = SLOTS[s]
            logits[chosen[keep + s]] = returned[way][at]


def vmem():
    return pl.BlockSpec(memory_space=pltpu.VMEM)


def smem():
    return pl.BlockSpec(memory_space=pltpu.SMEM)


def hbm():
    return pl.BlockSpec(memory_space=pl.ANY)


def block_scratch(rows):
    return [
        pltpu.VMEM((rows, D), F32),
        pltpu.VMEM((rows, D), BF),
        pltpu.VMEM((rows, 3 * D), BF),
        pltpu.VMEM((rows, D), BF),
    ]


def weight_scratch(*more):
    return [
        pltpu.VMEM((PD, D), BF),
        pltpu.VMEM((TT, D), BF),
        pltpu.VMEM((D, 3 * D), BF),
        pltpu.VMEM((D, D), BF),
        *more,
        pltpu.VMEM((D, LANES), BF),
        pltpu.SemaphoreType.DMA((4 + len(more),)),
    ]


def glance(coarse_pixels, small, large, join_weight):
    rows = CR * CC
    return pl.pallas_call(
        glance_kernel,
        out_shape=[jax.ShapeDtypeStruct((CR, CC, JW), BF)]
        + [jax.ShapeDtypeStruct((CC, JW), BF)] * 4,
        in_specs=[vmem()] * 4 + [hbm()] * 5,
        out_specs=[vmem()] * 5,
        scratch_shapes=weight_scratch(pltpu.VMEM((D, D), BF)) + block_scratch(rows),
        compiler_params=params(60),
        name="glance",
    )(coarse_pixels, *small, *large, join_weight)


def tile_cost(tiles):
    return pl.CostEstimate(flops=tiles * 3_500_000_000, bytes_accessed=12_000_000, transcendentals=0)


def params(limit):
    return pltpu.CompilerParams(vmem_limit_bytes=limit * MIB)


def chosen_scratch():
    return pltpu.SMEM((TILES,), jnp.int32)


def pack(place, flags, pixels, joined, *cells):
    return pl.pallas_call(
        functools.partial(pack_kernel, lax.axis_size("wide") - 1, lax.axis_size("narrow") - 1),
        out_shape=[jax.ShapeDtypeStruct((TR, RIM_K, JW), BF)]
        + [jax.ShapeDtypeStruct((n, SLOT_ROWS, PD), BF) for n in SEND],
        in_specs=[smem(), smem(), hbm()] + [vmem()] * (1 + len(cells)),
        out_specs=[vmem()] + [hbm()] * len(SEND),
        scratch_shapes=[
            chosen_scratch(),
            pltpu.VMEM((len(SLOTS), SLOT_ROWS, PD), BF),
            pltpu.SemaphoreType.DMA((len(SLOTS),)),
            pltpu.SemaphoreType.DMA((len(SLOTS),)),
            pltpu.VMEM((2, 32, JW), BF),
        ],
        compiler_params=params(60),
        name="pack",
    )(place, flags, pixels, joined, *cells)


def focus_local(flags, pixels, rims, lift, small, large):
    return pl.pallas_call(
        local_kernel,
        out_shape=jax.ShapeDtypeStruct((TILES, CLASSES, TT), BF),
        in_specs=[smem(), hbm()] + [vmem()] * 5 + [hbm()] * 4,
        out_specs=vmem(),
        scratch_shapes=[
            chosen_scratch(),
            pltpu.VMEM((4, TT, PD), BF),
            pltpu.SemaphoreType.DMA((4,)),
        ]
        + weight_scratch()
        + block_scratch(2 * TT),
        compiler_params=params(60),
        cost_estimate=tile_cost(9),
        name="focus_local",
    )(flags, pixels, rims, lift, *small, *large)


def focus_remote(got, base, rim_lift, small, large):
    return pl.pallas_call(
        remote_kernel,
        out_shape=[jax.ShapeDtypeStruct((n, CLASSES, TT), BF) for n in SEND],
        in_specs=[hbm()] * (len(SEND) + 1) + [vmem()] * 4 + [hbm()] * 4,
        out_specs=[vmem()] * len(SEND),
        scratch_shapes=[
            pltpu.SMEM((len(SLOTS),), jnp.int32),
            pltpu.VMEM((len(SLOTS), 16, PD), BF),
            pltpu.VMEM((4, SLOT_ROWS, PD), BF),
            pltpu.SemaphoreType.DMA((len(SLOTS),)),
            pltpu.SemaphoreType.DMA((4,)),
        ]
        + weight_scratch()
        + block_scratch(2 * TT),
        compiler_params=params(60),
        cost_estimate=tile_cost(4),
        name="focus_remote",
    )(*got, base, rim_lift, *small, *large)


def merge(flags, base, returned):
    return pl.pallas_call(
        merge_kernel,
        out_shape=jax.ShapeDtypeStruct((TILES, CLASSES, TT), BF),
        in_specs=[smem()] + [vmem()] * (1 + len(SEND)),
        out_specs=vmem(),
        scratch_shapes=[chosen_scratch()],
        compiler_params=params(6),
        name="merge",
    )(flags, base, *returned)


def routes():
    wide = lax.axis_size("wide")
    side = int(np.sqrt(wide))

    def along_x(step):
        return "wide", [(i, (i // side + step) % side * side + i % side) for i in range(wide)]

    def along_y(step):
        return "wide", [(i, i // side * side + (i % side + step) % side) for i in range(wide)]

    return [along_x(1), along_x(-1), along_y(1), along_y(-1)]


def shifted(x, axis, step):
    count = lax.axis_size(axis)
    pairs = [(i, i + step) for i in range(count) if 0 <= i + step < count]
    return lax.ppermute(x, axis, pairs)


def cornered(column, above, below):
    blank = jnp.zeros((32 - CR - 2, JW), BF)
    return jnp.concatenate([column[:CR], above, below, blank], axis=0)


def per_device(
    pixels,
    coarse_pixels,
    unsure,
    patch_weight,
    position,
    qkv_weight,
    out_weight,
    join_weight,
    gain_attn,
    gain_head,
    head_weight,
):
    tile_rows, tile_cols = unsure.shape
    flags = unsure.reshape(-1)
    gain_attn = gain_attn.reshape(1, D)
    gain_head = gain_head.reshape(1, D)
    small = (gain_attn, gain_head, head_weight.T)
    large = (patch_weight, position, qkv_weight, out_weight)
    lift = jnp.asarray(lift_tables(), BF)
    pick = jnp.asarray(side_tables(), BF)
    joined, top, bottom, first, last = glance(coarse_pixels, small, large, join_weight)
    up = shifted(bottom, "wide", 1)
    down = shifted(top, "wide", -1)
    wide_pos = lax.axis_index("wide")
    first_row = wide_pos == 0
    last_row = wide_pos == lax.axis_size("wide") - 1
    first = cornered(first, jnp.where(first_row, top[:1], up[:1]), jnp.where(last_row, bottom[:1], down[:1]))
    last = cornered(last, jnp.where(first_row, top[-1:], up[-1:]), jnp.where(last_row, bottom[-1:], down[-1:]))
    borders = [up, down, shifted(last, "narrow", 1), shifted(first, "narrow", -1)]
    place = jnp.stack([lax.axis_index("wide"), lax.axis_index("narrow")]).astype(jnp.int32)
    rim_pick, rim_lift = (jnp.asarray(t, BF) for t in rim_tables())
    flat_pixels = pixels.reshape(TILES, TT, PD)
    flat_joined = joined.reshape(CR * CC, JW)
    rims, *sends = pack(
        place, flags, flat_pixels, flat_joined, top, bottom, first, last, *borders, pick, rim_pick
    )
    ways = routes()
    got = [lax.ppermute(block, axis, pairs) for block, (axis, pairs) in zip(sends, ways)]
    base = focus_local(flags, flat_pixels, rims, lift, small, large)
    answers = focus_remote(got, base, rim_lift, small, large)
    returned = [
        lax.ppermute(block, axis, [(b, a) for a, b in pairs]) for block, (axis, pairs) in zip(answers, ways)
    ]
    logits = merge(flags, base, returned)
    return logits.reshape(tile_rows, tile_cols, CLASSES, TT)


def solution(mesh):
    return jax.shard_map(
        per_device,
        mesh=mesh,
        in_specs=(
            P("wide", "narrow", None, None),
            P("wide", "narrow", None),
            P("wide", "narrow"),
            P(),
            P(),
            P(),
            P(),
            P(),
            P(),
            P(),
            P(),
        ),
        out_specs=P("wide", "narrow", None, None),
        check_vma=False,
    )
```

```python
import functools

import jax
import jax.numpy as jnp
import numpy as np
from jax import lax
from jax.experimental import pallas as pl
from jax.experimental.pallas import tpu as pltpu
from jax.sharding import PartitionSpec as P

D = 1024
HEADS = 16
HD = 64
PD = 768
CLASSES = 16
TS = 16
TT = 256
CS = 4
EPS = 1e-06
LOG2E = 1.4426950408889634
GROUP = 256
GROUP_HEADS = GROUP // HD
LANES = 128
JW = D + LANES
RIM_K = 256
TR = 4
TC = 8
TILES = TR * TC
CR = TR * CS
CC = TC * CS
KEEP = 7
SEND = (4, 4, 4, 4)
SLOTS = tuple((way, at) for at in range(4) for way in (0, 2, 1, 3))
RIM = 48
SLOT_ROWS = TT + RIM + 16
BF = jnp.bfloat16
F32 = jnp.float32
NT = (((1,), (1,)), ((), ()))
MIB = 1024 * 1024


def interp_table():
    table = np.zeros((TS, CS + 2), np.float64)
    for p in range(TS):
        c = (2 * p - 3) / 8
        i = int(np.floor(c))
        table[p, i + 1] = 1 - (c - i)
        table[p, i + 2] = c - i
    return table


def rim_slots():
    slots = np.zeros((CS + 2, CC + 2), np.int64)
    for i in range(CS + 2):
        for c in range(1, CC + 1):
            slots[i, c] = i * CC + c - 1
        slots[i, 0] = (CS + 2) * CC + i
        slots[i, CC + 1] = (CS + 2) * CC + 8 + i
    return slots


def lift_tables():
    table = interp_table()
    slots = rim_slots()
    lift = np.zeros((TC, TT, RIM_K), np.float32)
    for b in range(TC):
        for i in range(CS + 2):
            for j in range(CS + 2):
                lift[b, :, slots[i, b * CS + j]] += np.outer(table[:, i], table[:, j]).reshape(-1)
    return lift


def side_tables():
    pick = np.zeros((2, TR, 16, 32), np.float32)
    for a in range(TR):
        for i in range(CS + 2):
            row = a * CS + i
            at = CR if row == 0 else CR + 1 if row == CR + 1 else row - 1
            pick[0, a, i, at] = 1
            pick[1, a, 8 + i, at] = 1
    return pick


def rim_tables():
    table = interp_table()
    slots = rim_slots()
    pick = np.zeros((TC, RIM, RIM_K), np.float32)
    lift = np.zeros((TT, RIM), np.float32)
    for i in range(CS + 2):
        for j in range(CS + 2):
            r = i * (CS + 2) + j
            lift[:, r] = np.outer(table[:, i], table[:, j]).reshape(-1)
            for b in range(TC):
                pick[b, r, slots[i, b * CS + j]] = 1
    return pick, lift


def dot(a, b):
    return jnp.dot(a, b, preferred_element_type=F32)


def dot_nt(a, b):
    return lax.dot_general(a, b, NT, preferred_element_type=F32)


def layer_norm(values, gain):
    center = values - jnp.mean(values, axis=-1, keepdims=True)
    spread = jnp.mean(center * center, axis=-1, keepdims=True)
    return center * lax.rsqrt(spread + EPS) * gain


def attend(tokens, normed, packed, mixed, gain_attn, qkv_weight, out_weight, need_qkv, need_out):
    count = tokens.shape[0] // TT
    normed[...] = layer_norm(tokens[...], gain_attn[...]).astype(BF)
    lane_head = lax.broadcasted_iota(jnp.int32, (TT, GROUP), 1) // HD
    need_qkv()
    for g in range(HEADS // GROUP_HEADS):
        for part in range(3):
            cols = slice(part * D + g * GROUP, part * D + (g + 1) * GROUP)
            packed[:, cols] = dot(normed[...], qkv_weight[:, cols]).astype(BF)
    for w in range(count):
        rows = slice(w * TT, (w + 1) * TT)
        for g in range(HEADS // GROUP_HEADS):
            queries = packed[rows, g * GROUP : (g + 1) * GROUP]
            keys = packed[rows, D + g * GROUP : D + (g + 1) * GROUP]
            values = packed[rows, 2 * D + g * GROUP : 2 * D + (g + 1) * GROUP]
            total = None
            norms = None
            for h in range(GROUP_HEADS):
                mine = lane_head == h
                scores = dot_nt(jnp.where(mine, queries, jnp.zeros_like(queries)), keys)
                top = jnp.max(scores, axis=-1, keepdims=True)
                weights = jnp.exp2((scores - top) * (HD ** (-0.5) * LOG2E))
                norm = 1.0 / jnp.sum(weights, axis=-1, keepdims=True)
                norms = norm if norms is None else jnp.where(lane_head >= h, norm, norms)
                term = dot(weights.astype(BF), jnp.where(mine, values, jnp.zeros_like(values)))
                total = term if total is None else total + term
            mixed[rows, g * GROUP : (g + 1) * GROUP] = (total * norms).astype(BF)
    need_out()
    for n in range(D // GROUP):
        cols = slice(n * GROUP, (n + 1) * GROUP)
        tokens[:, cols] = tokens[:, cols] + dot(mixed[...], out_weight[:, cols])


class Weights:
    def __init__(self, sources, scratch, sem):
        self.refs = scratch
        self.copies = [pltpu.make_async_copy(a, b, sem.at[i]) for i, (a, b) in enumerate(zip(sources, scratch))]

    def start(self, *which):
        for i in which:
            self.copies[i].start()

    def need(self, *which):
        for i in which:
            self.copies[i].wait()


def spread_head(head_rows, head):
    rows = head_rows[...].astype(F32)
    rows = jnp.concatenate([rows, rows, jnp.zeros((LANES - 2 * CLASSES, D), F32)], axis=0)
    head[...] = jnp.transpose(rows).astype(BF)


def glance_kernel(
    coarse, gain_attn, gain_head, head_rows, patch_hbm, position_hbm, qkv_hbm, out_hbm, join_hbm,
    joined, top, bottom, first, last,
    patch_weight, position, qkv_weight, out_weight, join_weight, head, sem, tokens, normed, packed, mixed,
):
    weights = Weights(
        [patch_hbm, position_hbm, qkv_hbm, out_hbm, join_hbm],
        [patch_weight, position, qkv_weight, out_weight, join_weight],
        sem,
    )
    weights.start(0, 1, 2, 3, 4)
    spread_head(head_rows, head)
    weights.need(0, 1)
    windows = CC // TS
    for w in range(windows):
        rows = slice(w * TT, (w + 1) * TT)
        cells = coarse[:, w * TS : (w + 1) * TS, :].reshape(TT, PD)
        tokens[rows, :] = dot(cells, patch_weight[...]) + position[...].astype(F32)
    attend(
        tokens, normed, packed, mixed, gain_attn, qkv_weight, out_weight, lambda: weights.need(2), lambda: weights.need(3)
    )
    features = tokens[...].astype(BF)
    normed[...] = layer_norm(features.astype(F32), gain_head[...]).astype(BF)
    mixed[...] = features
    logits = dot(normed[...], head[...])
    high = logits.astype(BF)
    low = (logits - high.astype(F32)).astype(BF)
    lane = lax.broadcasted_iota(jnp.int32, high.shape, 1)
    both = jnp.where(lane < CLASSES, high, low)
    weights.need(4)
    lifted = dot(mixed[...], join_weight[...]).astype(BF)
    for w in range(windows):
        rows = slice(w * TT, (w + 1) * TT)
        cols = slice(w * TS, (w + 1) * TS)
        joined[:, cols, :D] = lifted[rows].reshape(TS, TS, D)
        joined[:, cols, D:] = both[rows].reshape(TS, TS, LANES)
    top[...] = joined[0]
    bottom[...] = joined[CR - 1]
    blank = jnp.zeros((16, JW), F32)
    first[...] = jnp.concatenate([joined[r, :16].astype(F32)[:1] for r in range(CR)] + [blank], axis=0).astype(BF)
    last[...] = jnp.concatenate([joined[r, CC - 16 :].astype(F32)[15:] for r in range(CR)] + [blank], axis=0).astype(BF)


def list_flagged(flags, chosen):
    def mark(t, count):
        @pl.when(flags[t] == 1)
        def _():
            chosen[count] = t

        return count + flags[t]

    count = lax.fori_loop(0, TILES, mark, jnp.int32(0))
    away = jnp.clip(count - KEEP, 0, len(SLOTS))
    return count - away, away


def pack_kernel(
    wide_end, narrow_end, place, flags, pixels, joined, top, bottom, first, last, up, down, left, right,
    pick, rim_pick, rims, *refs,
):
    sends = refs[: len(SEND)]
    chosen, stage, in_sem, out_sem, sides = refs[len(SEND) :]
    wide_pos = place[0]
    narrow_pos = place[1]
    keep, away = list_flagged(flags, chosen)

    sent = [
        sum((jnp.int32(s) < away).astype(jnp.int32) for s in range(len(SLOTS)) if SLOTS[s][0] == way)
        for way in range(len(SEND))
    ]

    def pixel_copy(s):
        return pltpu.make_async_copy(pixels.at[chosen[keep + s]], stage.at[s, pl.ds(0, TT)], in_sem.at[s])

    def whole_copy(s):
        way, at = SLOTS[s]
        return pltpu.make_async_copy(stage.at[s], sends[way].at[at], out_sem.at[s])

    def tail_copy(s):
        way, at = SLOTS[s]
        rows = pl.ds(TT + RIM - 16, 16)
        return pltpu.make_async_copy(stage.at[s, rows], sends[way].at[at, rows], out_sem.at[s])

    for s in range(len(SLOTS)):

        @pl.when(s < away)
        def _():
            pixel_copy(s).start()

    def pick_side(at_edge, own, got):
        return jnp.where(at_edge, own.astype(F32), got.astype(F32))

    over = pick_side(wide_pos == 0, top[...], up[...]).astype(BF)
    under = pick_side(wide_pos == wide_end, bottom[...], down[...]).astype(BF)
    sides[0] = pick_side(narrow_pos == 0, first[...], left[...]).astype(BF)
    sides[1] = pick_side(narrow_pos == narrow_end, last[...], right[...]).astype(BF)
    for a in range(TR):
        for i in range(CS + 2):
            row = a * CS + i
            if row == 0:
                cells = over
            elif row == CR + 1:
                cells = under
            else:
                cells = joined[(row - 1) * CC : row * CC, :]
            rims[a, i * CC : (i + 1) * CC, :] = cells
        edge = (CS + 2) * CC
        block = dot(pick[0, a], sides[0]) + dot(pick[1, a], sides[1])
        rims[a, edge : edge + 16, :] = block.astype(BF)
        rims[a, edge + 16 :, :] = jnp.zeros((RIM_K - edge - 16, JW), BF)
    for s in range(len(SLOTS)):

        @pl.when(s < away)
        def _():
            tile = chosen[keep + s]
            rim = dot(rim_pick[tile % TC], rims[tile // TC, :, :D])
            row = lax.broadcasted_iota(jnp.int32, rim.shape, 0)
            rim = jnp.where(row == RIM - 1, sent[SLOTS[s][0]].astype(F32), rim).astype(BF)
            stage[s, TT : TT + RIM, :] = rim[:, :PD]
            for part in range(RIM // 16):
                cols = slice(part * GROUP, (part + 1) * GROUP)
                stage[s, TT + RIM :, cols] = rim[part * 16 : (part + 1) * 16, PD:]
            pixel_copy(s).wait()
            whole_copy(s).start()

        if SLOTS[s][1] == 0:

            @pl.when(s >= away)
            def _():
                stage[s, TT + RIM - 16 : TT + RIM, :] = jnp.zeros((16, PD), BF)
                tail_copy(s).start()

    for s in range(len(SLOTS)):

        @pl.when(s < away)
        def _():
            whole_copy(s).wait()

        if SLOTS[s][1] == 0:

            @pl.when(s >= away)
            def _():
                tail_copy(s).wait()


def run_tiles(count, fetch, wait, embed, finish, weights, gain_attn, gain_head, head, block):
    _, _, qkv_weight, out_weight = weights.refs
    tokens, normed, packed, mixed = block

    def body(k, need):
        wait(k)

        @pl.when(k + 1 < count)
        def _():
            fetch(k + 1)

        need(0, 1)
        embed(k, tokens)
        attend(
            tokens, normed, packed, mixed, gain_attn, qkv_weight, out_weight, lambda: need(2), lambda: need(3)
        )
        normed[...] = layer_norm(tokens[...], gain_head[...]).astype(BF)
        finish(k, jnp.transpose(dot(normed[...], head[...]))[:CLASSES].astype(BF))

    @pl.when(count > 0)
    def _():
        body(jnp.int32(0), weights.need)

    @pl.when(count == 0)
    def _():
        weights.need(0, 1, 2, 3)

    def later(k, carry):
        body(k, lambda *which: None)
        return carry

    lax.fori_loop(1, count, later, jnp.int32(0))


def local_kernel(
    flags, pixels, rims, lift, gain_attn, gain_head, head_rows, patch_hbm, position_hbm, qkv_hbm, out_hbm,
    logits, chosen, buffer, sem, patch_weight, position, qkv_weight, out_weight, head, weight_sem, *block,
):
    weights = Weights(
        [patch_hbm, position_hbm, qkv_hbm, out_hbm], [patch_weight, position, qkv_weight, out_weight], weight_sem
    )
    weights.start(0, 1)
    keep, _ = list_flagged(flags, chosen)

    def copy(k):
        return pltpu.make_async_copy(pixels.at[chosen[k]], buffer.at[k % 2], sem.at[k % 2])

    @pl.when(keep > 0)
    def _():
        copy(0).start()

    weights.start(2, 3)
    spread_head(head_rows, head)
    coarse = []
    for a in range(TR):
        turned = jnp.transpose(rims[a, :, D:].astype(F32))
        coarse.append(turned[: 2 * CLASSES])
    coarse = jnp.concatenate(coarse, axis=0).astype(BF)
    for b in range(TC):
        fine = dot_nt(coarse, lift[b])
        for a in range(TR):
            at = a * 2 * CLASSES
            logits[a * TC + b] = (fine[at : at + CLASSES] + fine[at + CLASSES : at + 2 * CLASSES]).astype(BF)

    def embed(k, tokens):
        tile = chosen[k]
        cells = dot(buffer[k % 2], patch_weight[...])
        cells = cells + dot(lift[tile % TC], rims[tile // TC, :, :D])
        tokens[...] = cells + position[...].astype(F32)

    def finish(k, answer):
        logits[chosen[k]] = answer

    run_tiles(
        keep, lambda k: copy(k).start(), lambda k: copy(k).wait(), embed, finish, weights, gain_attn, gain_head, head, block
    )


def remote_kernel(*refs):
    ways = len(SEND)
    got = refs[:ways]
    refs = refs[1:]
    rim_lift, gain_attn, gain_head, head_rows = refs[ways : ways + 4]
    sources = refs[ways + 4 : ways + 8]
    answers = refs[ways + 8 : 2 * ways + 8]
    filled, flag_rows, buffer, flag_sem, sem = refs[2 * ways + 8 : 2 * ways + 13]
    held = refs[2 * ways + 13 : 2 * ways + 17]
    head, weight_sem = refs[2 * ways + 17 : 2 * ways + 19]
    block = refs[2 * ways + 19 :]
    patch_weight, position = held[:2]
    weights = Weights(sources, held, weight_sem)

    marks = [
        pltpu.make_async_copy(got[way].at[0, pl.ds(TT + RIM - 16, 16)], flag_rows.at[way], flag_sem.at[way])
        for way in range(ways)
    ]
    for mark in marks:
        mark.start()
    weights.start(0, 1)
    for mark in marks:
        mark.wait()
    sent = [jnp.max(flag_rows[way, :, :LANES].astype(F32)[15:16]).astype(jnp.int32) for way in range(ways)]
    count = jnp.int32(0)
    for s, (way, at) in enumerate(SLOTS):
        filled[count] = s
        count = count + (at < sent[way]).astype(jnp.int32)

    def each_slot(k, then):
        for s in range(len(SLOTS)):

            @pl.when(filled[k] == s)
            def _():
                then(*SLOTS[s])

    def copy(k, way, at):
        return pltpu.make_async_copy(got[way].at[at], buffer.at[k % 2], sem.at[k % 2])

    def fetch(k):
        each_slot(k, lambda way, at: copy(k, way, at).start())

    @pl.when(count > 0)
    def _():
        fetch(0)

    weights.start(2, 3)
    spread_head(head_rows, head)

    def embed(k, tokens):
        slot = buffer.at[k % 2]
        tail = slot[TT + RIM :, :]
        rest = jnp.concatenate([tail[:, part * GROUP : (part + 1) * GROUP] for part in range(RIM // 16)], axis=0)
        place = position[...].astype(F32)
        cells = dot(slot[:TT, :], patch_weight[...])
        tokens[:, :PD] = cells[:, :PD] + dot(rim_lift[...], slot[TT : TT + RIM, :]) + place[:, :PD]
        tokens[:, PD:] = cells[:, PD:] + dot(rim_lift[...], rest) + place[:, PD:]

    def finish(k, answer):
        def store(way, at):
            answers[way][at] = answer

        each_slot(k, store)

    run_tiles(count, fetch, lambda k: copy(k, 0, 0).wait(), embed, finish, weights, gain_attn, gain_head, head, block)


def merge_kernel(flags, base, *refs):
    returned = refs[: len(SEND)]
    logits, chosen = refs[len(SEND) :]
    keep, away = list_flagged(flags, chosen)
    logits[...] = base[...]
    for s in range(len(SLOTS)):

        @pl.when(s < away)
        def _():
            way, at = SLOTS[s]
            logits[chosen[keep + s]] = returned[way][at]


def vmem():
    return pl.BlockSpec(memory_space=pltpu.VMEM)


def smem():
    return pl.BlockSpec(memory_space=pltpu.SMEM)


def hbm():
    return pl.BlockSpec(memory_space=pl.ANY)


def block_scratch(rows):
    return [
        pltpu.VMEM((rows, D), F32),
        pltpu.VMEM((rows, D), BF),
        pltpu.VMEM((rows, 3 * D), BF),
        pltpu.VMEM((rows, D), BF),
    ]


def weight_scratch(*more):
    return [
        pltpu.VMEM((PD, D), BF),
        pltpu.VMEM((TT, D), BF),
        pltpu.VMEM((D, 3 * D), BF),
        pltpu.VMEM((D, D), BF),
        *more,
        pltpu.VMEM((D, LANES), BF),
        pltpu.SemaphoreType.DMA((4 + len(more),)),
    ]


def glance(coarse_pixels, small, large, join_weight):
    rows = CR * CC
    return pl.pallas_call(
        glance_kernel,
        out_shape=[jax.ShapeDtypeStruct((CR, CC, JW), BF)]
        + [jax.ShapeDtypeStruct((CC, JW), BF)] * 4,
        in_specs=[vmem()] * 4 + [hbm()] * 5,
        out_specs=[vmem()] * 5,
        scratch_shapes=weight_scratch(pltpu.VMEM((D, D), BF)) + block_scratch(rows),
        compiler_params=params(60),
        name="glance",
    )(coarse_pixels, *small, *large, join_weight)


def tile_cost(tiles):
    return pl.CostEstimate(flops=tiles * 3_500_000_000, bytes_accessed=12_000_000, transcendentals=0)


def params(limit):
    return pltpu.CompilerParams(vmem_limit_bytes=limit * MIB)


def chosen_scratch():
    return pltpu.SMEM((TILES,), jnp.int32)


def pack(place, flags, pixels, joined, *cells):
    return pl.pallas_call(
        functools.partial(pack_kernel, lax.axis_size("wide") - 1, lax.axis_size("narrow") - 1),
        out_shape=[jax.ShapeDtypeStruct((TR, RIM_K, JW), BF)]
        + [jax.ShapeDtypeStruct((n, SLOT_ROWS, PD), BF) for n in SEND],
        in_specs=[smem(), smem(), hbm()] + [vmem()] * (1 + len(cells)),
        out_specs=[vmem()] + [hbm()] * len(SEND),
        scratch_shapes=[
            chosen_scratch(),
            pltpu.VMEM((len(SLOTS), SLOT_ROWS, PD), BF),
            pltpu.SemaphoreType.DMA((len(SLOTS),)),
            pltpu.SemaphoreType.DMA((len(SLOTS),)),
            pltpu.VMEM((2, 32, JW), BF),
        ],
        compiler_params=params(60),
        name="pack",
    )(place, flags, pixels, joined, *cells)


def focus_local(flags, pixels, rims, lift, small, large):
    return pl.pallas_call(
        local_kernel,
        out_shape=jax.ShapeDtypeStruct((TILES, CLASSES, TT), BF),
        in_specs=[smem(), hbm()] + [vmem()] * 5 + [hbm()] * 4,
        out_specs=vmem(),
        scratch_shapes=[
            chosen_scratch(),
            pltpu.VMEM((2, TT, PD), BF),
            pltpu.SemaphoreType.DMA((2,)),
        ]
        + weight_scratch()
        + block_scratch(TT),
        compiler_params=params(60),
        cost_estimate=tile_cost(9),
        name="focus_local",
    )(flags, pixels, rims, lift, *small, *large)


def focus_remote(got, base, rim_lift, small, large):
    return pl.pallas_call(
        remote_kernel,
        out_shape=[jax.ShapeDtypeStruct((n, CLASSES, TT), BF) for n in SEND],
        in_specs=[hbm()] * (len(SEND) + 1) + [vmem()] * 4 + [hbm()] * 4,
        out_specs=[vmem()] * len(SEND),
        scratch_shapes=[
            pltpu.SMEM((len(SLOTS) + 1,), jnp.int32),
            pltpu.VMEM((len(SEND), 16, PD), BF),
            pltpu.VMEM((2, SLOT_ROWS, PD), BF),
            pltpu.SemaphoreType.DMA((len(SEND),)),
            pltpu.SemaphoreType.DMA((2,)),
        ]
        + weight_scratch()
        + block_scratch(TT),
        compiler_params=params(60),
        cost_estimate=tile_cost(4),
        name="focus_remote",
    )(*got, base, rim_lift, *small, *large)


def merge(flags, base, returned):
    return pl.pallas_call(
        merge_kernel,
        out_shape=jax.ShapeDtypeStruct((TILES, CLASSES, TT), BF),
        in_specs=[smem()] + [vmem()] * (1 + len(SEND)),
        out_specs=vmem(),
        scratch_shapes=[chosen_scratch()],
        compiler_params=params(6),
        name="merge",
    )(flags, base, *returned)


def routes():
    wide = lax.axis_size("wide")
    side = int(np.sqrt(wide))

    def along_x(step):
        return "wide", [(i, (i // side + step) % side * side + i % side) for i in range(wide)]

    def along_y(step):
        return "wide", [(i, i // side * side + (i % side + step) % side) for i in range(wide)]

    return [along_x(1), along_x(-1), along_y(1), along_y(-1)]


def shifted(x, axis, step):
    count = lax.axis_size(axis)
    pairs = [(i, i + step) for i in range(count) if 0 <= i + step < count]
    return lax.ppermute(x, axis, pairs)


def cornered(column, above, below):
    blank = jnp.zeros((32 - CR - 2, JW), BF)
    return jnp.concatenate([column[:CR], above, below, blank], axis=0)


def per_device(
    pixels,
    coarse_pixels,
    unsure,
    patch_weight,
    position,
    qkv_weight,
    out_weight,
    join_weight,
    gain_attn,
    gain_head,
    head_weight,
):
    tile_rows, tile_cols = unsure.shape
    flags = unsure.reshape(-1)
    gain_attn = gain_attn.reshape(1, D)
    gain_head = gain_head.reshape(1, D)
    small = (gain_attn, gain_head, head_weight.T)
    large = (patch_weight, position, qkv_weight, out_weight)
    lift = jnp.asarray(lift_tables(), BF)
    pick = jnp.asarray(side_tables(), BF)
    joined, top, bottom, first, last = glance(coarse_pixels, small, large, join_weight)
    up = shifted(bottom, "wide", 1)
    down = shifted(top, "wide", -1)
    wide_pos = lax.axis_index("wide")
    first_row = wide_pos == 0
    last_row = wide_pos == lax.axis_size("wide") - 1
    first = cornered(first, jnp.where(first_row, top[:1], up[:1]), jnp.where(last_row, bottom[:1], down[:1]))
    last = cornered(last, jnp.where(first_row, top[-1:], up[-1:]), jnp.where(last_row, bottom[-1:], down[-1:]))
    borders = [up, down, shifted(last, "narrow", 1), shifted(first, "narrow", -1)]
    place = jnp.stack([lax.axis_index("wide"), lax.axis_index("narrow")]).astype(jnp.int32)
    rim_pick, rim_lift = (jnp.asarray(t, BF) for t in rim_tables())
    flat_pixels = pixels.reshape(TILES, TT, PD)
    flat_joined = joined.reshape(CR * CC, JW)
    rims, *sends = pack(
        place, flags, flat_pixels, flat_joined, top, bottom, first, last, *borders, pick, rim_pick
    )
    ways = routes()
    got = [lax.ppermute(block, axis, pairs) for block, (axis, pairs) in zip(sends, ways)]
    base = focus_local(flags, flat_pixels, rims, lift, small, large)
    answers = focus_remote(got, base, rim_lift, small, large)
    returned = [
        lax.ppermute(block, axis, [(b, a) for a, b in pairs]) for block, (axis, pairs) in zip(answers, ways)
    ]
    logits = merge(flags, base, returned)
    return logits.reshape(tile_rows, tile_cols, CLASSES, TT)


def solution(mesh):
    return jax.shard_map(
        per_device,
        mesh=mesh,
        in_specs=(
            P("wide", "narrow", None, None),
            P("wide", "narrow", None),
            P("wide", "narrow"),
            P(),
            P(),
            P(),
            P(),
            P(),
            P(),
            P(),
            P(),
        ),
        out_specs=P("wide", "narrow", None, None),
        check_vma=False,
    )
```

```python
import functools

import jax
import jax.numpy as jnp
import numpy as np
from jax import lax
from jax.experimental import pallas as pl
from jax.experimental.pallas import tpu as pltpu
from jax.sharding import PartitionSpec as P

D = 1024
HEADS = 16
HD = 64
PD = 768
CLASSES = 16
TS = 16
TT = 256
CS = 4
EPS = 1e-06
LOG2E = 1.4426950408889634
GROUP = 256
GROUP_HEADS = GROUP // HD
LANES = 128
JW = D + LANES
RIM_K = 256
TR = 4
TC = 8
TILES = TR * TC
CR = TR * CS
CC = TC * CS
KEEP = 7
SEND = (4, 4, 4, 4)
SLOTS = tuple((way, at) for at in range(4) for way in (0, 2, 1, 3))
RIM = 48
SLOT_ROWS = TT + RIM + 16
BF = jnp.bfloat16
F32 = jnp.float32
NT = (((1,), (1,)), ((), ()))
MIB = 1024 * 1024


def interp_table():
    table = np.zeros((TS, CS + 2), np.float64)
    for p in range(TS):
        c = (2 * p - 3) / 8
        i = int(np.floor(c))
        table[p, i + 1] = 1 - (c - i)
        table[p, i + 2] = c - i
    return table


def rim_slots():
    slots = np.zeros((CS + 2, CC + 2), np.int64)
    for i in range(CS + 2):
        for c in range(1, CC + 1):
            slots[i, c] = i * CC + c - 1
        slots[i, 0] = (CS + 2) * CC + i
        slots[i, CC + 1] = (CS + 2) * CC + 8 + i
    return slots


def lift_tables():
    table = interp_table()
    slots = rim_slots()
    lift = np.zeros((TC, TT, RIM_K), np.float32)
    for b in range(TC):
        for i in range(CS + 2):
            for j in range(CS + 2):
                lift[b, :, slots[i, b * CS + j]] += np.outer(table[:, i], table[:, j]).reshape(-1)
    return lift


def side_tables():
    pick = np.zeros((2, TR, 16, 32), np.float32)
    for a in range(TR):
        for i in range(CS + 2):
            row = a * CS + i
            at = CR if row == 0 else CR + 1 if row == CR + 1 else row - 1
            pick[0, a, i, at] = 1
            pick[1, a, 8 + i, at] = 1
    return pick


def rim_tables():
    table = interp_table()
    slots = rim_slots()
    pick = np.zeros((TC, RIM, RIM_K), np.float32)
    lift = np.zeros((TT, RIM), np.float32)
    for i in range(CS + 2):
        for j in range(CS + 2):
            r = i * (CS + 2) + j
            lift[:, r] = np.outer(table[:, i], table[:, j]).reshape(-1)
            for b in range(TC):
                pick[b, r, slots[i, b * CS + j]] = 1
    return pick, lift


def dot(a, b):
    return jnp.dot(a, b, preferred_element_type=F32)


def dot_nt(a, b):
    return lax.dot_general(a, b, NT, preferred_element_type=F32)


def layer_norm(values, gain):
    center = values - jnp.mean(values, axis=-1, keepdims=True)
    spread = jnp.mean(center * center, axis=-1, keepdims=True)
    return center * lax.rsqrt(spread + EPS) * gain


def attend(tokens, normed, packed, mixed, gain_attn, qkv_weight, out_weight, need_qkv, need_out):
    count = tokens.shape[0] // TT
    normed[...] = layer_norm(tokens[...], gain_attn[...]).astype(BF)
    lane_head = lax.broadcasted_iota(jnp.int32, (TT, GROUP), 1) // HD
    need_qkv()
    for g in range(HEADS // GROUP_HEADS):
        for part in range(3):
            cols = slice(part * D + g * GROUP, part * D + (g + 1) * GROUP)
            packed[:, cols] = dot(normed[...], qkv_weight[:, cols]).astype(BF)
    for w in range(count):
        rows = slice(w * TT, (w + 1) * TT)
        for g in range(HEADS // GROUP_HEADS):
            queries = packed[rows, g * GROUP : (g + 1) * GROUP]
            keys = packed[rows, D + g * GROUP : D + (g + 1) * GROUP]
            values = packed[rows, 2 * D + g * GROUP : 2 * D + (g + 1) * GROUP]
            total = None
            norms = None
            for h in range(GROUP_HEADS):
                mine = lane_head == h
                scores = dot_nt(jnp.where(mine, queries, jnp.zeros_like(queries)), keys)
                top = jnp.max(scores, axis=-1, keepdims=True)
                weights = jnp.exp2((scores - top) * (HD ** (-0.5) * LOG2E))
                norm = 1.0 / jnp.sum(weights, axis=-1, keepdims=True)
                norms = norm if norms is None else jnp.where(lane_head >= h, norm, norms)
                term = dot(weights.astype(BF), jnp.where(mine, values, jnp.zeros_like(values)))
                total = term if total is None else total + term
            mixed[rows, g * GROUP : (g + 1) * GROUP] = (total * norms).astype(BF)
    need_out()
    for n in range(D // GROUP):
        cols = slice(n * GROUP, (n + 1) * GROUP)
        tokens[:, cols] = tokens[:, cols] + dot(mixed[...], out_weight[:, cols])


class Weights:
    def __init__(self, sources, scratch, sem):
        self.refs = scratch
        self.copies = [pltpu.make_async_copy(a, b, sem.at[i]) for i, (a, b) in enumerate(zip(sources, scratch))]

    def start(self, *which):
        for i in which:
            self.copies[i].start()

    def need(self, *which):
        for i in which:
            self.copies[i].wait()


def spread_head(head_rows, head):
    rows = head_rows[...].astype(F32)
    rows = jnp.concatenate([rows, rows, jnp.zeros((LANES - 2 * CLASSES, D), F32)], axis=0)
    head[...] = jnp.transpose(rows).astype(BF)


def glance_kernel(
    coarse, gain_attn, gain_head, head_rows, patch_hbm, position_hbm, qkv_hbm, out_hbm, join_hbm,
    joined, top, bottom, first, last,
    patch_weight, position, qkv_weight, out_weight, join_weight, head, sem, tokens, normed, packed, mixed,
):
    weights = Weights(
        [patch_hbm, position_hbm, qkv_hbm, out_hbm, join_hbm],
        [patch_weight, position, qkv_weight, out_weight, join_weight],
        sem,
    )
    weights.start(0, 1, 2, 3, 4)
    spread_head(head_rows, head)
    weights.need(0, 1)
    windows = CC // TS
    for w in range(windows):
        rows = slice(w * TT, (w + 1) * TT)
        cells = coarse[:, w * TS : (w + 1) * TS, :].reshape(TT, PD)
        tokens[rows, :] = dot(cells, patch_weight[...]) + position[...].astype(F32)
    attend(
        tokens, normed, packed, mixed, gain_attn, qkv_weight, out_weight, lambda: weights.need(2), lambda: weights.need(3)
    )
    features = tokens[...].astype(BF)
    normed[...] = layer_norm(features.astype(F32), gain_head[...]).astype(BF)
    mixed[...] = features
    logits = dot(normed[...], head[...])
    high = logits.astype(BF)
    low = (logits - high.astype(F32)).astype(BF)
    lane = lax.broadcasted_iota(jnp.int32, high.shape, 1)
    both = jnp.where(lane < CLASSES, high, low)
    weights.need(4)
    lifted = dot(mixed[...], join_weight[...]).astype(BF)
    for w in range(windows):
        rows = slice(w * TT, (w + 1) * TT)
        cols = slice(w * TS, (w + 1) * TS)
        joined[:, cols, :D] = lifted[rows].reshape(TS, TS, D)
        joined[:, cols, D:] = both[rows].reshape(TS, TS, LANES)
    top[...] = joined[0]
    bottom[...] = joined[CR - 1]
    blank = jnp.zeros((16, JW), F32)
    first[...] = jnp.concatenate([joined[r, :16].astype(F32)[:1] for r in range(CR)] + [blank], axis=0).astype(BF)
    last[...] = jnp.concatenate([joined[r, CC - 16 :].astype(F32)[15:] for r in range(CR)] + [blank], axis=0).astype(BF)


def list_flagged(flags, chosen):
    def mark(t, count):
        @pl.when(flags[t] == 1)
        def _():
            chosen[count] = t

        return count + flags[t]

    count = lax.fori_loop(0, TILES, mark, jnp.int32(0))
    away = jnp.clip(count - KEEP, 0, len(SLOTS))
    return count - away, away


def stage_kernel(flags, pixels, _, *refs):
    sends = refs[: len(SEND)]
    chosen, stage, in_sem, out_sem = refs[len(SEND) :]
    keep, away = list_flagged(flags, chosen)

    def copy_in(s):
        return pltpu.make_async_copy(pixels.at[chosen[keep + s]], stage.at[s], in_sem.at[s])

    def copy_out(s):
        way, at = SLOTS[s]
        return pltpu.make_async_copy(stage.at[s], sends[way].at[at, pl.ds(0, TT)], out_sem.at[s])

    def each(then):
        for s in range(len(SLOTS)):

            @pl.when(s < away)
            def _():
                then(s)

    def pass_on(s):
        copy_in(s).wait()
        copy_out(s).start()

    @pl.when(away > 0)
    def _():
        each(lambda s: copy_in(s).start())
        each(pass_on)
        each(lambda s: copy_out(s).wait())


def pack_kernel(
    wide_end, narrow_end, place, flags, joined, top, bottom, first, last, up, down, left, right,
    pick, rim_pick, *refs,
):
    ways = len(SEND)
    rims = refs[ways]
    sends = refs[ways + 1 : 2 * ways + 1]
    chosen, stage, out_sem, sides = refs[2 * ways + 1 :]
    wide_pos = place[0]
    narrow_pos = place[1]
    keep, away = list_flagged(flags, chosen)
    sent = [
        sum((jnp.int32(s) < away).astype(jnp.int32) for s in range(len(SLOTS)) if SLOTS[s][0] == way)
        for way in range(ways)
    ]

    def rim_copy(s):
        way, at = SLOTS[s]
        return pltpu.make_async_copy(stage.at[s], sends[way].at[at, pl.ds(TT, RIM + 16)], out_sem.at[s])

    def mark_copy(s):
        way, at = SLOTS[s]
        rows = pl.ds(TT + RIM - 16, 16)
        return pltpu.make_async_copy(stage.at[s, pl.ds(RIM - 16, 16)], sends[way].at[at, rows], out_sem.at[s])

    def pick_side(at_edge, own, got):
        return jnp.where(at_edge, own.astype(F32), got.astype(F32))

    over = pick_side(wide_pos == 0, top[...], up[...]).astype(BF)
    under = pick_side(wide_pos == wide_end, bottom[...], down[...]).astype(BF)
    sides[0] = pick_side(narrow_pos == 0, first[...], left[...]).astype(BF)
    sides[1] = pick_side(narrow_pos == narrow_end, last[...], right[...]).astype(BF)
    for a in range(TR):
        for i in range(CS + 2):
            row = a * CS + i
            if row == 0:
                cells = over
            elif row == CR + 1:
                cells = under
            else:
                cells = joined[(row - 1) * CC : row * CC, :]
            rims[a, i * CC : (i + 1) * CC, :] = cells
        edge = (CS + 2) * CC
        block = dot(pick[0, a], sides[0]) + dot(pick[1, a], sides[1])
        rims[a, edge : edge + 16, :] = block.astype(BF)
        rims[a, edge + 16 :, :] = jnp.zeros((RIM_K - edge - 16, JW), BF)
    for s in range(len(SLOTS)):

        @pl.when(s < away)
        def _():
            tile = chosen[keep + s]
            rim = dot(rim_pick[tile % TC], rims[tile // TC, :, :D])
            row = lax.broadcasted_iota(jnp.int32, rim.shape, 0)
            rim = jnp.where(row == RIM - 1, sent[SLOTS[s][0]].astype(F32), rim).astype(BF)
            stage[s, :RIM, :] = rim[:, :PD]
            for part in range(RIM // 16):
                cols = slice(part * GROUP, (part + 1) * GROUP)
                stage[s, RIM:, cols] = rim[part * 16 : (part + 1) * 16, PD:]
            rim_copy(s).start()

        if SLOTS[s][1] == 0:

            @pl.when(s >= away)
            def _():
                stage[s, RIM - 16 : RIM, :] = jnp.zeros((16, PD), BF)
                mark_copy(s).start()

    for s in range(len(SLOTS)):

        @pl.when(s < away)
        def _():
            rim_copy(s).wait()

        if SLOTS[s][1] == 0:

            @pl.when(s >= away)
            def _():
                mark_copy(s).wait()


def run_tiles(count, fetch, wait, embed, finish, weights, gain_attn, gain_head, head, block):
    _, _, qkv_weight, out_weight = weights.refs
    tokens, normed, packed, mixed = block

    def body(k, need):
        wait(k)

        @pl.when(k + 1 < count)
        def _():
            fetch(k + 1)

        need(0, 1)
        embed(k, tokens)
        attend(
            tokens, normed, packed, mixed, gain_attn, qkv_weight, out_weight, lambda: need(2), lambda: need(3)
        )
        normed[...] = layer_norm(tokens[...], gain_head[...]).astype(BF)
        finish(k, jnp.transpose(dot(normed[...], head[...]))[:CLASSES].astype(BF))

    @pl.when(count > 0)
    def _():
        body(jnp.int32(0), weights.need)

    @pl.when(count == 0)
    def _():
        weights.need(0, 1, 2, 3)

    def later(k, carry):
        body(k, lambda *which: None)
        return carry

    lax.fori_loop(1, count, later, jnp.int32(0))


def local_kernel(
    flags, pixels, rims, lift, gain_attn, gain_head, head_rows, patch_hbm, position_hbm, qkv_hbm, out_hbm,
    logits, chosen, buffer, sem, patch_weight, position, qkv_weight, out_weight, head, weight_sem, *block,
):
    weights = Weights(
        [patch_hbm, position_hbm, qkv_hbm, out_hbm], [patch_weight, position, qkv_weight, out_weight], weight_sem
    )
    weights.start(0, 1)
    keep, _ = list_flagged(flags, chosen)

    def copy(k):
        return pltpu.make_async_copy(pixels.at[chosen[k]], buffer.at[k % 2], sem.at[k % 2])

    @pl.when(keep > 0)
    def _():
        copy(0).start()

    weights.start(2, 3)
    spread_head(head_rows, head)
    coarse = []
    for a in range(TR):
        turned = jnp.transpose(rims[a, :, D:].astype(F32))
        coarse.append(turned[: 2 * CLASSES])
    coarse = jnp.concatenate(coarse, axis=0).astype(BF)
    for b in range(TC):
        fine = dot_nt(coarse, lift[b])
        for a in range(TR):
            at = a * 2 * CLASSES
            logits[a * TC + b] = (fine[at : at + CLASSES] + fine[at + CLASSES : at + 2 * CLASSES]).astype(BF)

    def embed(k, tokens):
        tile = chosen[k]
        cells = dot(buffer[k % 2], patch_weight[...])
        cells = cells + dot(lift[tile % TC], rims[tile // TC, :, :D])
        tokens[...] = cells + position[...].astype(F32)

    def finish(k, answer):
        logits[chosen[k]] = answer

    run_tiles(
        keep, lambda k: copy(k).start(), lambda k: copy(k).wait(), embed, finish, weights, gain_attn, gain_head, head, block
    )


def remote_kernel(*refs):
    ways = len(SEND)
    got = refs[:ways]
    refs = refs[1:]
    rim_lift, gain_attn, gain_head, head_rows = refs[ways : ways + 4]
    sources = refs[ways + 4 : ways + 8]
    answers = refs[ways + 8 : 2 * ways + 8]
    filled, flag_rows, buffer, flag_sem, sem = refs[2 * ways + 8 : 2 * ways + 13]
    held = refs[2 * ways + 13 : 2 * ways + 17]
    head, weight_sem = refs[2 * ways + 17 : 2 * ways + 19]
    block = refs[2 * ways + 19 :]
    patch_weight, position = held[:2]
    weights = Weights(sources, held, weight_sem)

    marks = [
        pltpu.make_async_copy(got[way].at[0, pl.ds(TT + RIM - 16, 16)], flag_rows.at[way], flag_sem.at[way])
        for way in range(ways)
    ]
    for mark in marks:
        mark.start()
    weights.start(0, 1)
    for mark in marks:
        mark.wait()
    sent = [jnp.max(flag_rows[way, :, :LANES].astype(F32)[15:16]).astype(jnp.int32) for way in range(ways)]
    count = jnp.int32(0)
    for s, (way, at) in enumerate(SLOTS):
        filled[count] = s
        count = count + (at < sent[way]).astype(jnp.int32)

    def each_slot(k, then):
        for s in range(len(SLOTS)):

            @pl.when(filled[k] == s)
            def _():
                then(*SLOTS[s])

    def copy(k, way, at):
        return pltpu.make_async_copy(got[way].at[at], buffer.at[k % 2], sem.at[k % 2])

    def fetch(k):
        each_slot(k, lambda way, at: copy(k, way, at).start())

    @pl.when(count > 0)
    def _():
        fetch(0)

    weights.start(2, 3)
    spread_head(head_rows, head)

    def embed(k, tokens):
        slot = buffer.at[k % 2]
        tail = slot[TT + RIM :, :]
        rest = jnp.concatenate([tail[:, part * GROUP : (part + 1) * GROUP] for part in range(RIM // 16)], axis=0)
        place = position[...].astype(F32)
        cells = dot(slot[:TT, :], patch_weight[...])
        tokens[:, :PD] = cells[:, :PD] + dot(rim_lift[...], slot[TT : TT + RIM, :]) + place[:, :PD]
        tokens[:, PD:] = cells[:, PD:] + dot(rim_lift[...], rest) + place[:, PD:]

    def finish(k, answer):
        def store(way, at):
            answers[way][at] = answer

        each_slot(k, store)

    run_tiles(count, fetch, lambda k: copy(k, 0, 0).wait(), embed, finish, weights, gain_attn, gain_head, head, block)


def merge_kernel(flags, base, *refs):
    returned = refs[: len(SEND)]
    logits, chosen = refs[len(SEND) :]
    keep, away = list_flagged(flags, chosen)
    logits[...] = base[...]
    for s in range(len(SLOTS)):

        @pl.when(s < away)
        def _():
            way, at = SLOTS[s]
            logits[chosen[keep + s]] = returned[way][at]


def vmem():
    return pl.BlockSpec(memory_space=pltpu.VMEM)


def smem():
    return pl.BlockSpec(memory_space=pltpu.SMEM)


def hbm():
    return pl.BlockSpec(memory_space=pl.ANY)


def block_scratch(rows):
    return [
        pltpu.VMEM((rows, D), F32),
        pltpu.VMEM((rows, D), BF),
        pltpu.VMEM((rows, 3 * D), BF),
        pltpu.VMEM((rows, D), BF),
    ]


def weight_scratch(*more):
    return [
        pltpu.VMEM((PD, D), BF),
        pltpu.VMEM((TT, D), BF),
        pltpu.VMEM((D, 3 * D), BF),
        pltpu.VMEM((D, D), BF),
        *more,
        pltpu.VMEM((D, LANES), BF),
        pltpu.SemaphoreType.DMA((4 + len(more),)),
    ]


def glance(coarse_pixels, small, large, join_weight):
    rows = CR * CC
    return pl.pallas_call(
        glance_kernel,
        out_shape=[jax.ShapeDtypeStruct((CR, CC, JW), BF)]
        + [jax.ShapeDtypeStruct((CC, JW), BF)] * 4,
        in_specs=[vmem()] * 4 + [hbm()] * 5,
        out_specs=[vmem()] * 5,
        scratch_shapes=weight_scratch(pltpu.VMEM((D, D), BF)) + block_scratch(rows),
        compiler_params=params(60),
        name="glance",
    )(coarse_pixels, *small, *large, join_weight)


def tile_cost(tiles):
    return pl.CostEstimate(flops=tiles * 3_500_000_000, bytes_accessed=12_000_000, transcendentals=0)


def params(limit):
    return pltpu.CompilerParams(vmem_limit_bytes=limit * MIB)


def chosen_scratch():
    return pltpu.SMEM((TILES,), jnp.int32)


def stage_pixels(flags, pixels, after):
    return pl.pallas_call(
        stage_kernel,
        out_shape=[jax.ShapeDtypeStruct((n, SLOT_ROWS, PD), BF) for n in SEND],
        in_specs=[smem(), hbm(), hbm()],
        out_specs=[hbm()] * len(SEND),
        scratch_shapes=[
            chosen_scratch(),
            pltpu.VMEM((len(SLOTS), TT, PD), BF),
            pltpu.SemaphoreType.DMA((len(SLOTS),)),
            pltpu.SemaphoreType.DMA((len(SLOTS),)),
        ],
        compiler_params=params(60),
        cost_estimate=pl.CostEstimate(flops=0, bytes_accessed=10_000_000, transcendentals=0),
        name="stage",
    )(flags, pixels, after)


def pack(place, flags, joined, cells, sends):
    ways = len(SEND)
    return pl.pallas_call(
        functools.partial(pack_kernel, lax.axis_size("wide") - 1, lax.axis_size("narrow") - 1),
        out_shape=[jax.ShapeDtypeStruct((TR, RIM_K, JW), BF)]
        + [jax.ShapeDtypeStruct((n, SLOT_ROWS, PD), BF) for n in SEND],
        in_specs=[smem(), smem()] + [vmem()] * (1 + len(cells)) + [hbm()] * ways,
        out_specs=[vmem()] + [hbm()] * ways,
        input_output_aliases={3 + len(cells) + way: 1 + way for way in range(ways)},
        scratch_shapes=[
            chosen_scratch(),
            pltpu.VMEM((len(SLOTS), RIM + 16, PD), BF),
            pltpu.SemaphoreType.DMA((len(SLOTS),)),
            pltpu.VMEM((2, 32, JW), BF),
        ],
        compiler_params=params(60),
        name="pack",
    )(place, flags, joined, *cells, *sends)


def focus_local(flags, pixels, rims, lift, small, large):
    return pl.pallas_call(
        local_kernel,
        out_shape=jax.ShapeDtypeStruct((TILES, CLASSES, TT), BF),
        in_specs=[smem(), hbm()] + [vmem()] * 5 + [hbm()] * 4,
        out_specs=vmem(),
        scratch_shapes=[
            chosen_scratch(),
            pltpu.VMEM((2, TT, PD), BF),
            pltpu.SemaphoreType.DMA((2,)),
        ]
        + weight_scratch()
        + block_scratch(TT),
        compiler_params=params(60),
        cost_estimate=tile_cost(9),
        name="focus_local",
    )(flags, pixels, rims, lift, *small, *large)


def focus_remote(got, base, rim_lift, small, large):
    return pl.pallas_call(
        remote_kernel,
        out_shape=[jax.ShapeDtypeStruct((n, CLASSES, TT), BF) for n in SEND],
        in_specs=[hbm()] * (len(SEND) + 1) + [vmem()] * 4 + [hbm()] * 4,
        out_specs=[vmem()] * len(SEND),
        scratch_shapes=[
            pltpu.SMEM((len(SLOTS) + 1,), jnp.int32),
            pltpu.VMEM((len(SEND), 16, PD), BF),
            pltpu.VMEM((2, SLOT_ROWS, PD), BF),
            pltpu.SemaphoreType.DMA((len(SEND),)),
            pltpu.SemaphoreType.DMA((2,)),
        ]
        + weight_scratch()
        + block_scratch(TT),
        compiler_params=params(60),
        cost_estimate=tile_cost(4),
        name="focus_remote",
    )(*got, base, rim_lift, *small, *large)


def merge(flags, base, returned):
    return pl.pallas_call(
        merge_kernel,
        out_shape=jax.ShapeDtypeStruct((TILES, CLASSES, TT), BF),
        in_specs=[smem()] + [vmem()] * (1 + len(SEND)),
        out_specs=vmem(),
        scratch_shapes=[chosen_scratch()],
        compiler_params=params(6),
        name="merge",
    )(flags, base, *returned)


def routes():
    wide = lax.axis_size("wide")
    side = int(np.sqrt(wide))

    def along_x(step):
        return "wide", [(i, (i // side + step) % side * side + i % side) for i in range(wide)]

    def along_y(step):
        return "wide", [(i, i // side * side + (i % side + step) % side) for i in range(wide)]

    return [along_x(1), along_x(-1), along_y(1), along_y(-1)]


def shifted(x, axis, step):
    count = lax.axis_size(axis)
    pairs = [(i, i + step) for i in range(count) if 0 <= i + step < count]
    return lax.ppermute(x, axis, pairs)


def cornered(column, above, below):
    blank = jnp.zeros((32 - CR - 2, JW), BF)
    return jnp.concatenate([column[:CR], above, below, blank], axis=0)


def per_device(
    pixels,
    coarse_pixels,
    unsure,
    patch_weight,
    position,
    qkv_weight,
    out_weight,
    join_weight,
    gain_attn,
    gain_head,
    head_weight,
):
    tile_rows, tile_cols = unsure.shape
    flags = unsure.reshape(-1)
    gain_attn = gain_attn.reshape(1, D)
    gain_head = gain_head.reshape(1, D)
    small = (gain_attn, gain_head, head_weight.T)
    large = (patch_weight, position, qkv_weight, out_weight)
    lift = jnp.asarray(lift_tables(), BF)
    pick = jnp.asarray(side_tables(), BF)
    joined, top, bottom, first, last = glance(coarse_pixels, small, large, join_weight)
    up = shifted(bottom, "wide", 1)
    down = shifted(top, "wide", -1)
    wide_pos = lax.axis_index("wide")
    first_row = wide_pos == 0
    last_row = wide_pos == lax.axis_size("wide") - 1
    first = cornered(first, jnp.where(first_row, top[:1], up[:1]), jnp.where(last_row, bottom[:1], down[:1]))
    last = cornered(last, jnp.where(first_row, top[-1:], up[-1:]), jnp.where(last_row, bottom[-1:], down[-1:]))
    borders = [up, down, shifted(last, "narrow", 1), shifted(first, "narrow", -1)]
    place = jnp.stack([lax.axis_index("wide"), lax.axis_index("narrow")]).astype(jnp.int32)
    rim_pick, rim_lift = (jnp.asarray(t, BF) for t in rim_tables())
    flat_pixels = pixels.reshape(TILES, TT, PD)
    flat_joined = joined.reshape(CR * CC, JW)
    staged = stage_pixels(flags, flat_pixels, joined)
    cells = (top, bottom, first, last, *borders, pick, rim_pick)
    rims, *sends = pack(place, flags, flat_joined, cells, staged)
    ways = routes()
    got = [lax.ppermute(block, axis, pairs) for block, (axis, pairs) in zip(sends, ways)]
    base = focus_local(flags, flat_pixels, rims, lift, small, large)
    answers = focus_remote(got, base, rim_lift, small, large)
    returned = [
        lax.ppermute(block, axis, [(b, a) for a, b in pairs]) for block, (axis, pairs) in zip(answers, ways)
    ]
    logits = merge(flags, base, returned)
    return logits.reshape(tile_rows, tile_cols, CLASSES, TT)


def solution(mesh):
    return jax.shard_map(
        per_device,
        mesh=mesh,
        in_specs=(
            P("wide", "narrow", None, None),
            P("wide", "narrow", None),
            P("wide", "narrow"),
            P(),
            P(),
            P(),
            P(),
            P(),
            P(),
            P(),
            P(),
        ),
        out_specs=P("wide", "narrow", None, None),
        check_vma=False,
    )
```

```python
import functools

import jax
import jax.numpy as jnp
import numpy as np
from jax import lax
from jax.experimental import pallas as pl
from jax.experimental.pallas import tpu as pltpu
from jax.sharding import PartitionSpec as P

D = 1024
HEADS = 16
HD = 64
PD = 768
CLASSES = 16
TS = 16
TT = 256
CS = 4
EPS = 1e-06
LOG2E = 1.4426950408889634
GROUP = 256
GROUP_HEADS = GROUP // HD
LANES = 128
JW = D + LANES
RIM_K = 256
TR = 4
TC = 8
TILES = TR * TC
CR = TR * CS
CC = TC * CS
KEEP = 7
SEND = (4, 4, 4, 4)
SLOTS = tuple((way, at) for at in range(4) for way in (0, 2, 1, 3))
RIM = 48
SLOT_ROWS = TT + RIM + 16
BF = jnp.bfloat16
F32 = jnp.float32
NT = (((1,), (1,)), ((), ()))
MIB = 1024 * 1024


def interp_table():
    table = np.zeros((TS, CS + 2), np.float64)
    for p in range(TS):
        c = (2 * p - 3) / 8
        i = int(np.floor(c))
        table[p, i + 1] = 1 - (c - i)
        table[p, i + 2] = c - i
    return table


def rim_slots():
    slots = np.zeros((CS + 2, CC + 2), np.int64)
    for i in range(CS + 2):
        for c in range(1, CC + 1):
            slots[i, c] = i * CC + c - 1
        slots[i, 0] = (CS + 2) * CC + i
        slots[i, CC + 1] = (CS + 2) * CC + 8 + i
    return slots


def lift_tables():
    table = interp_table()
    slots = rim_slots()
    lift = np.zeros((TC, TT, RIM_K), np.float32)
    for b in range(TC):
        for i in range(CS + 2):
            for j in range(CS + 2):
                lift[b, :, slots[i, b * CS + j]] += np.outer(table[:, i], table[:, j]).reshape(-1)
    return lift


def side_tables():
    pick = np.zeros((2, TR, 16, 32), np.float32)
    for a in range(TR):
        for i in range(CS + 2):
            row = a * CS + i
            at = CR if row == 0 else CR + 1 if row == CR + 1 else row - 1
            pick[0, a, i, at] = 1
            pick[1, a, 8 + i, at] = 1
    return pick


def rim_tables():
    table = interp_table()
    slots = rim_slots()
    pick = np.zeros((TC, RIM, RIM_K), np.float32)
    lift = np.zeros((TT, RIM), np.float32)
    for i in range(CS + 2):
        for j in range(CS + 2):
            r = i * (CS + 2) + j
            lift[:, r] = np.outer(table[:, i], table[:, j]).reshape(-1)
            for b in range(TC):
                pick[b, r, slots[i, b * CS + j]] = 1
    return pick, lift


def dot(a, b):
    return jnp.dot(a, b, preferred_element_type=F32)


def dot_nt(a, b):
    return lax.dot_general(a, b, NT, preferred_element_type=F32)


def layer_norm(values, gain):
    center = values - jnp.mean(values, axis=-1, keepdims=True)
    spread = jnp.mean(center * center, axis=-1, keepdims=True)
    return center * lax.rsqrt(spread + EPS) * gain


def attend(tokens, normed, packed, mixed, gain_attn, qkv_weight, out_weight, need_qkv, need_out):
    count = tokens.shape[0] // TT
    normed[...] = layer_norm(tokens[...], gain_attn[...]).astype(BF)
    lane_head = lax.broadcasted_iota(jnp.int32, (TT, GROUP), 1) // HD
    need_qkv()
    for g in range(HEADS // GROUP_HEADS):
        for part in range(3):
            cols = slice(part * D + g * GROUP, part * D + (g + 1) * GROUP)
            packed[:, cols] = dot(normed[...], qkv_weight[:, cols]).astype(BF)
    for w in range(count):
        rows = slice(w * TT, (w + 1) * TT)
        for g in range(HEADS // GROUP_HEADS):
            queries = packed[rows, g * GROUP : (g + 1) * GROUP]
            keys = packed[rows, D + g * GROUP : D + (g + 1) * GROUP]
            values = packed[rows, 2 * D + g * GROUP : 2 * D + (g + 1) * GROUP]
            total = None
            norms = None
            for h in range(GROUP_HEADS):
                mine = lane_head == h
                scores = dot_nt(jnp.where(mine, queries, jnp.zeros_like(queries)), keys)
                top = jnp.max(scores, axis=-1, keepdims=True)
                weights = jnp.exp2((scores - top) * (HD ** (-0.5) * LOG2E))
                norm = 1.0 / jnp.sum(weights, axis=-1, keepdims=True)
                norms = norm if norms is None else jnp.where(lane_head >= h, norm, norms)
                term = dot(weights.astype(BF), jnp.where(mine, values, jnp.zeros_like(values)))
                total = term if total is None else total + term
            mixed[rows, g * GROUP : (g + 1) * GROUP] = (total * norms).astype(BF)
    need_out()
    for n in range(D // GROUP):
        cols = slice(n * GROUP, (n + 1) * GROUP)
        tokens[:, cols] = tokens[:, cols] + dot(mixed[...], out_weight[:, cols])


class Weights:
    def __init__(self, sources, scratch, sem):
        self.refs = scratch
        self.copies = [pltpu.make_async_copy(a, b, sem.at[i]) for i, (a, b) in enumerate(zip(sources, scratch))]

    def start(self, *which):
        for i in which:
            self.copies[i].start()

    def need(self, *which):
        for i in which:
            self.copies[i].wait()


def spread_head(head_rows, head):
    rows = head_rows[...].astype(F32)
    rows = jnp.concatenate([rows, rows, jnp.zeros((LANES - 2 * CLASSES, D), F32)], axis=0)
    head[...] = jnp.transpose(rows).astype(BF)


def glance_kernel(
    coarse, gain_attn, gain_head, head_rows, patch_hbm, position_hbm, qkv_hbm, out_hbm, join_hbm,
    joined, top, bottom, first, last,
    patch_weight, position, qkv_weight, out_weight, join_weight, head, sem, tokens, normed, packed, mixed,
):
    weights = Weights(
        [patch_hbm, position_hbm, qkv_hbm, out_hbm, join_hbm],
        [patch_weight, position, qkv_weight, out_weight, join_weight],
        sem,
    )
    weights.start(0, 1, 2, 3, 4)
    spread_head(head_rows, head)
    weights.need(0, 1)
    windows = CC // TS
    for w in range(windows):
        rows = slice(w * TT, (w + 1) * TT)
        cells = coarse[:, w * TS : (w + 1) * TS, :].reshape(TT, PD)
        tokens[rows, :] = dot(cells, patch_weight[...]) + position[...].astype(F32)
    attend(
        tokens, normed, packed, mixed, gain_attn, qkv_weight, out_weight, lambda: weights.need(2), lambda: weights.need(3)
    )
    features = tokens[...].astype(BF)
    normed[...] = layer_norm(features.astype(F32), gain_head[...]).astype(BF)
    mixed[...] = features
    logits = dot(normed[...], head[...])
    high = logits.astype(BF)
    low = (logits - high.astype(F32)).astype(BF)
    lane = lax.broadcasted_iota(jnp.int32, high.shape, 1)
    both = jnp.where(lane < CLASSES, high, low)
    weights.need(4)
    lifted = dot(mixed[...], join_weight[...]).astype(BF)
    for w in range(windows):
        rows = slice(w * TT, (w + 1) * TT)
        cols = slice(w * TS, (w + 1) * TS)
        joined[:, cols, :D] = lifted[rows].reshape(TS, TS, D)
        joined[:, cols, D:] = both[rows].reshape(TS, TS, LANES)
    top[...] = joined[0]
    bottom[...] = joined[CR - 1]
    blank = jnp.zeros((16, JW), F32)
    first[...] = jnp.concatenate([joined[r, :16].astype(F32)[:1] for r in range(CR)] + [blank], axis=0).astype(BF)
    last[...] = jnp.concatenate([joined[r, CC - 16 :].astype(F32)[15:] for r in range(CR)] + [blank], axis=0).astype(BF)


def list_flagged(flags, chosen):
    def mark(t, count):
        @pl.when(flags[t] == 1)
        def _():
            chosen[count] = t

        return count + flags[t]

    count = lax.fori_loop(0, TILES, mark, jnp.int32(0))
    away = jnp.clip(count - KEEP, 0, len(SLOTS))
    chosen[TILES] = count - away
    chosen[TILES + 1] = away
    return count - away, away


def listed(chosen):
    return chosen[TILES], chosen[TILES + 1]


def stage_kernel(flags, pixels, _, *refs):
    chosen = refs[0]
    sends = refs[1 : 1 + len(SEND)]
    stage, in_sem, out_sem = refs[1 + len(SEND) :]
    keep, away = list_flagged(flags, chosen)

    def copy_in(s):
        return pltpu.make_async_copy(pixels.at[chosen[keep + s]], stage.at[s], in_sem.at[s])

    def copy_out(s):
        way, at = SLOTS[s]
        return pltpu.make_async_copy(stage.at[s], sends[way].at[at, pl.ds(0, TT)], out_sem.at[s])

    def each(then):
        for s in range(len(SLOTS)):

            @pl.when(s < away)
            def _():
                then(s)

    def pass_on(s):
        copy_in(s).wait()
        copy_out(s).start()

    @pl.when(away > 0)
    def _():
        each(lambda s: copy_in(s).start())
        each(pass_on)
        each(lambda s: copy_out(s).wait())


def pack_kernel(
    wide_end, narrow_end, place, chosen, joined, top, bottom, first, last, up, down, left, right,
    pick, rim_pick, *refs,
):
    ways = len(SEND)
    rims = refs[ways]
    sends = refs[ways + 1 : 2 * ways + 1]
    stage, out_sem, sides, all_rims = refs[2 * ways + 1 :]
    wide_pos = place[0]
    narrow_pos = place[1]
    keep, away = listed(chosen)
    sent = [
        sum((jnp.int32(s) < away).astype(jnp.int32) for s in range(len(SLOTS)) if SLOTS[s][0] == way)
        for way in range(ways)
    ]

    def rim_copy(s):
        way, at = SLOTS[s]
        return pltpu.make_async_copy(stage.at[s], sends[way].at[at, pl.ds(TT, RIM + 16)], out_sem.at[s])

    def mark_copy(s):
        way, at = SLOTS[s]
        rows = pl.ds(TT + RIM - 16, 16)
        return pltpu.make_async_copy(stage.at[s, pl.ds(RIM - 16, 16)], sends[way].at[at, rows], out_sem.at[s])

    def pick_side(at_edge, own, got):
        return jnp.where(at_edge, own.astype(F32), got.astype(F32))

    over = pick_side(wide_pos == 0, top[...], up[...]).astype(BF)
    under = pick_side(wide_pos == wide_end, bottom[...], down[...]).astype(BF)
    sides[0] = pick_side(narrow_pos == 0, first[...], left[...]).astype(BF)
    sides[1] = pick_side(narrow_pos == narrow_end, last[...], right[...]).astype(BF)
    for a in range(TR):
        for i in range(CS + 2):
            row = a * CS + i
            if row == 0:
                cells = over
            elif row == CR + 1:
                cells = under
            else:
                cells = joined[(row - 1) * CC : row * CC, :]
            rims[a, i * CC : (i + 1) * CC, :] = cells
        edge = (CS + 2) * CC
        block = dot(pick[0, a], sides[0]) + dot(pick[1, a], sides[1])
        rims[a, edge : edge + 16, :] = block.astype(BF)
        rims[a, edge + 16 :, :] = jnp.zeros((RIM_K - edge - 16, JW), BF)

    @pl.when(away > 0)
    def _():
        for a in range(TR):
            all_rims[a * TC * RIM : (a + 1) * TC * RIM, :] = dot(rim_pick[...], rims[a, :, :D]).astype(BF)

    for s in range(len(SLOTS)):

        @pl.when(s < away)
        def _():
            rim = all_rims[pl.ds(pl.multiple_of(chosen[keep + s] * RIM, RIM), RIM), :].astype(F32)
            row = lax.broadcasted_iota(jnp.int32, rim.shape, 0)
            rim = jnp.where(row == RIM - 1, sent[SLOTS[s][0]].astype(F32), rim).astype(BF)
            stage[s, :RIM, :] = rim[:, :PD]
            for part in range(RIM // 16):
                cols = slice(part * GROUP, (part + 1) * GROUP)
                stage[s, RIM:, cols] = rim[part * 16 : (part + 1) * 16, PD:]
            rim_copy(s).start()

        if SLOTS[s][1] == 0:

            @pl.when(s >= away)
            def _():
                stage[s, RIM - 16 : RIM, :] = jnp.zeros((16, PD), BF)
                mark_copy(s).start()

    for s in range(len(SLOTS)):

        @pl.when(s < away)
        def _():
            rim_copy(s).wait()

        if SLOTS[s][1] == 0:

            @pl.when(s >= away)
            def _():
                mark_copy(s).wait()


def run_tiles(count, fetch, wait, embed, finish, weights, gain_attn, gain_head, head, block):
    _, _, qkv_weight, out_weight = weights.refs
    tokens, normed, packed, mixed = block

    def body(k, need):
        wait(k)

        @pl.when(k + 1 < count)
        def _():
            fetch(k + 1)

        need(0, 1)
        embed(k, tokens)
        attend(
            tokens, normed, packed, mixed, gain_attn, qkv_weight, out_weight, lambda: need(2), lambda: need(3)
        )
        normed[...] = layer_norm(tokens[...], gain_head[...]).astype(BF)
        finish(k, jnp.transpose(dot(normed[...], head[...]))[:CLASSES].astype(BF))

    @pl.when(count > 0)
    def _():
        body(jnp.int32(0), weights.need)

    @pl.when(count == 0)
    def _():
        weights.need(0, 1, 2, 3)

    def later(k, carry):
        body(k, lambda *which: None)
        return carry

    lax.fori_loop(1, count, later, jnp.int32(0))


def local_kernel(
    chosen, pixels, rims, lift, gain_attn, gain_head, head_rows, patch_hbm, position_hbm, qkv_hbm, out_hbm,
    logits, buffer, sem, patch_weight, position, qkv_weight, out_weight, head, weight_sem, *block,
):
    weights = Weights(
        [patch_hbm, position_hbm, qkv_hbm, out_hbm], [patch_weight, position, qkv_weight, out_weight], weight_sem
    )
    weights.start(0, 1)
    keep, _ = listed(chosen)

    def copy(k):
        return pltpu.make_async_copy(pixels.at[chosen[k]], buffer.at[k % 2], sem.at[k % 2])

    @pl.when(keep > 0)
    def _():
        copy(0).start()

    weights.start(2, 3)
    spread_head(head_rows, head)
    coarse = []
    for a in range(TR):
        turned = jnp.transpose(rims[a, :, D:].astype(F32))
        coarse.append(turned[: 2 * CLASSES])
    coarse = jnp.concatenate(coarse, axis=0).astype(BF)
    for b in range(TC):
        fine = dot_nt(coarse, lift[b])
        for a in range(TR):
            at = a * 2 * CLASSES
            logits[a * TC + b] = (fine[at : at + CLASSES] + fine[at + CLASSES : at + 2 * CLASSES]).astype(BF)

    def embed(k, tokens):
        tile = chosen[k]
        cells = dot(buffer[k % 2], patch_weight[...])
        cells = cells + dot(lift[tile % TC], rims[tile // TC, :, :D])
        tokens[...] = cells + position[...].astype(F32)

    def finish(k, answer):
        logits[chosen[k]] = answer

    run_tiles(
        keep, lambda k: copy(k).start(), lambda k: copy(k).wait(), embed, finish, weights, gain_attn, gain_head, head, block
    )


def remote_kernel(*refs):
    ways = len(SEND)
    got = refs[:ways]
    refs = refs[1:]
    rim_lift, gain_attn, gain_head, head_rows = refs[ways : ways + 4]
    sources = refs[ways + 4 : ways + 8]
    answers = refs[ways + 8 : 2 * ways + 8]
    filled, flag_rows, buffer, flag_sem, sem = refs[2 * ways + 8 : 2 * ways + 13]
    held = refs[2 * ways + 13 : 2 * ways + 17]
    head, weight_sem = refs[2 * ways + 17 : 2 * ways + 19]
    block = refs[2 * ways + 19 :]
    patch_weight, position = held[:2]
    weights = Weights(sources, held, weight_sem)

    marks = [
        pltpu.make_async_copy(got[way].at[0, pl.ds(TT + RIM - 16, 16)], flag_rows.at[way], flag_sem.at[way])
        for way in range(ways)
    ]
    for mark in marks:
        mark.start()
    weights.start(0, 1)
    for mark in marks:
        mark.wait()
    sent = [jnp.max(flag_rows[way, :, :LANES].astype(F32)[15:16]).astype(jnp.int32) for way in range(ways)]
    count = jnp.int32(0)
    for s, (way, at) in enumerate(SLOTS):
        filled[count] = s
        count = count + (at < sent[way]).astype(jnp.int32)

    def each_slot(k, then):
        for s in range(len(SLOTS)):

            @pl.when(filled[k] == s)
            def _():
                then(*SLOTS[s])

    def copy(k, way, at):
        return pltpu.make_async_copy(got[way].at[at], buffer.at[k % 2], sem.at[k % 2])

    def fetch(k):
        each_slot(k, lambda way, at: copy(k, way, at).start())

    @pl.when(count > 0)
    def _():
        fetch(0)

    weights.start(2, 3)
    spread_head(head_rows, head)

    def embed(k, tokens):
        slot = buffer.at[k % 2]
        tail = slot[TT + RIM :, :]
        rest = jnp.concatenate([tail[:, part * GROUP : (part + 1) * GROUP] for part in range(RIM // 16)], axis=0)
        place = position[...].astype(F32)
        cells = dot(slot[:TT, :], patch_weight[...])
        tokens[:, :PD] = cells[:, :PD] + dot(rim_lift[...], slot[TT : TT + RIM, :]) + place[:, :PD]
        tokens[:, PD:] = cells[:, PD:] + dot(rim_lift[...], rest) + place[:, PD:]

    def finish(k, answer):
        def store(way, at):
            answers[way][at] = answer

        each_slot(k, store)

    run_tiles(count, fetch, lambda k: copy(k, 0, 0).wait(), embed, finish, weights, gain_attn, gain_head, head, block)


def merge_kernel(chosen, base, *refs):
    returned = refs[: len(SEND)]
    logits = refs[len(SEND)]
    keep, away = listed(chosen)
    logits[...] = base[...]
    for s in range(len(SLOTS)):

        @pl.when(s < away)
        def _():
            way, at = SLOTS[s]
            logits[chosen[keep + s]] = returned[way][at]


def vmem():
    return pl.BlockSpec(memory_space=pltpu.VMEM)


def smem():
    return pl.BlockSpec(memory_space=pltpu.SMEM)


def hbm():
    return pl.BlockSpec(memory_space=pl.ANY)


def block_scratch(rows):
    return [
        pltpu.VMEM((rows, D), F32),
        pltpu.VMEM((rows, D), BF),
        pltpu.VMEM((rows, 3 * D), BF),
        pltpu.VMEM((rows, D), BF),
    ]


def weight_scratch(*more):
    return [
        pltpu.VMEM((PD, D), BF),
        pltpu.VMEM((TT, D), BF),
        pltpu.VMEM((D, 3 * D), BF),
        pltpu.VMEM((D, D), BF),
        *more,
        pltpu.VMEM((D, LANES), BF),
        pltpu.SemaphoreType.DMA((4 + len(more),)),
    ]


def glance(coarse_pixels, small, large, join_weight):
    rows = CR * CC
    return pl.pallas_call(
        glance_kernel,
        out_shape=[jax.ShapeDtypeStruct((CR, CC, JW), BF)]
        + [jax.ShapeDtypeStruct((CC, JW), BF)] * 4,
        in_specs=[vmem()] * 4 + [hbm()] * 5,
        out_specs=[vmem()] * 5,
        scratch_shapes=weight_scratch(pltpu.VMEM((D, D), BF)) + block_scratch(rows),
        compiler_params=params(60),
        name="glance",
    )(coarse_pixels, *small, *large, join_weight)


def tile_cost(tiles):
    return pl.CostEstimate(flops=tiles * 3_500_000_000, bytes_accessed=12_000_000, transcendentals=0)


def params(limit):
    return pltpu.CompilerParams(vmem_limit_bytes=limit * MIB)


def stage_pixels(flags, pixels, after):
    return pl.pallas_call(
        stage_kernel,
        out_shape=[jax.ShapeDtypeStruct((TILES + 2,), jnp.int32)]
        + [jax.ShapeDtypeStruct((n, SLOT_ROWS, PD), BF) for n in SEND],
        in_specs=[smem(), hbm(), hbm()],
        out_specs=[smem()] + [hbm()] * len(SEND),
        scratch_shapes=[
            pltpu.VMEM((len(SLOTS), TT, PD), BF),
            pltpu.SemaphoreType.DMA((len(SLOTS),)),
            pltpu.SemaphoreType.DMA((len(SLOTS),)),
        ],
        compiler_params=params(60),
        cost_estimate=pl.CostEstimate(flops=0, bytes_accessed=10_000_000, transcendentals=0),
        name="stage",
    )(flags, pixels, after)


def pack(place, chosen, joined, cells, sends):
    ways = len(SEND)
    return pl.pallas_call(
        functools.partial(pack_kernel, lax.axis_size("wide") - 1, lax.axis_size("narrow") - 1),
        out_shape=[jax.ShapeDtypeStruct((TR, RIM_K, JW), BF)]
        + [jax.ShapeDtypeStruct((n, SLOT_ROWS, PD), BF) for n in SEND],
        in_specs=[smem(), smem()] + [vmem()] * (1 + len(cells)) + [hbm()] * ways,
        out_specs=[vmem()] + [hbm()] * ways,
        input_output_aliases={3 + len(cells) + way: 1 + way for way in range(ways)},
        scratch_shapes=[
            pltpu.VMEM((len(SLOTS), RIM + 16, PD), BF),
            pltpu.SemaphoreType.DMA((len(SLOTS),)),
            pltpu.VMEM((2, 32, JW), BF),
            pltpu.VMEM((TILES * RIM, D), BF),
        ],
        compiler_params=params(60),
        name="pack",
    )(place, chosen, joined, *cells, *sends)


def focus_local(chosen, pixels, rims, lift, small, large):
    return pl.pallas_call(
        local_kernel,
        out_shape=jax.ShapeDtypeStruct((TILES, CLASSES, TT), BF),
        in_specs=[smem(), hbm()] + [vmem()] * 5 + [hbm()] * 4,
        out_specs=vmem(),
        scratch_shapes=[
            pltpu.VMEM((2, TT, PD), BF),
            pltpu.SemaphoreType.DMA((2,)),
        ]
        + weight_scratch()
        + block_scratch(TT),
        compiler_params=params(60),
        cost_estimate=tile_cost(9),
        name="focus_local",
    )(chosen, pixels, rims, lift, *small, *large)


def focus_remote(got, base, rim_lift, small, large):
    return pl.pallas_call(
        remote_kernel,
        out_shape=[jax.ShapeDtypeStruct((n, CLASSES, TT), BF) for n in SEND],
        in_specs=[hbm()] * (len(SEND) + 1) + [vmem()] * 4 + [hbm()] * 4,
        out_specs=[vmem()] * len(SEND),
        scratch_shapes=[
            pltpu.SMEM((len(SLOTS) + 1,), jnp.int32),
            pltpu.VMEM((len(SEND), 16, PD), BF),
            pltpu.VMEM((2, SLOT_ROWS, PD), BF),
            pltpu.SemaphoreType.DMA((len(SEND),)),
            pltpu.SemaphoreType.DMA((2,)),
        ]
        + weight_scratch()
        + block_scratch(TT),
        compiler_params=params(60),
        cost_estimate=tile_cost(4),
        name="focus_remote",
    )(*got, base, rim_lift, *small, *large)


def merge(chosen, base, returned):
    return pl.pallas_call(
        merge_kernel,
        out_shape=jax.ShapeDtypeStruct((TILES, CLASSES, TT), BF),
        in_specs=[smem()] + [vmem()] * (1 + len(SEND)),
        out_specs=vmem(),
        compiler_params=params(6),
        name="merge",
    )(chosen, base, *returned)


def routes():
    wide = lax.axis_size("wide")
    side = int(np.sqrt(wide))

    def along_x(step):
        return "wide", [(i, (i // side + step) % side * side + i % side) for i in range(wide)]

    def along_y(step):
        return "wide", [(i, i // side * side + (i % side + step) % side) for i in range(wide)]

    return [along_x(1), along_x(-1), along_y(1), along_y(-1)]


def shifted(x, axis, step):
    count = lax.axis_size(axis)
    pairs = [(i, i + step) for i in range(count) if 0 <= i + step < count]
    return lax.ppermute(x, axis, pairs)


def cornered(column, above, below):
    blank = jnp.zeros((32 - CR - 2, JW), BF)
    return jnp.concatenate([column[:CR], above, below, blank], axis=0)


def per_device(
    pixels,
    coarse_pixels,
    unsure,
    patch_weight,
    position,
    qkv_weight,
    out_weight,
    join_weight,
    gain_attn,
    gain_head,
    head_weight,
):
    tile_rows, tile_cols = unsure.shape
    flags = unsure.reshape(-1)
    gain_attn = gain_attn.reshape(1, D)
    gain_head = gain_head.reshape(1, D)
    small = (gain_attn, gain_head, head_weight.T)
    large = (patch_weight, position, qkv_weight, out_weight)
    lift = jnp.asarray(lift_tables(), BF)
    pick = jnp.asarray(side_tables(), BF)
    joined, top, bottom, first, last = glance(coarse_pixels, small, large, join_weight)
    up = shifted(bottom, "wide", 1)
    down = shifted(top, "wide", -1)
    wide_pos = lax.axis_index("wide")
    first_row = wide_pos == 0
    last_row = wide_pos == lax.axis_size("wide") - 1
    first = cornered(first, jnp.where(first_row, top[:1], up[:1]), jnp.where(last_row, bottom[:1], down[:1]))
    last = cornered(last, jnp.where(first_row, top[-1:], up[-1:]), jnp.where(last_row, bottom[-1:], down[-1:]))
    borders = [up, down, shifted(last, "narrow", 1), shifted(first, "narrow", -1)]
    place = jnp.stack([lax.axis_index("wide"), lax.axis_index("narrow")]).astype(jnp.int32)
    rim_pick, rim_lift = (jnp.asarray(t, BF) for t in rim_tables())
    flat_pixels = pixels.reshape(TILES, TT, PD)
    flat_joined = joined.reshape(CR * CC, JW)
    chosen, *staged = stage_pixels(flags, flat_pixels, joined)
    cells = (top, bottom, first, last, *borders, pick, rim_pick.reshape(TC * RIM, RIM_K))
    rims, *sends = pack(place, chosen, flat_joined, cells, staged)
    ways = routes()
    got = [lax.ppermute(block, axis, pairs) for block, (axis, pairs) in zip(sends, ways)]
    base = focus_local(chosen, flat_pixels, rims, lift, small, large)
    answers = focus_remote(got, base, rim_lift, small, large)
    returned = [
        lax.ppermute(block, axis, [(b, a) for a, b in pairs]) for block, (axis, pairs) in zip(answers, ways)
    ]
    logits = merge(chosen, base, returned)
    return logits.reshape(tile_rows, tile_cols, CLASSES, TT)


def solution(mesh):
    return jax.shard_map(
        per_device,
        mesh=mesh,
        in_specs=(
            P("wide", "narrow", None, None),
            P("wide", "narrow", None),
            P("wide", "narrow"),
            P(),
            P(),
            P(),
            P(),
            P(),
            P(),
            P(),
            P(),
        ),
        out_specs=P("wide", "narrow", None, None),
        check_vma=False,
    )
```
